32 devices in a mesh: dp: 8 (over z, x), psg: 4 (over y, core).
Axes of the slice: x: 2, y: 2, z: 4, core: 2. Of those that a mesh axis runs over, the one named last changes fastest.
Arguments:
- decoder_input: bfloat16 [64, 512, 768], P(('dp', 'psg')), may hold values from -6 to 6
- encoder_out: bfloat16 [64, 8, 384, 768], P('dp', 'psg'), may hold values from -6 to 6
- cotangent: bfloat16 [64, 512, 768], P(('dp', 'psg')), may hold values from -12 to 12
- task_ids: int32 [64], P(('dp', 'psg')), may hold values from 0 to 2
- passage_ids: int32 [64, 8], P('dp', 'psg'), may hold values from 0 to 2047
- target_lengths: int32 [64], P(('dp', 'psg')), may hold values from 128 to 512, as said below
- query_embed: float32 [64, 768], P('dp'), may hold values from -0.21875 to 0.21875
- passage_bank: bfloat16 [2048, 768], replicated, may hold values from -6 to 6
- self_in: bfloat16 [768, 2304], P(('dp', 'psg')), may hold values from -0.21875 to 0.21875
- self_out: bfloat16 [768, 768], P(('dp', 'psg')), may hold values from -1.75 to 1.75
- cross_query: bfloat16 [768, 768], P(('dp', 'psg')), may hold values from -0.21875 to 0.21875
- cross_keyval: bfloat16 [768, 1536], P(('dp', 'psg')), may hold values from -0.21875 to 0.21875
- cross_out: bfloat16 [768, 768], P(('dp', 'psg')), may hold values from -7 to 7
- hidden_in: bfloat16 [768, 3072], P(('dp', 'psg')), may hold values from -0.21875 to 0.21875
- hidden_output_weight: bfloat16 [3072, 768], P(('dp', 'psg')), may hold values from -0.109375 to 0.109375
- norm_gains: bfloat16 [3, 768], P(None, ('dp', 'psg')), may hold values from 0.5 to 1.5
- task_table: bfloat16 [3, 768], P(None, ('dp', 'psg')), may hold values from -6 to 6
Outputs:
- output: bfloat16 [64, 512, 768], P(('dp', 'psg'))
- input_grad: float32 [64, 512, 768], P(('dp', 'psg'))
- encoder_grad: float32 [64, 8, 384, 768], P('dp', 'psg')
- grad_self_in: float32 [768, 2304], P(('dp', 'psg'))
- grad_self_out: float32 [768, 768], P(('dp', 'psg'))
- grad_cross_query: float32 [768, 768], P(('dp', 'psg'))
- grad_cross_keyval: float32 [768, 1536], P(('dp', 'psg'))
- grad_cross_out: float32 [768, 768], P(('dp', 'psg'))
- grad_hidden_in: float32 [768, 3072], P(('dp', 'psg'))
- grad_hidden_out: float32 [3072, 768], P(('dp', 'psg'))
- grad_norm_gains: float32 [3, 768], P(None, ('dp', 'psg'))
- grad_task_table: float32 [3, 768], P(None, ('dp', 'psg'))
- query_grad: float32 [64, 768], P('dp')
The draws below stay inside these ranges and needn't reach their ends.
Inputs may be any that keep to these rules, and one draw needn't show every extreme that they name: `target_lengths`: in each aligned block of 8 queries one query uses all 512 decoder tokens.
All inputs are finite; a program needn't handle non-finite values.
Results may differ from the reference program's by a relative error of at most 0.02.
Values may be sent and summed in bfloat16 or wider, within the bound.
A program may use at most 384 MiB of HBM per device.

```python
import jax
import jax.numpy as jnp
from jax import lax

D = 768
H = 12
DH = 64
FF = 3072
E = 768
DEC = 512
PTOK = 384
TASKS = 3
BANK = 2048
Q_DEV = 8
QUERIES = 64
PASSAGES = 8


def draw_target_lengths(key, part):
    key_lengths = jax.random.fold_in(key, 11)
    key_chosen = jax.random.fold_in(key, 12)
    lengths = jax.random.randint(key_lengths, (QUERIES,), DEC // 4, DEC + 1)
    chosen = jax.random.randint(key_chosen, (QUERIES // Q_DEV,), 0, Q_DEV)
    places = jnp.arange(QUERIES, dtype=jnp.int32) % Q_DEV
    complete = places == jnp.repeat(chosen, Q_DEV)
    return jnp.where(complete, DEC, lengths).astype(jnp.int32)


def plant(values, key, least, top_value):
    place = [jax.random.randint(jax.random.fold_in(key, axis), (), 0, length) for axis, length in enumerate(values.shape)]
    widest = values.shape.index(max(values.shape))
    beside = place[:widest] + [(place[widest] + 1) % values.shape[widest]] + place[widest + 1:]
    return values.at[tuple(place)].set(least).at[tuple(beside)].set(top_value)


def spiked(drawn, own_key, source, target, blocks, factor):
    def block_of(axis_at):
        return (jnp.arange(drawn.shape[axis_at]) // (drawn.shape[axis_at] // blocks)).reshape((-1,) + (1,) * (drawn.ndim - 1 - axis_at))

    first = jax.random.permutation(own_key, blocks)[block_of(target)]
    other_side = (block_of(target) + blocks // 2) % blocks
    return jnp.where((block_of(source) == first) | (block_of(source) == other_side), factor * drawn, drawn)


def steps_of(rng, dims, shards, low, largest):
    gain = 1.0
    for position, shards_of in shards:
        steps = jax.random.uniform(jax.random.fold_in(jax.random.fold_in(rng, 6), position), (shards_of,), jnp.float32, low / len(shards), largest / len(shards))
        gain = gain * jnp.repeat(jnp.exp(steps), dims[position] // shards_of).reshape((-1,) + (1,) * (len(dims) - 1 - position))
    return gain


def centred(key, shape, spread, bound, cuts=(), kind=jnp.bfloat16):
    factor_of = steps_of(key, shape, cuts, -0.22, 0.18) if cuts else 1.0
    entries = jax.random.normal(key, shape, jnp.float32) * spread * factor_of
    return jnp.minimum(jnp.maximum(entries, -bound), bound).astype(kind)


def bell_draw_with(rng, dims, spread, bound, pieces, heavy, kind=jnp.bfloat16):
    entries = spread * jax.random.normal(rng, dims, jnp.float32)
    if pieces:
        entries = entries * steps_of(rng, dims, pieces, -0.22, 0.18)
    return jnp.clip(spiked(entries, jax.random.fold_in(rng, 3), *heavy), -bound, bound).astype(kind)


def setup_inputs(seed: int = 0) -> dict:
    seeds = jax.random.split(jax.random.key(seed), 18)
    decoder_input = centred(seeds[0], (QUERIES, DEC, D), 1.0, 6.0, ((0, 32),))
    encoder_out = centred(seeds[1], (QUERIES, PASSAGES, PTOK, D), 1.0, 6.0, ((0, 8), (1, 4)))
    cotangent = bell_draw_with(seeds[2], (QUERIES, DEC, D), 1.0, 12.0, ((0, 32),), (0, 2, 32, 2.75))
    task_ids = plant(jax.random.randint(seeds[3], (QUERIES,), 0, TASKS), jax.random.fold_in(seeds[3], 1), 0, TASKS - 1).astype(jnp.int32)
    passage_ids = plant(jax.random.randint(seeds[4], (QUERIES, PASSAGES), 0, BANK), jax.random.fold_in(seeds[4], 1), 0, BANK - 1).astype(jnp.int32)
    target_lengths = draw_target_lengths(jax.random.fold_in(seeds[17], 71), 0)
    query_embed = centred(seeds[6], (QUERIES, E), (E ** -0.5), 0.21875, ((0, 8),), jnp.float32)
    passage_bank = centred(seeds[7], (BANK, E), 1.0, 6.0)
    self_in = centred(seeds[8], (D, 3 * D), D ** -0.5, 0.21875, ((0, 32),))
    self_out = centred(seeds[9], (D, D), ((DEC / 8 / D) ** 0.5), 1.75, ((0, 32),))
    cross_query = centred(seeds[10], (D, D), D ** -0.5, 0.21875, ((0, 32),))
    cross_keyval = centred(seeds[11], (D, 2 * D), D ** -0.5, 0.21875, ((0, 32),))
    cross_out = centred(seeds[12], (D, D), ((PASSAGES * PTOK / 3 / D) ** 0.5), 7.0, ((0, 32),))
    hidden_in = centred(seeds[13], (D, FF), D ** -0.5, 0.21875, ((0, 32),))
    hidden_output_weight = centred(seeds[14], (FF, D), FF ** -0.5, 0.109375, ((0, 32),))
    norm_gains = jnp.clip(1.0 + 0.1 * jax.random.normal(seeds[15], (3, D), jnp.float32), 0.5, 1.5).astype(jnp.bfloat16)
    task_table = centred(seeds[16], (TASKS, D), 1.0, 6.0, ((1, 32),))
    return {"decoder_input": decoder_input, "encoder_out": encoder_out, "cotangent": cotangent, "task_ids": task_ids, "passage_ids": passage_ids, "target_lengths": target_lengths, "query_embed": query_embed, "passage_bank": passage_bank, "self_in": self_in, "self_out": self_out, "cross_query": cross_query, "cross_keyval": cross_keyval, "cross_out": cross_out, "hidden_in": hidden_in, "hidden_output_weight": hidden_output_weight, "norm_gains": norm_gains, "task_table": task_table}


@jax.custom_vjp
def low(v):
    return lax.optimization_barrier(v.astype(jnp.bfloat16)).astype(jnp.float32)

@jax.custom_vjp
def low_back(v):
    return v

def low_keep(v):
    return (low(v), None)

def low_pass(kept, grad):
    return (grad,)

def back_keep(v):
    return (v, None)

def back_low(kept, grad):
    return (low(grad),)
low.defvjp(low_keep, low_pass)
low_back.defvjp(back_keep, back_low)

def matmul(left, right):
    return jnp.matmul(left, right, precision=lax.Precision.HIGHEST)

def rms_norm(tensor, gain_row):
    return tensor * lax.rsqrt(lax.optimization_barrier(jnp.mean(tensor * tensor, axis=-1, keepdims=True)) + 1e-06) * gain_row

def gelu_tanh(tensor):
    return 0.5 * tensor * (1.0 + jnp.tanh(0.7978845608028654 * (tensor + 0.044715 * tensor * tensor * tensor)))

def softmax_rows(scores):
    biggest = lax.optimization_barrier(jnp.max(scores, axis=-1, keepdims=True))
    exponent = jnp.exp(scores - biggest)
    return exponent / lax.optimization_barrier(jnp.sum(exponent, axis=-1, keepdims=True))

def decoder_query(weights, packed):
    w_self_in, w_self_out, w_cross_query, w_cross_keyval, w_cross_out, w_hidden_in, w_hidden_out, gains, unused_table = weights
    inputs, task_row, encoded, length = packed
    stream = inputs + task_row[None, :]
    normed_one = low(rms_norm(stream, gains[0]))
    qkv_rows = low_back(low(matmul(normed_one, w_self_in))).reshape(DEC, 3, H, DH)
    self_scores = low_back(jnp.einsum('ihd,jhd->hij', qkv_rows[:, 0], qkv_rows[:, 1], precision=lax.Precision.HIGHEST) * 0.125)
    row_pos = lax.broadcasted_iota(jnp.int32, (DEC, DEC), 0)
    col_pos = lax.broadcasted_iota(jnp.int32, (DEC, DEC), 1)
    allowed = (col_pos <= row_pos) & (col_pos < length)
    self_probs = low(softmax_rows(jnp.where(allowed[None], self_scores, -1e+30)))
    self_att = jnp.einsum('hij,jhd->ihd', self_probs, qkv_rows[:, 2], precision=lax.Precision.HIGHEST)
    self_att = low_back(low(self_att.reshape(DEC, D)))
    middle = stream + low_back(matmul(self_att, w_self_out))
    normed_two = low(rms_norm(middle, gains[1]))
    cross_query_rows = low_back(low(matmul(normed_two, w_cross_query))).reshape(DEC, H, DH)
    cross_kv = low_back(low(matmul(encoded, w_cross_keyval))).reshape(PASSAGES * PTOK, 2, H, DH)
    cross_scores = low_back(jnp.einsum('ihd,jhd->hij', cross_query_rows, cross_kv[:, 0], precision=lax.Precision.HIGHEST) * 0.125)
    cross_full = softmax_rows(cross_scores)
    mass = lax.optimization_barrier(jnp.sum(cross_full.reshape(H, DEC, PASSAGES, PTOK), axis=(0, 1, 3))) / (H * DEC)
    cross_att = jnp.einsum('hij,jhd->ihd', low(cross_full), cross_kv[:, 1], precision=lax.Precision.HIGHEST)
    cross_att = low_back(low(cross_att.reshape(DEC, D)))
    latter = middle + low_back(matmul(cross_att, w_cross_out))
    normed_three = low(rms_norm(latter, gains[2]))
    hidden_pre = low_back(matmul(normed_three, w_hidden_in))
    activated = low(gelu_tanh(hidden_pre))
    return (latter + low_back(matmul(activated, w_hidden_out)), mass)

def reference(decoder_input, encoder_out, cotangent, task_ids, passage_ids, target_lengths, query_embed, passage_bank, self_in, self_out, cross_query, cross_keyval, cross_out, hidden_in, hidden_output_weight, norm_gains, task_table):
    weights = tuple((tensor.astype(jnp.float32) for tensor in (self_in, self_out, cross_query, cross_keyval, cross_out, hidden_in, hidden_output_weight, norm_gains, task_table)))
    inputs = decoder_input.astype(jnp.float32)
    encoded = encoder_out.astype(jnp.float32).reshape(QUERIES, PASSAGES * PTOK, D)
    choose = (task_ids[:, None] == jnp.arange(TASKS, dtype=jnp.int32)[None, :]).astype(jnp.float32)

    def forward(inputs, encoded, weights):
        task_rows = matmul(choose, weights[8])

        def single(packed):
            return decoder_query(weights, packed)
        return lax.map(jax.checkpoint(single), (inputs, task_rows, encoded, target_lengths))
    (result, mass), pullback = jax.vjp(forward, inputs, encoded, weights)
    grad_inputs, grad_encoded, grad_weights = pullback((cotangent.astype(jnp.float32), jnp.zeros_like(mass)))
    embeds = passage_bank.astype(jnp.float32)[passage_ids]

    def divergence(embedding):
        scores = jnp.einsum('qe,qpe->qp', embedding, embeds, precision=lax.Precision.HIGHEST)
        biggest = lax.optimization_barrier(jnp.max(scores, axis=-1, keepdims=True))
        log_probs = scores - biggest - jnp.log(lax.optimization_barrier(jnp.sum(jnp.exp(scores - biggest), axis=-1, keepdims=True)))
        return jnp.sum(mass * (jnp.log(mass) - log_probs))
    unused_loss, kl_pull = jax.vjp(divergence, query_embed)
    query_grad = kl_pull(jnp.ones((), jnp.float32))[0]
    return (result.astype(jnp.bfloat16), grad_inputs, grad_encoded.reshape(QUERIES, PASSAGES, PTOK, D), grad_weights[0], grad_weights[1], grad_weights[2], grad_weights[3], grad_weights[4], grad_weights[5], grad_weights[6], grad_weights[7], grad_weights[8], query_grad)
```

```python
import functools

import jax
import jax.numpy as jnp
from jax import lax
from jax.experimental import pallas as pl
from jax.experimental.pallas import tpu as pltpu
from jax.sharding import PartitionSpec as P

H = 12
DH = 64
PAIR = 2 * DH
BF = jnp.bfloat16
F32 = jnp.float32
LN2 = 0.6931471805599453
QSCALE = 0.125 / LN2
ALL = ("dp", "psg")
NN = (((1,), (0,)), ((), ()))
NT = (((1,), (1,)), ((), ()))
TN = (((0,), (0,)), ((), ()))
VMEM_BYTES = 56 * 2**20


def dot(a, b, dims=NN):
    return lax.dot_general(a, b, dims, preferred_element_type=F32)


def mm(a, b, dims=NN):
    return lax.dot_general(a, b, dims, preferred_element_type=F32)


def head_mask(rows, h):
    lane = lax.broadcasted_iota(jnp.int32, (rows, PAIR), 1)
    return (lane >= DH) == (h == 1)


def cross_fwd_body(idx, q_ref, k_ref, v_ref, o_ref, lse_ref, share_ref, *, npass):
    q, k, v = q_ref[0], k_ref[0], v_ref[0]
    keys, rows = k.shape[0], q.shape[0]
    vt = v.T
    col = lax.broadcasted_iota(jnp.int32, (16, keys), 1) // (keys // npass)
    row = lax.broadcasted_iota(jnp.int32, (16, keys), 0)
    member = (col == row).astype(BF)
    outs = []
    for h in range(2):
        qh = jnp.where(head_mask(rows, h), q, jnp.zeros((), BF))
        s = dot(k, qh, NT)
        m = jnp.max(s, axis=0, keepdims=True)
        p = jnp.exp2(s - m).astype(BF)
        ot = dot(jnp.concatenate([vt[h * DH : (h + 1) * DH], member], axis=0), p)
        parts = ot[DH : DH + npass]
        total = jnp.sum(parts, axis=0, keepdims=True)
        inv = 1.0 / total
        outs.append(ot[:DH] * inv)
        lse_ref[0, 0, h : h + 1, :] = m + jnp.log2(total)
        share_ref[0, 0, h, :, :] = parts * inv
    o_ref[0] = jnp.concatenate(outs, axis=0).T.astype(o_ref.dtype)


def cross_fwd(idx, q, kv, npass):
    nq, rows, width = q.shape
    keys, pairs = kv.shape[1], width // PAIR
    grid = pltpu.PrefetchScalarGridSpec(
        num_scalar_prefetch=1,
        grid=(nq, pairs),
        in_specs=[
            pl.BlockSpec((1, rows, PAIR), lambda n, p, i: (n, 0, p)),
            pl.BlockSpec((1, keys, PAIR), lambda n, p, i: (i[n], 0, p)),
            pl.BlockSpec((1, keys, PAIR), lambda n, p, i: (i[n], 0, pairs + p)),
        ],
        out_specs=[
            pl.BlockSpec((1, rows, PAIR), lambda n, p, i: (n, 0, p)),
            pl.BlockSpec((1, 1, 2, rows), lambda n, p, i: (n, p, 0, 0)),
            pl.BlockSpec((1, 1, 2, npass, rows), lambda n, p, i: (n, p, 0, 0, 0)),
        ],
    )
    return pl.pallas_call(
        functools.partial(cross_fwd_body, npass=npass),
        grid_spec=grid,
        out_shape=[
            jax.ShapeDtypeStruct(q.shape, BF),
            jax.ShapeDtypeStruct((nq, pairs, 2, rows), F32),
            jax.ShapeDtypeStruct((nq, pairs, 2, npass, rows), F32),
        ],
        compiler_params=pltpu.CompilerParams(vmem_limit_bytes=VMEM_BYTES),
        cost_estimate=pl.CostEstimate(
            flops=16 * nq * rows * keys * width,
            bytes_accessed=4 * nq * (rows + keys) * width,
            transcendentals=nq * H * rows * keys,
        ),
    )(idx, q, kv, kv)


def cross_bwd_body(idx, q_ref, k_ref, v_ref, do_ref, stat_ref, *rest, chunk):
    dq_ref, dkv_ref = rest[-2:]
    pair = pl.program_id(1)
    width = dkv_ref.shape[2] // 2
    q, k, v, do = q_ref[0], k_ref[0], v_ref[0], do_ref[0]
    rows = q.shape[0]
    kt = k.T
    dk, dv = 0.0, 0.0
    for c in range(0, rows, chunk):
        outs = []
        for h in range(2):
            mask = head_mask(chunk, h)
            qh = jnp.where(mask, q[c : c + chunk], jnp.zeros((), BF))
            doh = jnp.where(mask, do[c : c + chunk], jnp.zeros((), BF))
            p = jnp.exp2(dot(k, qh, NT) - stat_ref[0, 0, h : h + 1, c : c + chunk])
            dp = dot(v, doh, NT)
            ds = (p * (dp - stat_ref[0, 0, 2 + h : 3 + h, c : c + chunk])).astype(BF)
            dv = dv + dot(p.astype(BF), doh)
            dk = dk + dot(ds, qh)
            outs.append(dot(kt[h * DH : (h + 1) * DH], ds))
        dq_ref[0, c : c + chunk, :] = (jnp.concatenate(outs, axis=0).T * 0.125).astype(BF)
    at = pl.multiple_of(pair * PAIR, PAIR)
    dkv_ref[0, :, pl.ds(at, PAIR)] = (dk * LN2).astype(BF)
    at = pl.multiple_of(width + pair * PAIR, PAIR)
    dkv_ref[0, :, pl.ds(at, PAIR)] = dv.astype(BF)


def cross_bwd(idx, q, kv, do, stats, earlier=None):
    nq, rows, width = q.shape
    keys, pairs = kv.shape[1], width // PAIR
    in_specs = [
        pl.BlockSpec((1, rows, PAIR), lambda n, p, i: (n, 0, p)),
        pl.BlockSpec((1, keys, PAIR), lambda n, p, i: (i[n], 0, p)),
        pl.BlockSpec((1, keys, PAIR), lambda n, p, i: (i[n], 0, pairs + p)),
        pl.BlockSpec((1, rows, PAIR), lambda n, p, i: (n, 0, p)),
        pl.BlockSpec((1, 1, 4, rows), lambda n, p, i: (n, p, 0, 0)),
    ]
    operands = [idx, q, kv, kv, do, stats]
    aliases = {}
    if earlier is not None:
        in_specs.append(pl.BlockSpec(memory_space=pl.ANY))
        operands.append(earlier)
        aliases = {6: 1}
    grid = pltpu.PrefetchScalarGridSpec(
        num_scalar_prefetch=1,
        grid=(nq, pairs),
        in_specs=in_specs,
        out_specs=[
            pl.BlockSpec((1, rows, PAIR), lambda n, p, i: (n, 0, p)),
            pl.BlockSpec((1, keys, 2 * width), lambda n, p, i: (i[n], 0, 0)),
        ],
    )
    return pl.pallas_call(
        functools.partial(cross_bwd_body, chunk=min(rows, 256)),
        grid_spec=grid,
        input_output_aliases=aliases,
        out_shape=[jax.ShapeDtypeStruct(q.shape, BF), jax.ShapeDtypeStruct(kv.shape, BF)],
        compiler_params=pltpu.CompilerParams(vmem_limit_bytes=VMEM_BYTES),
        cost_estimate=pl.CostEstimate(
            flops=40 * nq * rows * keys * width,
            bytes_accessed=nq * (6 * rows + 8 * keys) * width,
            transcendentals=nq * H * rows * keys,
        ),
    )(*operands)


def self_mask(keys, start, chunk, length):
    key = lax.broadcasted_iota(jnp.int32, (keys, chunk), 0)
    row = lax.broadcasted_iota(jnp.int32, (keys, chunk), 1) + start
    return (key <= row) & (key < length)


def self_fwd_body(length_ref, q_ref, k_ref, v_ref, o_ref, lse_ref, *, chunk):
    length = length_ref[pl.program_id(0)]
    q, k, v = q_ref[0], k_ref[0], v_ref[0]
    rows = q.shape[0]
    vt = v.T
    for c in range(0, rows, chunk):
        keys = c + chunk
        allowed = self_mask(keys, c, chunk, length)
        ones = jnp.ones((16, keys), BF)
        outs = []
        for h in range(2):
            qh = jnp.where(head_mask(chunk, h), q[c : c + chunk], jnp.zeros((), BF))
            s = jnp.where(allowed, dot(k[:keys], qh, NT), -1e30)
            m = jnp.max(s, axis=0, keepdims=True)
            p = jnp.exp2(s - m).astype(BF)
            ot = dot(jnp.concatenate([vt[h * DH : (h + 1) * DH, :keys], ones], axis=0), p)
            total = ot[DH : DH + 1]
            outs.append(ot[:DH] * (1.0 / total))
            lse_ref[0, 0, h : h + 1, c : c + chunk] = m + jnp.log2(total)
        o_ref[0, c : c + chunk, :] = jnp.concatenate(outs, axis=0).T.astype(BF)


def self_fwd(lengths, qkv):
    nq, rows, width3 = qkv.shape
    width = width3 // 3
    pairs = width // PAIR
    grid = pltpu.PrefetchScalarGridSpec(
        num_scalar_prefetch=1,
        grid=(nq, pairs),
        in_specs=[
            pl.BlockSpec((1, rows, PAIR), lambda n, p, i: (n, 0, p)),
            pl.BlockSpec((1, rows, PAIR), lambda n, p, i: (n, 0, pairs + p)),
            pl.BlockSpec((1, rows, PAIR), lambda n, p, i: (n, 0, 2 * pairs + p)),
        ],
        out_specs=[
            pl.BlockSpec((1, rows, PAIR), lambda n, p, i: (n, 0, p)),
            pl.BlockSpec((1, 1, 2, rows), lambda n, p, i: (n, p, 0, 0)),
        ],
    )
    return pl.pallas_call(
        functools.partial(self_fwd_body, chunk=min(rows, 256)),
        grid_spec=grid,
        out_shape=[
            jax.ShapeDtypeStruct((nq, rows, width), BF),
            jax.ShapeDtypeStruct((nq, pairs, 2, rows), F32),
        ],
        compiler_params=pltpu.CompilerParams(vmem_limit_bytes=VMEM_BYTES),
        cost_estimate=pl.CostEstimate(
            flops=16 * nq * rows * rows * width,
            bytes_accessed=8 * nq * rows * width,
            transcendentals=nq * H * rows * rows,
        ),
    )(lengths, qkv, qkv, qkv)


def self_bwd_body(length_ref, q_ref, k_ref, v_ref, do_ref, lse_ref, out_ref, dk_acc, dv_acc, *, chunk):
    length = length_ref[pl.program_id(0)]
    pair = pl.program_id(1)
    width = out_ref.shape[2] // 3
    q, k, v, do = q_ref[0], k_ref[0], v_ref[0], do_ref[0]
    rows = q.shape[0]
    kt = k.T
    at = pl.multiple_of(pair * PAIR, PAIR)
    dk_acc[...] = jnp.zeros_like(dk_acc)
    dv_acc[...] = jnp.zeros_like(dv_acc)
    for c in range(0, rows, chunk):
        keys = c + chunk
        allowed = self_mask(keys, c, chunk, length)
        outs = []
        for h in range(2):
            mask = head_mask(chunk, h)
            qh = jnp.where(mask, q[c : c + chunk], jnp.zeros((), BF))
            doh = jnp.where(mask, do[c : c + chunk], jnp.zeros((), BF))
            s = jnp.where(allowed, dot(k[:keys], qh, NT), -1e30)
            p = jnp.exp2(s - lse_ref[0, 0, h : h + 1, c : c + chunk])
            dp = dot(v[:keys], doh, NT)
            delta = jnp.sum(p * dp, axis=0, keepdims=True)
            ds = (p * (dp - delta)).astype(BF)
            dv_acc[:keys] += dot(p.astype(BF), doh)
            dk_acc[:keys] += dot(ds, qh)
            outs.append(dot(kt[h * DH : (h + 1) * DH, :keys], ds))
        out_ref[0, c : c + chunk, pl.ds(at, PAIR)] = (
            jnp.concatenate(outs, axis=0).T * 0.125
        ).astype(BF)
    at = pl.multiple_of(width + pair * PAIR, PAIR)
    out_ref[0, :, pl.ds(at, PAIR)] = (dk_acc[...] * LN2).astype(BF)
    at = pl.multiple_of(2 * width + pair * PAIR, PAIR)
    out_ref[0, :, pl.ds(at, PAIR)] = dv_acc[...].astype(BF)


def self_bwd(lengths, qkv, do, lse):
    nq, rows, width3 = qkv.shape
    width = width3 // 3
    pairs = width // PAIR
    grid = pltpu.PrefetchScalarGridSpec(
        num_scalar_prefetch=1,
        grid=(nq, pairs),
        in_specs=[
            pl.BlockSpec((1, rows, PAIR), lambda n, p, i: (n, 0, p)),
            pl.BlockSpec((1, rows, PAIR), lambda n, p, i: (n, 0, pairs + p)),
            pl.BlockSpec((1, rows, PAIR), lambda n, p, i: (n, 0, 2 * pairs + p)),
            pl.BlockSpec((1, rows, PAIR), lambda n, p, i: (n, 0, p)),
            pl.BlockSpec((1, 1, 2, rows), lambda n, p, i: (n, p, 0, 0)),
        ],
        out_specs=[pl.BlockSpec((1, rows, width3), lambda n, p, i: (n, 0, 0))],
        scratch_shapes=[pltpu.VMEM((rows, PAIR), F32), pltpu.VMEM((rows, PAIR), F32)],
    )
    return pl.pallas_call(
        functools.partial(self_bwd_body, chunk=min(rows, 256)),
        grid_spec=grid,
        out_shape=[jax.ShapeDtypeStruct(qkv.shape, BF)],
        compiler_params=pltpu.CompilerParams(vmem_limit_bytes=VMEM_BYTES),
        cost_estimate=pl.CostEstimate(
            flops=40 * nq * rows * rows * width,
            bytes_accessed=16 * nq * rows * width,
            transcendentals=nq * H * rows * rows,
        ),
    )(lengths, qkv, qkv, qkv, do, lse)[0]


def rms_parts(v):
    return lax.rsqrt(jnp.mean(v * v, axis=-1, keepdims=True) + 1e-06)


def rms_back(v, gain, b):
    r = rms_parts(v)
    gb = gain * b
    grad = r * gb - v * (r * r * r * jnp.mean(v * gb, axis=-1, keepdims=True))
    return grad, jnp.sum(v * r * b, axis=tuple(range(v.ndim - 1)))


def gelu_and_slope(u):
    t = jnp.tanh(0.7978845608028654 * (u + 0.044715 * u * u * u))
    slope = 0.5 * (1.0 + t) + 0.5 * u * (1.0 - t * t) * (
        0.7978845608028654 * (1.0 + 3.0 * 0.044715 * u * u)
    )
    return 0.5 * u * (1.0 + t), slope


def spread(per_head, rows):
    nq = per_head.shape[0]
    flat = jnp.swapaxes(per_head.reshape(nq, H, rows), 1, 2)
    return jnp.repeat(flat, DH, axis=2)


def merge(parts):
    rows = parts[0][0].shape[1]
    top = functools.reduce(jnp.maximum, [lse for _, lse in parts])
    weights = [jnp.exp2(lse - top) for _, lse in parts]
    total = functools.reduce(jnp.add, weights)
    out = 0.0
    for (value, _), weight in zip(parts, weights):
        out = out + value.astype(F32) * spread(weight / total, rows)
    return out, top + jnp.log2(total)


def on_device(
    decoder_input,
    encoder_out,
    cotangent,
    task_ids,
    passage_ids,
    target_lengths,
    query_embed,
    passage_bank,
    self_in,
    self_out,
    cross_query,
    cross_keyval,
    cross_out,
    hidden_in,
    hidden_output_weight,
    norm_gains,
    task_table,
):
    count, rows, width = decoder_input.shape
    group, npass, tokens, _ = encoder_out.shape
    keys = npass * tokens
    psg = lax.axis_size("psg")
    chips = psg // 2
    me = lax.axis_index("psg")
    chip, core = me // 2, me % 2
    shard = self_in.shape[0]
    ff = hidden_in.shape[1]
    n_tasks = task_table.shape[0]

    swap = [(p, p ^ 1) for p in range(psg)]

    def core_swap(x):
        return jax.tree.map(lambda a: lax.ppermute(a, "psg", swap), x)

    def chip_shift(x, step):
        perm = [(p, (p + 2 * step) % psg) for p in range(psg)]
        return jax.tree.map(lambda a: lax.ppermute(a, "psg", perm), x)

    def ids_of(chip_at, core_at):
        return (chip_at * 2 + core_at) * count + jnp.arange(count, dtype=jnp.int32)

    small = jnp.concatenate([norm_gains, task_table], axis=0).T
    small = jnp.pad(small, ((0, 0), (0, 128 - small.shape[1])))
    first = lax.all_gather(
        jnp.concatenate([self_in, cross_keyval, self_out, cross_query, small], axis=1),
        ALL,
        axis=0,
        tiled=True,
    )
    edges = [0, 3 * width, 5 * width, 6 * width, 7 * width, 7 * width + 128]
    w_self_in, w_cross_keyval, w_self_out, w_cross_query, w_small = (
        first[:, a:b] for a, b in zip(edges[:-1], edges[1:])
    )
    second = lax.all_gather(
        jnp.concatenate([cross_out, hidden_in], axis=1), ALL, axis=0, tiled=True
    )
    w_cross_out, w_hidden_in = second[:, :width], second[:, width:]
    w_hidden_out = lax.all_gather(hidden_output_weight, ALL, axis=0, tiled=True)

    embeds = jnp.take(passage_bank, passage_ids, axis=0).astype(F32)
    score = jnp.sum(query_embed[:, None, :] * embeds, axis=-1)
    others = [
        lax.ppermute(score, "psg", [(p, (p + k) % psg) for p in range(psg)]) for k in range(1, psg)
    ]
    every = jnp.concatenate([score] + others, axis=1)
    top = jnp.max(every, axis=1, keepdims=True)
    retrieval = jnp.exp(score - top) / jnp.sum(jnp.exp(every - top), axis=1, keepdims=True)

    smalls = w_small.T.astype(F32)
    gains, table = smalls[:3], smalls[3 : 3 + n_tasks]
    choose = task_ids[:, None] == jnp.arange(n_tasks, dtype=jnp.int32)[None, :]
    task_rows = jnp.sum(jnp.where(choose[:, :, None], table[None], 0.0), axis=1)

    stream = decoder_input.astype(F32) + task_rows[:, None, :]
    normed_one = (stream * rms_parts(stream) * gains[0]).astype(BF)
    col = lax.broadcasted_iota(jnp.int32, (1, 3 * width), 1)
    scale = jnp.where(col < width, QSCALE, 1.0)
    flat = (count * rows, width)
    qkv = (mm(normed_one.reshape(flat), w_self_in) * scale).astype(BF)
    qkv = qkv.reshape(count, rows, 3 * width)
    self_att, self_lse = self_fwd(target_lengths, qkv)
    middle = stream + mm(self_att.reshape(flat), w_self_out).reshape(stream.shape)
    normed_two = (middle * rms_parts(middle) * gains[1]).astype(BF)
    own_q = (mm(normed_two.reshape(flat), w_cross_query) * QSCALE).astype(BF)
    own_q = own_q.reshape(count, rows, width)

    enc = encoder_out.reshape(group * keys, width)
    kv = mm(enc, w_cross_keyval).astype(BF).reshape(group, keys, 2 * width)
    peer_q = core_swap(own_q)
    far_q = []
    for step in range(1, chips):
        same = [chip_shift(own_q[n : n + 1], step) for n in range(count)]
        far_q.append([(s, core_swap(s)) for s in same])

    far_local, far_back = [], []
    for step in range(1, chips):
        source = (chip - step) % chips
        local, back = [], []
        for n in range(count):
            ids = jnp.stack([ids_of(source, core)[n], ids_of(source, 1 - core)[n]])
            queries = jnp.concatenate(far_q[step - 1][n], axis=0)
            part, lse, share = cross_fwd(ids, queries, kv, npass)
            got = core_swap((part[1:], lse[1:]))
            value, joint = merge([(part[:1], lse[:1]), got])
            back.append(chip_shift((value.astype(BF), joint), chips - step))
            local.append((lse, share))
        far_local.append(local)
        far_back.append(back)
    near_ids = jnp.concatenate([ids_of(chip, core), ids_of(chip, 1 - core)])
    part, near_lse, near_share = cross_fwd(
        near_ids, jnp.concatenate([own_q, peer_q], axis=0), kv, npass
    )
    parts = [(part[:count], near_lse[:count]), core_swap((part[count:], near_lse[count:]))]
    for back in far_back:
        parts.append(
            (
                jnp.concatenate([b[0] for b in back], axis=0),
                jnp.concatenate([b[1] for b in back], axis=0),
            )
        )
    cross_sum, cross_lse = merge(parts)
    cross_att = cross_sum.astype(BF)

    latter = middle + mm(cross_att.reshape(flat), w_cross_out).reshape(stream.shape)
    normed_three = (latter * rms_parts(latter) * gains[2]).astype(BF)
    hidden_pre = mm(normed_three.reshape(flat), w_hidden_in)
    activated, slope = gelu_and_slope(hidden_pre)
    activated = activated.astype(BF)
    output = (latter + mm(activated, w_hidden_out).reshape(stream.shape)).astype(BF)
    cot = cotangent.reshape(flat)
    grad_hidden_out = mm(activated, cot, TN).astype(BF)
    grad_pre = (mm(cot, w_hidden_out, NT) * slope).astype(BF)
    grad_hidden_in = mm(normed_three.reshape(flat), grad_pre, TN).astype(BF)
    grad_normed_three = mm(grad_pre, w_hidden_in, NT).reshape(stream.shape)
    grad_latter, gain_three = rms_back(latter, gains[2], grad_normed_three)
    grad_latter = grad_latter + cotangent.astype(F32)
    grad_cross_part = grad_latter.astype(BF)
    grad_cross_out = mm(cross_att.reshape(flat), grad_cross_part.reshape(flat), TN).astype(BF)
    grad_catt = mm(grad_cross_part.reshape(flat), w_cross_out, NT).astype(BF)
    grad_catt = grad_catt.reshape(count, rows, width)
    sum_hidden_out = lax.psum_scatter(grad_hidden_out, ALL, scatter_dimension=0, tiled=True)
    sum_second = lax.psum_scatter(
        jnp.concatenate([grad_cross_out, grad_hidden_in], axis=1),
        ALL,
        scatter_dimension=0,
        tiled=True,
    )

    delta = jnp.sum((grad_catt.astype(F32) * cross_sum).reshape(count, rows, H, DH), axis=-1)
    delta = jnp.swapaxes(delta, 1, 2).reshape(cross_lse.shape)
    own_sent = (grad_catt, jnp.concatenate([cross_lse, delta], axis=2))
    peer_sent = core_swap(own_sent)
    far_sent = []
    for step in range(1, chips):
        same = chip_shift(own_sent, step)
        far_sent.append((same, core_swap(same)))

    dq_own, dkv = cross_bwd(ids_of(chip, core), own_q, kv, *own_sent)
    dq_parts = []
    for step in range(1, chips):
        source = (chip - step) % chips
        ids = jnp.concatenate([ids_of(source, core), ids_of(source, 1 - core)])
        queries = jnp.concatenate(
            [pair[0] for pair in far_q[step - 1]] + [pair[1] for pair in far_q[step - 1]], axis=0
        )
        same, crossed = far_sent[step - 1]
        dq, dkv = cross_bwd(
            ids,
            queries,
            kv,
            jnp.concatenate([same[0], crossed[0]], axis=0),
            jnp.concatenate([same[1], crossed[1]], axis=0),
            dkv,
        )
        joint = dq[:count].astype(F32) + core_swap(dq[count:]).astype(F32)
        dq_parts.append(chip_shift(joint.astype(BF), chips - step))
    dq_peer, dkv = cross_bwd(ids_of(chip, 1 - core), peer_q, kv, *peer_sent, dkv)
    total = dq_own.astype(F32) + core_swap(dq_peer).astype(F32)
    for dq in dq_parts:
        total = total + dq.astype(F32)
    grad_cross_q = total.astype(BF).reshape(flat)

    dkv_flat = dkv.reshape(group * keys, 2 * width)
    grad_cross_query = mm(normed_two.reshape(flat), grad_cross_q, TN).astype(BF)
    grad_cross_keyval = mm(enc, dkv_flat, TN).astype(BF)
    sum_cross = lax.psum_scatter(
        jnp.concatenate([grad_cross_query, grad_cross_keyval], axis=1),
        ALL,
        scatter_dimension=0,
        tiled=True,
    )
    encoder_grad = mm(dkv_flat, w_cross_keyval, NT).reshape(encoder_out.shape)

    grad_normed_two = mm(grad_cross_q, w_cross_query, NT).reshape(stream.shape)
    grad_middle, gain_two = rms_back(middle, gains[1], grad_normed_two)
    grad_middle = grad_middle + grad_latter
    grad_self_part = grad_middle.astype(BF).reshape(flat)
    grad_self_out = mm(self_att.reshape(flat), grad_self_part, TN).astype(BF)
    grad_satt = mm(grad_self_part, w_self_out, NT).astype(BF).reshape(count, rows, width)
    grad_qkv = self_bwd(target_lengths, qkv, grad_satt, self_lse).reshape(count * rows, 3 * width)
    grad_self_in = mm(normed_one.reshape(flat), grad_qkv, TN).astype(BF)
    grad_normed_one = mm(grad_qkv, w_self_in, NT).reshape(stream.shape)
    grad_stream, gain_one = rms_back(stream, gains[0], grad_normed_one)
    input_grad = grad_stream + grad_middle
    per_query = jnp.sum(input_grad, axis=1)
    grad_table = jnp.sum(jnp.where(choose[:, :, None], per_query[:, None, :], 0.0), axis=0)
    tiny = jnp.concatenate([jnp.stack([gain_one, gain_two, gain_three]), grad_table], axis=0).T
    tiny = jnp.pad(tiny, ((0, 0), (0, 256 - tiny.shape[1]))).astype(BF)
    sum_self = lax.psum_scatter(
        jnp.concatenate([grad_self_in, grad_self_out, tiny], axis=1),
        ALL,
        scatter_dimension=0,
        tiled=True,
    )

    sets = [
        (ids_of(chip, core), near_lse[:count], near_share[:count], own_sent[1]),
        (ids_of(chip, 1 - core), near_lse[count:], near_share[count:], peer_sent[1]),
    ]
    for step in range(1, chips):
        source = (chip - step) % chips
        for side in range(2):
            lse = jnp.concatenate([lo[0][side : side + 1] for lo in far_local[step - 1]], axis=0)
            share = jnp.concatenate([lo[1][side : side + 1] for lo in far_local[step - 1]], axis=0)
            ids = ids_of(source, core if side == 0 else 1 - core)
            sets.append((ids, lse, share, far_sent[step - 1][side][1]))
    ids = jnp.concatenate([s[0] for s in sets])
    masses = []
    for _, lse, share, stats in sets:
        weight = jnp.exp2(lse - stats[:, :, :2])
        masses.append(jnp.sum(share * weight[:, :, :, None, :], axis=(1, 2, 4)) / (H * rows))
    masses = jnp.concatenate(masses, axis=0)
    place = ids[None, :] == jnp.arange(group, dtype=jnp.int32)[:, None]
    mass = jnp.sum(jnp.where(place[:, :, None], masses[None], 0.0), axis=1)
    query_grad = jnp.sum((retrieval - mass)[:, :, None] * embeds, axis=1)
    hop = 1
    while hop < psg:
        perm = [(p, p ^ hop) for p in range(psg)]
        query_grad = query_grad + lax.ppermute(query_grad, "psg", perm)
        hop *= 2

    small_sum = sum_self[:, 4 * width :].astype(F32).T
    return (
        output,
        input_grad,
        encoder_grad,
        sum_self[:, : 3 * width].astype(F32),
        sum_self[:, 3 * width : 4 * width].astype(F32),
        sum_cross[:, :width].astype(F32),
        sum_cross[:, width:].astype(F32),
        sum_second[:, :width].astype(F32),
        sum_second[:, width:].astype(F32),
        sum_hidden_out.astype(F32),
        small_sum[:3],
        small_sum[3 : 3 + n_tasks],
        query_grad,
    )


def solution(mesh):
    rows = P(ALL, None)
    tokens = P(ALL, None, None)
    passages = P("dp", "psg", None, None)
    columns = P(None, ALL)
    return jax.shard_map(
        on_device,
        mesh=mesh,
        in_specs=(tokens, passages, tokens, P(ALL), P("dp", "psg"), P(ALL), P("dp", None), P())
        + (rows,) * 7
        + (columns, columns),
        out_specs=(tokens, tokens, passages) + (rows,) * 7 + (columns, columns, P("dp", None)),
        check_vma=False,
    )
```

```python
import functools

import jax
import jax.numpy as jnp
from jax import lax
from jax.experimental import pallas as pl
from jax.experimental.pallas import tpu as pltpu
from jax.sharding import PartitionSpec as P

H = 12
DH = 64
PAIR = 2 * DH
BF = jnp.bfloat16
F32 = jnp.float32
LN2 = 0.6931471805599453
QSCALE = 0.125 / LN2
ALL = ("dp", "psg")
NN = (((1,), (0,)), ((), ()))
NT = (((1,), (1,)), ((), ()))
TN = (((0,), (0,)), ((), ()))
VMEM_BYTES = 56 * 2**20


def dot(a, b, dims=NN):
    return lax.dot_general(a, b, dims, preferred_element_type=F32)


def mm(a, b, dims=NN):
    return lax.dot_general(a, b, dims, preferred_element_type=F32)


STEP = 3
SAFE = 80.0


def halves_of(x, h):
    lane = lax.broadcasted_iota(jnp.int32, x.shape, 1)
    return jnp.where((lane >= DH) == (h == 1), x, jnp.zeros((), x.dtype))


def squared_norms(x):
    wide = x.astype(F32)
    return dot(selector(16, 1), (wide * wide).astype(BF), NT)


def params():
    return pltpu.CompilerParams(vmem_limit_bytes=VMEM_BYTES)


def cross_fwd_body(idx, q_ref, k_ref, v_ref, o_ref, lse_ref, share_ref, *, npass):
    keys = k_ref.shape[1]
    blocks = [slice(j * PAIR, (j + 1) * PAIR) for j in range(q_ref.shape[2] // PAIR)]
    col = lax.broadcasted_iota(jnp.int32, (16, keys), 1) // (keys // npass)
    row = lax.broadcasted_iota(jnp.int32, (16, keys), 0)
    member = (col == row).astype(BF)

    def run(shift):
        for j, at in enumerate(blocks):
            q, k, vt = q_ref[0, :, at], k_ref[0, :, at], v_ref[0, :, at].T
            outs = []
            for h in range(2):
                s = dot(k, halves_of(q, h), NT)
                top = jnp.max(s, axis=0, keepdims=True) if shift else None
                p = jnp.exp2(s - top if shift else s).astype(BF)
                ot = dot(jnp.concatenate([vt[h * DH : (h + 1) * DH], member], axis=0), p)
                parts = ot[DH : DH + npass]
                total = jnp.sum(parts, axis=0, keepdims=True)
                inv = 1.0 / total
                outs.append(ot[:DH] * inv)
                lse = jnp.log2(total)
                lse_ref[0, j, h : h + 1, :] = top + lse if shift else lse
                share_ref[0, j, h, :, :] = parts * inv
            o_ref[0, :, at] = jnp.concatenate(outs, axis=0).T.astype(o_ref.dtype)

    longest_q = functools.reduce(jnp.maximum, [squared_norms(q_ref[0, :, at]) for at in blocks])
    longest_k = functools.reduce(jnp.maximum, [squared_norms(k_ref[0, :, at]) for at in blocks])
    small = jnp.max(longest_q) * jnp.max(longest_k) < SAFE * SAFE
    pl.when(small)(lambda: run(False))
    pl.when(jnp.logical_not(small))(lambda: run(True))


def cross_fwd(idx, q, kv, npass):
    nq, rows, width = q.shape
    keys, pairs = kv.shape[1], width // PAIR
    steps, wide = pairs // STEP, STEP * PAIR
    grid = pltpu.PrefetchScalarGridSpec(
        num_scalar_prefetch=1,
        grid=(nq, steps),
        in_specs=[
            pl.BlockSpec((1, rows, wide), lambda n, p, i: (n, 0, p)),
            pl.BlockSpec((1, keys, wide), lambda n, p, i: (i[n], 0, p)),
            pl.BlockSpec((1, keys, wide), lambda n, p, i: (i[n], 0, steps + p)),
        ],
        out_specs=[
            pl.BlockSpec((1, rows, wide), lambda n, p, i: (n, 0, p)),
            pl.BlockSpec((1, STEP, 2, rows), lambda n, p, i: (n, p, 0, 0)),
            pl.BlockSpec((1, STEP, 2, npass, rows), lambda n, p, i: (n, p, 0, 0, 0)),
        ],
    )
    return pl.pallas_call(
        functools.partial(cross_fwd_body, npass=npass),
        grid_spec=grid,
        out_shape=[
            jax.ShapeDtypeStruct(q.shape, BF),
            jax.ShapeDtypeStruct((nq, pairs, 2, rows), F32),
            jax.ShapeDtypeStruct((nq, pairs, 2, npass, rows), F32),
        ],
        compiler_params=params(),
        cost_estimate=pl.CostEstimate(
            flops=16 * nq * rows * keys * width,
            bytes_accessed=4 * nq * (rows + keys) * width,
            transcendentals=nq * H * rows * keys,
        ),
    )(idx, q, kv, kv)


def cross_bwd_body(idx, q_ref, k_ref, v_ref, do_ref, stat_ref, *rest, chunk):
    dq_ref, dkv_ref = rest[-2:]
    first = pl.program_id(1) * STEP
    width = dkv_ref.shape[2] // 2
    rows = q_ref.shape[1]
    for j in range(STEP):
        at = slice(j * PAIR, (j + 1) * PAIR)
        q, k, v, do = q_ref[0, :, at], k_ref[0, :, at], v_ref[0, :, at], do_ref[0, :, at]
        kt = k.T
        dk, dv = 0.0, 0.0
        for c in range(0, rows, chunk):
            outs = []
            for h in range(2):
                qh = halves_of(q[c : c + chunk], h)
                doh = halves_of(do[c : c + chunk], h)
                p = jnp.exp2(dot(k, qh, NT) - stat_ref[0, j, h : h + 1, c : c + chunk])
                dp = dot(v, doh, NT)
                ds = (p * (dp - stat_ref[0, j, 2 + h : 3 + h, c : c + chunk])).astype(BF)
                dv = dv + dot(p.astype(BF), doh)
                dk = dk + dot(ds, qh)
                outs.append(dot(kt[h * DH : (h + 1) * DH], ds))
            dq_ref[0, c : c + chunk, at] = (jnp.concatenate(outs, axis=0).T * 0.125).astype(BF)
        start = pl.multiple_of((first + j) * PAIR, PAIR)
        dkv_ref[0, :, pl.ds(start, PAIR)] = (dk * LN2).astype(BF)
        start = pl.multiple_of(width + (first + j) * PAIR, PAIR)
        dkv_ref[0, :, pl.ds(start, PAIR)] = dv.astype(BF)


def cross_bwd(idx, q, kv, do, stats, earlier=None):
    nq, rows, width = q.shape
    keys, steps, wide = kv.shape[1], width // PAIR // STEP, STEP * PAIR
    in_specs = [
        pl.BlockSpec((1, rows, wide), lambda n, p, i: (n, 0, p)),
        pl.BlockSpec((1, keys, wide), lambda n, p, i: (i[n], 0, p)),
        pl.BlockSpec((1, keys, wide), lambda n, p, i: (i[n], 0, steps + p)),
        pl.BlockSpec((1, rows, wide), lambda n, p, i: (n, 0, p)),
        pl.BlockSpec((1, STEP, 4, rows), lambda n, p, i: (n, p, 0, 0)),
    ]
    operands = [idx, q, kv, kv, do, stats]
    aliases = {}
    if earlier is not None:
        in_specs.append(pl.BlockSpec(memory_space=pl.ANY))
        operands.append(earlier)
        aliases = {6: 1}
    grid = pltpu.PrefetchScalarGridSpec(
        num_scalar_prefetch=1,
        grid=(nq, steps),
        in_specs=in_specs,
        out_specs=[
            pl.BlockSpec((1, rows, wide), lambda n, p, i: (n, 0, p)),
            pl.BlockSpec((1, keys, 2 * width), lambda n, p, i: (i[n], 0, 0)),
        ],
    )
    return pl.pallas_call(
        functools.partial(cross_bwd_body, chunk=min(rows, 256)),
        grid_spec=grid,
        input_output_aliases=aliases,
        out_shape=[jax.ShapeDtypeStruct(q.shape, BF), jax.ShapeDtypeStruct(kv.shape, BF)],
        compiler_params=params(),
        cost_estimate=pl.CostEstimate(
            flops=40 * nq * rows * keys * width,
            bytes_accessed=nq * (6 * rows + 8 * keys) * width,
            transcendentals=nq * H * rows * keys,
        ),
    )(*operands)


def self_mask(rows, length):
    key = lax.broadcasted_iota(jnp.int32, (rows, rows), 0)
    row = lax.broadcasted_iota(jnp.int32, (rows, rows), 1)
    return (key <= row) & (key < length)


def self_fwd_body(length_ref, q_ref, k_ref, v_ref, o_ref, lse_ref):
    rows = q_ref.shape[1]
    allowed = self_mask(rows, length_ref[pl.program_id(0)])
    ones = jnp.ones((16, rows), BF)
    for j in range(STEP):
        at = slice(j * PAIR, (j + 1) * PAIR)
        q, k, vt = q_ref[0, :, at], k_ref[0, :, at], v_ref[0, :, at].T
        outs = []
        for h in range(2):
            s = jnp.where(allowed, dot(k, halves_of(q, h), NT), -1e30)
            top = jnp.max(s, axis=0, keepdims=True)
            p = jnp.exp2(s - top).astype(BF)
            ot = dot(jnp.concatenate([vt[h * DH : (h + 1) * DH], ones], axis=0), p)
            total = ot[DH : DH + 1]
            outs.append(ot[:DH] * (1.0 / total))
            lse_ref[0, j, h : h + 1, :] = top + jnp.log2(total)
        o_ref[0, :, at] = jnp.concatenate(outs, axis=0).T.astype(BF)


def self_fwd(lengths, qkv):
    nq, rows, width = qkv.shape[0], qkv.shape[1], qkv.shape[2] // 3
    pairs = width // PAIR
    steps, wide = pairs // STEP, STEP * PAIR
    grid = pltpu.PrefetchScalarGridSpec(
        num_scalar_prefetch=1,
        grid=(nq, steps),
        in_specs=[
            pl.BlockSpec((1, rows, wide), lambda n, p, i: (n, 0, p)),
            pl.BlockSpec((1, rows, wide), lambda n, p, i: (n, 0, steps + p)),
            pl.BlockSpec((1, rows, wide), lambda n, p, i: (n, 0, 2 * steps + p)),
        ],
        out_specs=[
            pl.BlockSpec((1, rows, wide), lambda n, p, i: (n, 0, p)),
            pl.BlockSpec((1, STEP, 2, rows), lambda n, p, i: (n, p, 0, 0)),
        ],
    )
    return pl.pallas_call(
        self_fwd_body,
        grid_spec=grid,
        out_shape=[
            jax.ShapeDtypeStruct((nq, rows, width), BF),
            jax.ShapeDtypeStruct((nq, pairs, 2, rows), F32),
        ],
        compiler_params=params(),
        cost_estimate=pl.CostEstimate(
            flops=16 * nq * rows * rows * width,
            bytes_accessed=8 * nq * rows * width,
            transcendentals=nq * H * rows * rows,
        ),
    )(lengths, qkv, qkv, qkv)


def self_bwd_body(length_ref, q_ref, k_ref, v_ref, do_ref, lse_ref, out_ref, dk_acc, dv_acc, *, chunk):
    length = length_ref[pl.program_id(0)]
    first = pl.program_id(1) * STEP
    width = out_ref.shape[2] // 3
    rows = q_ref.shape[1]
    for j in range(STEP):
        at = slice(j * PAIR, (j + 1) * PAIR)
        q, k, v, do = q_ref[0, :, at], k_ref[0, :, at], v_ref[0, :, at], do_ref[0, :, at]
        kt = k.T
        start = pl.multiple_of((first + j) * PAIR, PAIR)
        for c in reversed(range(0, rows, chunk)):
            keys = c + chunk
            key = lax.broadcasted_iota(jnp.int32, (keys, chunk), 0)
            row = lax.broadcasted_iota(jnp.int32, (keys, chunk), 1) + c
            allowed = (key <= row) & (key < length)
            outs = []
            dk, dv = 0.0, 0.0
            for h in range(2):
                qh = halves_of(q[c : c + chunk], h)
                doh = halves_of(do[c : c + chunk], h)
                s = jnp.where(allowed, dot(k[:keys], qh, NT), -1e30)
                p = jnp.exp2(s - lse_ref[0, j, h : h + 1, c : c + chunk])
                dp = dot(v[:keys], doh, NT)
                delta = jnp.sum(p * dp, axis=0, keepdims=True)
                ds = (p * (dp - delta)).astype(BF)
                dv = dv + dot(p.astype(BF), doh)
                dk = dk + dot(ds, qh)
                outs.append(dot(kt[h * DH : (h + 1) * DH, :keys], ds))
            if keys == rows:
                dk_acc[...], dv_acc[...] = dk, dv
            else:
                dk_acc[:keys] += dk
                dv_acc[:keys] += dv
            out_ref[0, c : c + chunk, pl.ds(start, PAIR)] = (
                jnp.concatenate(outs, axis=0).T * 0.125
            ).astype(BF)
        start = pl.multiple_of(width + (first + j) * PAIR, PAIR)
        out_ref[0, :, pl.ds(start, PAIR)] = (dk_acc[...] * LN2).astype(BF)
        start = pl.multiple_of(2 * width + (first + j) * PAIR, PAIR)
        out_ref[0, :, pl.ds(start, PAIR)] = dv_acc[...].astype(BF)


def self_bwd(lengths, qkv, do, lse):
    nq, rows, width = do.shape
    steps, wide = width // PAIR // STEP, STEP * PAIR
    grid = pltpu.PrefetchScalarGridSpec(
        num_scalar_prefetch=1,
        grid=(nq, steps),
        in_specs=[
            pl.BlockSpec((1, rows, wide), lambda n, p, i: (n, 0, p)),
            pl.BlockSpec((1, rows, wide), lambda n, p, i: (n, 0, steps + p)),
            pl.BlockSpec((1, rows, wide), lambda n, p, i: (n, 0, 2 * steps + p)),
            pl.BlockSpec((1, rows, wide), lambda n, p, i: (n, 0, p)),
            pl.BlockSpec((1, STEP, 2, rows), lambda n, p, i: (n, p, 0, 0)),
        ],
        out_specs=[pl.BlockSpec((1, rows, 3 * width), lambda n, p, i: (n, 0, 0))],
        scratch_shapes=[pltpu.VMEM((rows, PAIR), F32), pltpu.VMEM((rows, PAIR), F32)],
    )
    return pl.pallas_call(
        functools.partial(self_bwd_body, chunk=min(rows, 256)),
        grid_spec=grid,
        out_shape=[jax.ShapeDtypeStruct((nq, rows, 3 * width), BF)],
        compiler_params=params(),
        cost_estimate=pl.CostEstimate(
            flops=40 * nq * rows * rows * width,
            bytes_accessed=16 * nq * rows * width,
            transcendentals=nq * H * rows * rows,
        ),
    )(lengths, qkv, qkv, qkv, do, lse)[0]


def selector(rows, levels):
    row = lax.broadcasted_iota(jnp.int32, (rows, PAIR), 0)
    lane = lax.broadcasted_iota(jnp.int32, (rows, PAIR), 1)
    return (((lane >= DH) == (row % 2 == 1)) & (row < 2 * levels)).astype(BF)


def merge_body(*refs, parts, full):
    values, lses, outs = refs[:parts], refs[parts : 2 * parts], refs[2 * parts :]
    rows = values[0].shape[1]
    row = lax.broadcasted_iota(jnp.int32, (16, rows), 0)
    pick = selector(16, 2)
    for j in range(values[0].shape[2] // PAIR):
        at = slice(j * PAIR, (j + 1) * PAIR)
        top = functools.reduce(jnp.maximum, [lse[0, j] for lse in lses])
        weights = [jnp.exp2(lse[0, j] - top) for lse in lses]
        total = functools.reduce(jnp.add, weights)
        inv = 1.0 / total
        out = 0.0
        for value, weight in zip(values, weights):
            w = weight * inv
            both = jnp.where(row % 2 == 1, w[1:2], w[0:1])
            high = both.astype(BF).astype(F32)
            split = jnp.where(row < 2, high, both - high).astype(BF)
            out = out + value[0, :, at].astype(F32) * dot(split, pick, TN)
        outs[0][0, :, at] = out.astype(BF)
        outs[1][0, j] = top + jnp.log2(total)
        if full:
            outs[2][0, :, at] = out


def merge(parts, full=False):
    nq, rows, width = parts[0][0].shape
    pairs = width // PAIR
    wide = pl.BlockSpec((1, rows, width), lambda n: (n, 0, 0))
    stat = pl.BlockSpec((1, pairs, 2, rows), lambda n: (n, 0, 0, 0))
    return pl.pallas_call(
        functools.partial(merge_body, parts=len(parts), full=full),
        grid=(nq,),
        in_specs=[wide] * len(parts) + [stat] * len(parts),
        out_specs=[wide, stat] + [wide] * full,
        out_shape=[
            jax.ShapeDtypeStruct((nq, rows, width), BF),
            jax.ShapeDtypeStruct((nq, pairs, 2, rows), F32),
        ]
        + [jax.ShapeDtypeStruct((nq, rows, width), F32)] * full,
        compiler_params=params(),
        cost_estimate=pl.CostEstimate(
            flops=4 * nq * rows * width,
            bytes_accessed=nq * rows * width * (2 * len(parts) + 2 + 4 * full),
            transcendentals=nq * H * rows,
        ),
    )(*[p[0] for p in parts], *[p[1] for p in parts])


def stats_body(do_ref, sum_ref, lse_ref, out_ref):
    pick = selector(16, 1)
    for j in range(do_ref.shape[2] // PAIR):
        at = slice(j * PAIR, (j + 1) * PAIR)
        product = do_ref[0, :, at].astype(F32) * sum_ref[0, :, at]
        high = product.astype(BF)
        low = (product - high.astype(F32)).astype(BF)
        out_ref[0, j, 0:2] = lse_ref[0, j]
        out_ref[0, j, 2:4] = (dot(pick, high, NT) + dot(pick, low, NT))[0:2]


def row_stats(do, cross_sum, lse):
    nq, rows, width = do.shape
    pairs = width // PAIR
    wide = pl.BlockSpec((1, rows, width), lambda n: (n, 0, 0))
    return pl.pallas_call(
        stats_body,
        grid=(nq,),
        in_specs=[wide, wide, pl.BlockSpec((1, pairs, 2, rows), lambda n: (n, 0, 0, 0))],
        out_specs=pl.BlockSpec((1, pairs, 4, rows), lambda n: (n, 0, 0, 0)),
        out_shape=jax.ShapeDtypeStruct((nq, pairs, 4, rows), F32),
        compiler_params=params(),
        cost_estimate=pl.CostEstimate(
            flops=4 * nq * rows * width, bytes_accessed=6 * nq * rows * width, transcendentals=0
        ),
    )(do, cross_sum, lse)


def keyval_body(enc_ref, w_ref, out_ref):
    out_ref[...] = dot(enc_ref[...], w_ref[...]).astype(BF)


def keyval(enc, w):
    n, depth = enc.shape
    width = w.shape[1]
    block = 512
    return pl.pallas_call(
        keyval_body,
        grid=(n // block,),
        in_specs=[
            pl.BlockSpec((block, depth), lambda i: (i, 0)),
            pl.BlockSpec((depth, width), lambda i: (0, 0)),
        ],
        out_specs=pl.BlockSpec((block, width), lambda i: (i, 0)),
        out_shape=jax.ShapeDtypeStruct((n, width), BF),
        compiler_params=params(),
        cost_estimate=pl.CostEstimate(
            flops=2 * n * depth * width, bytes_accessed=2 * n * (depth + width), transcendentals=0
        ),
    )(enc, w)


def bits_below(n):
    return [1 << b for b in range(n.bit_length() - 1)]


def exchanges():
    dp, psg = lax.axis_size("dp"), lax.axis_size("psg")
    flat = bits_below(dp)
    cut = max(1, len(flat) // 3)
    xs = [("dp", b) for b in flat[:cut]]
    zs = [("dp", b) for b in flat[cut:]]
    ys = [("psg", b) for b in bits_below(psg)[1:]]
    order = [("dp", b) for b in reversed(flat)] + [("psg", b) for b in reversed(bits_below(psg))]
    return ("psg", 1), xs, ys, zs, order


def swap_bit(x, hop):
    axis, bit = hop
    n = lax.axis_size(axis)
    return lax.ppermute(x, axis, [(p, p ^ bit) for p in range(n)])


def my_bit(hop):
    return (lax.axis_index(hop[0]) // hop[1]) % 2


def after(x, *others):
    return lax.optimization_barrier((x, others))[0]


def partner(hop):
    axis, bit = hop
    me = lax.axis_index(axis)
    return {axis: me + bit * (1 - 2 * ((me // bit) % 2))}


def gather_body(*refs, columns, core, orders, order):
    n, n_out = len(columns), 1 + max(c[0] for c in columns)
    ins, outs = refs[:n], refs[n : n + n_out]
    local, send, recv = refs[n + n_out :]
    place = tuple(my_bit(h) for h in order)

    def block(k, have, flip=None):
        out, start, width = columns[k]
        at = tuple(
            slice(None) if h in have else 1 - p if h == flip else p for h, p in zip(order, place)
        )
        return outs[out].at[at + (slice(None), pl.ds(start, width))]

    def copy(k, ref, hop, sem):
        moved = pltpu.make_async_remote_copy(
            src_ref=ref,
            dst_ref=ref,
            send_sem=send.at[k, sem],
            recv_sem=recv.at[k, sem],
            device_id=partner(hop),
            device_id_type=pl.DeviceIdType.MESH,
        )
        moved.start()
        return moved

    own = [pltpu.make_async_copy(ins[k], block(k, ()), local.at[k]) for k in range(n)]
    for c in own:
        c.start()
    barrier = pltpu.get_barrier_semaphore()
    for hop in order:
        pl.semaphore_signal(
            barrier, inc=1, device_id=partner(hop), device_id_type=pl.DeviceIdType.MESH
        )
    pl.semaphore_wait(barrier, len(order))
    for c in own:
        c.wait()
    steps = len(order) - 1
    far = [[] for _ in range(n)]
    near = [[] for _ in range(n)]
    for k in range(n):
        far[k].append(copy(k, block(k, ()), orders[k][0], 0))
        near[k].append(copy(k, block(k, ()), core, steps))
    for t in range(steps):
        for k in range(n):
            have = orders[k][:t]
            far[k][t].wait_recv()
            if t + 1 < steps:
                far[k].append(copy(k, block(k, orders[k][: t + 1]), orders[k][t + 1], t + 1))
            near[k].append(copy(k, block(k, have, orders[k][t]), core, steps + 1 + t))
    for k in range(n):
        for c in far[k]:
            c.wait_send()
        for c in near[k]:
            c.wait()


def gather_rows(stripes, columns, widths):
    core, xs, ys, zs, order = exchanges()
    orders = [zs + xs + ys, zs + ys + xs, xs + zs + ys, ys + zs + xs, xs + ys + zs]
    orders = [orders[k % len(orders)] for k in range(len(stripes))]
    rows, n = stripes[0].shape[0], len(stripes)
    outs = pl.pallas_call(
        functools.partial(gather_body, columns=columns, core=core, orders=orders, order=order),
        in_specs=[pl.BlockSpec(memory_space=pl.ANY)] * n,
        out_specs=[pl.BlockSpec(memory_space=pl.ANY)] * len(widths),
        out_shape=[
            jax.ShapeDtypeStruct((2,) * len(order) + (rows, w), stripes[0].dtype) for w in widths
        ],
        scratch_shapes=[
            pltpu.SemaphoreType.DMA((n,)),
            pltpu.SemaphoreType.DMA((n, 2 * len(order))),
            pltpu.SemaphoreType.DMA((n, 2 * len(order))),
        ],
        compiler_params=pltpu.CompilerParams(collective_id=0, has_side_effects=True),
    )(*stripes)
    return [o.reshape(rows << len(order), o.shape[-1]) for o in outs]


def sum_rows(stripes, work):
    core, xs, ys, zs, order = exchanges()
    hops = [[core] + h for h in (xs + ys + zs, ys + zs + xs, zs + xs + ys)]
    states = [[a.reshape((2,) * len(order) + (-1, a.shape[1])) for a in s] for s in stripes]
    names = [order] * len(stripes)
    made = []
    for step in range(len(order)):
        keep, send = [], []
        for arrays, held, hop in zip(states, names, [h[step] for h in hops]):
            at, bit = held.index(hop), my_bit(hop)
            for side, b in ((keep, bit), (send, 1 - bit)):
                side.append(
                    jnp.concatenate(
                        [lax.dynamic_index_in_dim(a, b, at, keepdims=False) for a in arrays], axis=-1
                    )
                )
        send = lax.optimization_barrier(send)
        got = [swap_bit(x, h[step]) for x, h in zip(send, hops)]
        if step < len(work):
            made.append(work[step](send))
            got = after(got, made[-1])
        got = lax.optimization_barrier(got)
        states = [[(k.astype(F32) + g.astype(F32)).astype(BF)] for k, g in zip(keep, got)]
        names = [[n for n in held if n != h[step]] for held, h in zip(names, hops)]
    return [arrays[0] for arrays in states], made


def rms_parts(v):
    return lax.rsqrt(jnp.mean(v * v, axis=-1, keepdims=True) + 1e-06)


def rms_back(v, gain, b):
    r = rms_parts(v)
    gb = gain * b
    grad = r * gb - v * (r * r * r * jnp.mean(v * gb, axis=-1, keepdims=True))
    return grad, jnp.sum(v * r * b, axis=tuple(range(v.ndim - 1)))


def gelu_and_slope(u):
    t = jnp.tanh(0.7978845608028654 * (u + 0.044715 * u * u * u))
    slope = 0.5 * (1.0 + t) + 0.5 * u * (1.0 - t * t) * (
        0.7978845608028654 * (1.0 + 3.0 * 0.044715 * u * u)
    )
    return 0.5 * u * (1.0 + t), slope


def on_device(
    decoder_input,
    encoder_out,
    cotangent,
    task_ids,
    passage_ids,
    target_lengths,
    query_embed,
    passage_bank,
    self_in,
    self_out,
    cross_query,
    cross_keyval,
    cross_out,
    hidden_in,
    hidden_output_weight,
    norm_gains,
    task_table,
):
    count, rows, width = decoder_input.shape
    group, npass, tokens, _ = encoder_out.shape
    keys = npass * tokens
    psg = lax.axis_size("psg")
    chips = psg // 2
    me = lax.axis_index("psg")
    chip, core = me // 2, me % 2
    shard = self_in.shape[0]
    ff = hidden_in.shape[1]
    n_tasks = task_table.shape[0]

    swap = [(p, p ^ 1) for p in range(psg)]

    def core_swap(x):
        return jax.tree.map(lambda a: lax.ppermute(a, "psg", swap), x)

    def chip_shift(x, step):
        perm = [(p, (p + 2 * step) % psg) for p in range(psg)]
        return jax.tree.map(lambda a: lax.ppermute(a, "psg", perm), x)

    def ids_of(chip_at, core_at):
        return (chip_at * 2 + core_at) * count + jnp.arange(count, dtype=jnp.int32)

    small = jnp.concatenate([norm_gains, task_table], axis=0).T
    small = jnp.pad(small, ((0, 0), (0, 128 - small.shape[1])))
    enc = encoder_out.reshape(group * keys, width)
    w_self_in, w_out, w_rest = gather_rows(
        [self_in[:, k * width : (k + 1) * width] for k in range(3)]
        + [self_out, jnp.concatenate([cross_query, small], axis=1)],
        [(0, 0, width), (0, width, width), (0, 2 * width, width), (1, 0, width), (2, 0, width + 128)],
        [3 * width, width, width + 128],
    )
    w_self_out, w_cross_query, w_small = w_out, w_rest[:, :width], w_rest[:, width:]
    w_keyval = lax.all_gather(cross_keyval, ALL, axis=0, tiled=True)

    embeds = jnp.take(passage_bank, passage_ids, axis=0).astype(F32)
    score = jnp.sum(query_embed[:, None, :] * embeds, axis=-1)
    others = [
        lax.ppermute(score, "psg", [(p, (p + k) % psg) for p in range(psg)]) for k in range(1, psg)
    ]
    every = jnp.concatenate([score] + others, axis=1)
    top = jnp.max(every, axis=1, keepdims=True)
    retrieval = jnp.exp(score - top) / jnp.sum(jnp.exp(every - top), axis=1, keepdims=True)

    smalls = w_small.T.astype(F32)
    gains, table = smalls[:3], smalls[3 : 3 + n_tasks]
    choose = task_ids[:, None] == jnp.arange(n_tasks, dtype=jnp.int32)[None, :]
    task_rows = jnp.sum(jnp.where(choose[:, :, None], table[None], 0.0), axis=1)

    stream = decoder_input.astype(F32) + task_rows[:, None, :]
    normed_one = (stream * rms_parts(stream) * gains[0]).astype(BF)
    col = lax.broadcasted_iota(jnp.int32, (1, 3 * width), 1)
    scale = jnp.where(col < width, QSCALE, 1.0)
    flat = (count * rows, width)
    qkv = (mm(normed_one.reshape(flat), w_self_in) * scale).astype(BF)
    qkv = qkv.reshape(count, rows, 3 * width)
    self_att, self_lse = self_fwd(target_lengths, qkv)
    second = lax.all_gather(
        after(jnp.concatenate([cross_out, hidden_in], axis=1), self_att), ALL, axis=0, tiled=True
    )
    w_cross_out, w_hidden_in = second[:, :width], second[:, width:]
    w_hidden_out = lax.all_gather(
        after(hidden_output_weight, self_att), ALL, axis=0, tiled=True
    )
    middle = stream + mm(self_att.reshape(flat), w_self_out).reshape(stream.shape)
    normed_two = (middle * rms_parts(middle) * gains[1]).astype(BF)
    own_q = (mm(normed_two.reshape(flat), w_cross_query) * QSCALE).astype(BF)
    own_q = own_q.reshape(count, rows, width)

    near_ids = (ids_of(chip, core), ids_of(chip, 1 - core))
    far_ids, far_same_q = [], []
    for step in range(1, chips):
        far_same_q.append([chip_shift(own_q[n : n + 1], step) for n in range(count)])
        source = (chip - step) % chips
        far_ids.append((ids_of(source, core), ids_of(source, 1 - core)))
    peer_q = core_swap(own_q)
    kv = keyval(after(enc, own_q), w_keyval).reshape(group, keys, 2 * width)
    peer_part = cross_fwd(near_ids[1], peer_q, kv, npass)
    latest = peer_part
    far_q, far_local, far_back = [], [], []
    for step in range(1, chips):
        queries, local, back = [], [], []
        for n in range(count):
            same_q = after(far_same_q[step - 1][n], latest)
            crossed_q = core_swap(same_q)
            same = cross_fwd(far_ids[step - 1][0][n : n + 1], same_q, kv, npass)
            crossed = cross_fwd(
                far_ids[step - 1][1][n : n + 1], after(crossed_q, same), kv, npass
            )
            value, joint = merge([same[:2], core_swap(crossed[:2])])
            latest = crossed
            back.append(chip_shift((value, joint), chips - step))
            local.append((same[1:], crossed[1:]))
            queries.append((same_q, crossed_q))
        far_q.append(queries)
        far_local.append(local)
        far_back.append(back)
    own_part = cross_fwd(near_ids[0], after(own_q, latest), kv, npass)
    parts = [own_part[:2], core_swap(peer_part[:2])]
    for back in far_back:
        parts.append(tuple(jnp.concatenate([b[k] for b in back], axis=0) for k in range(2)))
    cross_att, cross_lse, cross_sum = merge(parts, full=True)

    latter = middle + mm(cross_att.reshape(flat), w_cross_out).reshape(stream.shape)
    normed_three = (latter * rms_parts(latter) * gains[2]).astype(BF)
    hidden_pre = mm(normed_three.reshape(flat), w_hidden_in)
    activated, slope = gelu_and_slope(hidden_pre)
    activated = activated.astype(BF)
    output = (latter + mm(activated, w_hidden_out).reshape(stream.shape)).astype(BF)
    cot = cotangent.reshape(flat)
    grad_hidden_out = mm(activated, cot, TN).astype(BF)
    grad_pre = (mm(cot, w_hidden_out, NT) * slope).astype(BF)
    grad_hidden_in = mm(normed_three.reshape(flat), grad_pre, TN).astype(BF)
    grad_normed_three = mm(grad_pre, w_hidden_in, NT).reshape(stream.shape)
    grad_latter, gain_three = rms_back(latter, gains[2], grad_normed_three)
    grad_latter = grad_latter + cotangent.astype(F32)
    grad_cross_part = grad_latter.astype(BF)
    grad_cross_out = mm(cross_att.reshape(flat), grad_cross_part.reshape(flat), TN).astype(BF)
    grad_catt = mm(grad_cross_part.reshape(flat), w_cross_out, NT).astype(BF)
    grad_catt = grad_catt.reshape(count, rows, width)
    fold = hidden_output_weight.shape[0] // shard
    folded = grad_hidden_out.reshape(-1, fold, shard, width)
    folded = [folded[:, k].reshape(-1, width) for k in range(fold)]
    grad_second = jnp.concatenate([grad_cross_out, grad_hidden_in] + folded, axis=1)
    sum_second = lax.psum_scatter(grad_second, ALL, scatter_dimension=0, tiled=True)

    own_sent = (grad_catt, row_stats(grad_catt, cross_sum, cross_lse))
    far_same = [chip_shift(own_sent, step) for step in range(1, chips)]
    peer_sent = core_swap(own_sent)
    dq_own, dkv = cross_bwd(near_ids[0], own_q, kv, *after(own_sent, grad_second))
    far_same = [after(same, dq_own) for same in far_same]
    far_sent = [(same, core_swap(same)) for same in far_same]
    dq_peer, dkv = cross_bwd(near_ids[1], peer_q, kv, *after(peer_sent, dq_own), dkv)
    dq_back = core_swap(dq_peer)
    latest = dq_peer
    dq_parts = []
    for step in range(1, chips):
        same, crossed = far_sent[step - 1]
        back = []
        for n in range(count):
            same_q, crossed_q = far_q[step - 1][n]
            one = slice(n, n + 1)
            sent = [x[one] for x in after(crossed, latest)]
            dq_crossed, dkv = cross_bwd(far_ids[step - 1][1][one], crossed_q, kv, *sent, dkv)
            sent = [x[one] for x in same]
            dq_same, dkv = cross_bwd(far_ids[step - 1][0][one], same_q, kv, *sent, dkv)
            joint = (dq_same.astype(F32) + core_swap(dq_crossed).astype(F32)).astype(BF)
            latest = dq_same
            back.append(chip_shift(joint, chips - step))
        dq_parts.append(jnp.concatenate(back, axis=0))
    dkv_flat = after(dkv, joint).reshape(group * keys, 2 * width)
    grad_cross_keyval = mm(enc, dkv_flat, TN).astype(BF)
    total = dq_own.astype(F32) + dq_back.astype(F32)
    for dq in after(dq_parts, grad_cross_keyval, sum_second):
        total = total + dq.astype(F32)
    grad_cross_q = total.astype(BF).reshape(flat)
    grad_cross_query = mm(normed_two.reshape(flat), grad_cross_q, TN).astype(BF)

    grad_normed_two = mm(grad_cross_q, w_cross_query, NT).reshape(stream.shape)
    grad_middle, gain_two = rms_back(middle, gains[1], grad_normed_two)
    grad_middle = grad_middle + grad_latter
    grad_self_part = grad_middle.astype(BF).reshape(flat)
    grad_self_out = mm(self_att.reshape(flat), grad_self_part, TN).astype(BF)
    grad_satt = mm(grad_self_part, w_self_out, NT).astype(BF).reshape(count, rows, width)
    grad_qkv = self_bwd(target_lengths, qkv, grad_satt, self_lse)
    grad_qkv = grad_qkv.reshape(count * rows, 3 * width)
    grad_normed_one = mm(grad_qkv, w_self_in, NT).reshape(stream.shape)
    grad_stream, gain_one = rms_back(stream, gains[0], grad_normed_one)
    input_grad = grad_stream + grad_middle
    per_query = jnp.sum(input_grad, axis=1)
    grad_table = jnp.sum(jnp.where(choose[:, :, None], per_query[:, None, :], 0.0), axis=0)
    tiny = jnp.concatenate([jnp.stack([gain_one, gain_two, gain_three]), grad_table], axis=0).T
    tiny = jnp.pad(tiny, ((0, 0), (0, 128 - tiny.shape[1]))).astype(BF)
    grad_self_in = mm(normed_one.reshape(flat), grad_qkv, TN).astype(BF)

    def distillation(sent):
        sets = [
            (near_ids[0], *own_part[1:], own_sent[1]),
            (near_ids[1], *peer_part[1:], peer_sent[1]),
        ]
        for step in range(1, chips):
            for side in range(2):
                lse, share = (
                    jnp.concatenate([lo[side][k] for lo in far_local[step - 1]], axis=0)
                    for k in range(2)
                )
                sets.append((far_ids[step - 1][side], lse, share, far_sent[step - 1][side][1]))
        ids = jnp.concatenate([s[0] for s in sets])
        masses = []
        for _, lse, share, stats in sets:
            weight = jnp.exp2(lse - stats[:, :, :2])
            masses.append(jnp.sum(share * weight[:, :, :, None, :], axis=(1, 2, 4)) / (H * rows))
        masses = jnp.concatenate(masses, axis=0)
        place = ids[None, :] == jnp.arange(group, dtype=jnp.int32)[:, None]
        mass = jnp.sum(jnp.where(place[:, :, None], masses[None], 0.0), axis=1)
        query_grad = jnp.sum((after(retrieval, sent) - mass)[:, :, None] * embeds, axis=1)
        hop = 1
        while hop < psg:
            perm = [(p, p ^ hop) for p in range(psg)]
            query_grad = query_grad + lax.ppermute(query_grad, "psg", perm)
            hop *= 2
        return query_grad

    def encoder_part(sent):
        return mm(after(dkv_flat, sent), w_keyval, NT).reshape(encoder_out.shape)

    half = width // 2
    summed, (query_grad, encoder_grad) = sum_rows(
        [
            [grad_self_in[:, :width], grad_cross_query, tiny],
            [grad_self_in[:, width : 2 * width], grad_cross_keyval[:, :width], grad_self_out[:, :half]],
            [grad_self_in[:, 2 * width :], grad_cross_keyval[:, width:], grad_self_out[:, half:]],
        ],
        [distillation, encoder_part],
    )
    summed = [x.astype(F32) for x in summed]
    small_sum = summed[0][:, 2 * width :].T
    return (
        output,
        input_grad,
        encoder_grad,
        jnp.concatenate([x[:, :width] for x in summed], axis=1),
        jnp.concatenate([x[:, 2 * width :] for x in summed[1:]], axis=1),
        summed[0][:, width : 2 * width],
        jnp.concatenate([x[:, width : 2 * width] for x in summed[1:]], axis=1),
        sum_second[:, :width].astype(F32),
        sum_second[:, width : width + ff].astype(F32),
        jnp.concatenate(
            [sum_second[:, width * k : width * (k + 1)] for k in range(1 + ff // width, 1 + ff // width + fold)]
        ).astype(F32),
        small_sum[:3],
        small_sum[3 : 3 + n_tasks],
        query_grad,
    )


def solution(mesh):
    rows = P(ALL, None)
    tokens = P(ALL, None, None)
    passages = P("dp", "psg", None, None)
    columns = P(None, ALL)
    return jax.shard_map(
        on_device,
        mesh=mesh,
        in_specs=(tokens, passages, tokens, P(ALL), P("dp", "psg"), P(ALL), P("dp", None), P())
        + (rows,) * 7
        + (columns, columns),
        out_specs=(tokens, tokens, passages) + (rows,) * 7 + (columns, columns, P("dp", None)),
        check_vma=False,
    )
```

```python
import functools

import jax
import jax.numpy as jnp
from jax import lax
from jax.experimental import pallas as pl
from jax.experimental.pallas import tpu as pltpu
from jax.sharding import PartitionSpec as P

H = 12
DH = 64
PAIR = 2 * DH
BF = jnp.bfloat16
F32 = jnp.float32
LN2 = 0.6931471805599453
QSCALE = 0.125 / LN2
ALL = ("dp", "psg")
NN = (((1,), (0,)), ((), ()))
NT = (((1,), (1,)), ((), ()))
TN = (((0,), (0,)), ((), ()))
VMEM_BYTES = 56 * 2**20


def dot(a, b, dims=NN):
    return lax.dot_general(a, b, dims, preferred_element_type=F32)


def mm(a, b, dims=NN):
    return lax.dot_general(a, b, dims, preferred_element_type=F32)


STEP = 3
SAFE = 80.0


def halves_of(x, h):
    lane = lax.broadcasted_iota(jnp.int32, x.shape, 1)
    return jnp.where((lane >= DH) == (h == 1), x, jnp.zeros((), x.dtype))


def squared_norms(x):
    wide = x.astype(F32)
    return dot(selector(16, 1), (wide * wide).astype(BF), NT)


def params():
    return pltpu.CompilerParams(vmem_limit_bytes=VMEM_BYTES)


def cross_fwd_body(idx, q_ref, k_ref, v_ref, o_ref, lse_ref, share_ref, *, npass):
    keys = k_ref.shape[1]
    blocks = [slice(j * PAIR, (j + 1) * PAIR) for j in range(q_ref.shape[2] // PAIR)]
    col = lax.broadcasted_iota(jnp.int32, (16, keys), 1) // (keys // npass)
    row = lax.broadcasted_iota(jnp.int32, (16, keys), 0)
    member = (col == row).astype(BF)

    def run(shift):
        for j, at in enumerate(blocks):
            q, k, vt = q_ref[0, :, at], k_ref[0, :, at], v_ref[0, :, at].T
            outs = []
            for h in range(2):
                s = dot(k, halves_of(q, h), NT)
                top = jnp.max(s, axis=0, keepdims=True) if shift else None
                p = jnp.exp2(s - top if shift else s).astype(BF)
                ot = dot(jnp.concatenate([vt[h * DH : (h + 1) * DH], member], axis=0), p)
                parts = ot[DH : DH + npass]
                total = jnp.sum(parts, axis=0, keepdims=True)
                inv = 1.0 / total
                outs.append(ot[:DH] * inv)
                lse = jnp.log2(total)
                lse_ref[0, j, h : h + 1, :] = top + lse if shift else lse
                share_ref[0, j, h, :, :] = parts * inv
            o_ref[0, :, at] = jnp.concatenate(outs, axis=0).T.astype(o_ref.dtype)

    longest_q = functools.reduce(jnp.maximum, [squared_norms(q_ref[0, :, at]) for at in blocks])
    longest_k = functools.reduce(jnp.maximum, [squared_norms(k_ref[0, :, at]) for at in blocks])
    small = jnp.max(longest_q) * jnp.max(longest_k) < SAFE * SAFE
    pl.when(small)(lambda: run(False))
    pl.when(jnp.logical_not(small))(lambda: run(True))


def cross_fwd(idx, q, kv, npass):
    nq, rows, width = q.shape
    keys, pairs = kv.shape[1], width // PAIR
    steps, wide = pairs // STEP, STEP * PAIR
    grid = pltpu.PrefetchScalarGridSpec(
        num_scalar_prefetch=1,
        grid=(nq, steps),
        in_specs=[
            pl.BlockSpec((1, rows, wide), lambda n, p, i: (n, 0, p)),
            pl.BlockSpec((1, keys, wide), lambda n, p, i: (i[n], 0, p)),
            pl.BlockSpec((1, keys, wide), lambda n, p, i: (i[n], 0, steps + p)),
        ],
        out_specs=[
            pl.BlockSpec((1, rows, wide), lambda n, p, i: (n, 0, p)),
            pl.BlockSpec((1, STEP, 2, rows), lambda n, p, i: (n, p, 0, 0)),
            pl.BlockSpec((1, STEP, 2, npass, rows), lambda n, p, i: (n, p, 0, 0, 0)),
        ],
    )
    return pl.pallas_call(
        functools.partial(cross_fwd_body, npass=npass),
        grid_spec=grid,
        out_shape=[
            jax.ShapeDtypeStruct(q.shape, BF),
            jax.ShapeDtypeStruct((nq, pairs, 2, rows), F32),
            jax.ShapeDtypeStruct((nq, pairs, 2, npass, rows), F32),
        ],
        compiler_params=params(),
        cost_estimate=pl.CostEstimate(
            flops=16 * nq * rows * keys * width,
            bytes_accessed=4 * nq * (rows + keys) * width,
            transcendentals=nq * H * rows * keys,
        ),
    )(idx, q, kv, kv)


def cross_bwd_body(idx, q_ref, k_ref, v_ref, do_ref, stat_ref, *rest, chunk):
    dq_ref, dkv_ref = rest[-2:]
    first = pl.program_id(1) * STEP
    width = dkv_ref.shape[2] // 2
    rows = q_ref.shape[1]
    for j in range(STEP):
        at = slice(j * PAIR, (j + 1) * PAIR)
        q, k, v, do = q_ref[0, :, at], k_ref[0, :, at], v_ref[0, :, at], do_ref[0, :, at]
        kt = k.T
        dk, dv = 0.0, 0.0
        for c in range(0, rows, chunk):
            outs = []
            for h in range(2):
                qh = halves_of(q[c : c + chunk], h)
                doh = halves_of(do[c : c + chunk], h)
                p = jnp.exp2(dot(k, qh, NT) - stat_ref[0, j, h : h + 1, c : c + chunk])
                dp = dot(v, doh, NT)
                ds = (p * (dp - stat_ref[0, j, 2 + h : 3 + h, c : c + chunk])).astype(BF)
                dv = dv + dot(p.astype(BF), doh)
                dk = dk + dot(ds, qh)
                outs.append(dot(kt[h * DH : (h + 1) * DH], ds))
            dq_ref[0, c : c + chunk, at] = (jnp.concatenate(outs, axis=0).T * 0.125).astype(BF)
        start = pl.multiple_of((first + j) * PAIR, PAIR)
        dkv_ref[0, :, pl.ds(start, PAIR)] = (dk * LN2).astype(BF)
        start = pl.multiple_of(width + (first + j) * PAIR, PAIR)
        dkv_ref[0, :, pl.ds(start, PAIR)] = dv.astype(BF)


def cross_bwd(idx, q, kv, do, stats, earlier=None):
    nq, rows, width = q.shape
    keys, steps, wide = kv.shape[1], width // PAIR // STEP, STEP * PAIR
    in_specs = [
        pl.BlockSpec((1, rows, wide), lambda n, p, i: (n, 0, p)),
        pl.BlockSpec((1, keys, wide), lambda n, p, i: (i[n], 0, p)),
        pl.BlockSpec((1, keys, wide), lambda n, p, i: (i[n], 0, steps + p)),
        pl.BlockSpec((1, rows, wide), lambda n, p, i: (n, 0, p)),
        pl.BlockSpec((1, STEP, 4, rows), lambda n, p, i: (n, p, 0, 0)),
    ]
    operands = [idx, q, kv, kv, do, stats]
    aliases = {}
    if earlier is not None:
        in_specs.append(pl.BlockSpec(memory_space=pl.ANY))
        operands.append(earlier)
        aliases = {6: 1}
    grid = pltpu.PrefetchScalarGridSpec(
        num_scalar_prefetch=1,
        grid=(nq, steps),
        in_specs=in_specs,
        out_specs=[
            pl.BlockSpec((1, rows, wide), lambda n, p, i: (n, 0, p)),
            pl.BlockSpec((1, keys, 2 * width), lambda n, p, i: (i[n], 0, 0)),
        ],
    )
    return pl.pallas_call(
        functools.partial(cross_bwd_body, chunk=min(rows, 256)),
        grid_spec=grid,
        input_output_aliases=aliases,
        out_shape=[jax.ShapeDtypeStruct(q.shape, BF), jax.ShapeDtypeStruct(kv.shape, BF)],
        compiler_params=params(),
        cost_estimate=pl.CostEstimate(
            flops=40 * nq * rows * keys * width,
            bytes_accessed=nq * (6 * rows + 8 * keys) * width,
            transcendentals=nq * H * rows * keys,
        ),
    )(*operands)


def self_mask(rows, length):
    key = lax.broadcasted_iota(jnp.int32, (rows, rows), 0)
    row = lax.broadcasted_iota(jnp.int32, (rows, rows), 1)
    return (key <= row) & (key < length)


def self_fwd_body(length_ref, q_ref, k_ref, v_ref, o_ref, lse_ref):
    rows = q_ref.shape[1]
    allowed = self_mask(rows, length_ref[pl.program_id(0)])
    ones = jnp.ones((16, rows), BF)
    for j in range(STEP):
        at = slice(j * PAIR, (j + 1) * PAIR)
        q, k, vt = q_ref[0, :, at], k_ref[0, :, at], v_ref[0, :, at].T
        outs = []
        for h in range(2):
            s = jnp.where(allowed, dot(k, halves_of(q, h), NT), -1e30)
            top = jnp.max(s, axis=0, keepdims=True)
            p = jnp.exp2(s - top).astype(BF)
            ot = dot(jnp.concatenate([vt[h * DH : (h + 1) * DH], ones], axis=0), p)
            total = ot[DH : DH + 1]
            outs.append(ot[:DH] * (1.0 / total))
            lse_ref[0, j, h : h + 1, :] = top + jnp.log2(total)
        o_ref[0, :, at] = jnp.concatenate(outs, axis=0).T.astype(BF)


def self_fwd(lengths, qkv):
    nq, rows, width = qkv.shape[0], qkv.shape[1], qkv.shape[2] // 3
    pairs = width // PAIR
    steps, wide = pairs // STEP, STEP * PAIR
    grid = pltpu.PrefetchScalarGridSpec(
        num_scalar_prefetch=1,
        grid=(nq, steps),
        in_specs=[
            pl.BlockSpec((1, rows, wide), lambda n, p, i: (n, 0, p)),
            pl.BlockSpec((1, rows, wide), lambda n, p, i: (n, 0, steps + p)),
            pl.BlockSpec((1, rows, wide), lambda n, p, i: (n, 0, 2 * steps + p)),
        ],
        out_specs=[
            pl.BlockSpec((1, rows, wide), lambda n, p, i: (n, 0, p)),
            pl.BlockSpec((1, STEP, 2, rows), lambda n, p, i: (n, p, 0, 0)),
        ],
    )
    return pl.pallas_call(
        self_fwd_body,
        grid_spec=grid,
        out_shape=[
            jax.ShapeDtypeStruct((nq, rows, width), BF),
            jax.ShapeDtypeStruct((nq, pairs, 2, rows), F32),
        ],
        compiler_params=params(),
        cost_estimate=pl.CostEstimate(
            flops=16 * nq * rows * rows * width,
            bytes_accessed=8 * nq * rows * width,
            transcendentals=nq * H * rows * rows,
        ),
    )(lengths, qkv, qkv, qkv)


def self_bwd_body(length_ref, q_ref, k_ref, v_ref, do_ref, lse_ref, out_ref, dk_acc, dv_acc, *, chunk):
    length = length_ref[pl.program_id(0)]
    first = pl.program_id(1) * STEP
    width = out_ref.shape[2] // 3
    rows = q_ref.shape[1]
    for j in range(STEP):
        at = slice(j * PAIR, (j + 1) * PAIR)
        q, k, v, do = q_ref[0, :, at], k_ref[0, :, at], v_ref[0, :, at], do_ref[0, :, at]
        kt = k.T
        start = pl.multiple_of((first + j) * PAIR, PAIR)
        for c in reversed(range(0, rows, chunk)):
            keys = c + chunk
            key = lax.broadcasted_iota(jnp.int32, (keys, chunk), 0)
            row = lax.broadcasted_iota(jnp.int32, (keys, chunk), 1) + c
            allowed = (key <= row) & (key < length)
            outs = []
            dk, dv = 0.0, 0.0
            for h in range(2):
                qh = halves_of(q[c : c + chunk], h)
                doh = halves_of(do[c : c + chunk], h)
                s = jnp.where(allowed, dot(k[:keys], qh, NT), -1e30)
                p = jnp.exp2(s - lse_ref[0, j, h : h + 1, c : c + chunk])
                dp = dot(v[:keys], doh, NT)
                delta = jnp.sum(p * dp, axis=0, keepdims=True)
                ds = (p * (dp - delta)).astype(BF)
                dv = dv + dot(p.astype(BF), doh)
                dk = dk + dot(ds, qh)
                outs.append(dot(kt[h * DH : (h + 1) * DH, :keys], ds))
            if keys == rows:
                dk_acc[...], dv_acc[...] = dk, dv
            else:
                dk_acc[:keys] += dk
                dv_acc[:keys] += dv
            out_ref[0, c : c + chunk, pl.ds(start, PAIR)] = (
                jnp.concatenate(outs, axis=0).T * 0.125
            ).astype(BF)
        start = pl.multiple_of(width + (first + j) * PAIR, PAIR)
        out_ref[0, :, pl.ds(start, PAIR)] = (dk_acc[...] * LN2).astype(BF)
        start = pl.multiple_of(2 * width + (first + j) * PAIR, PAIR)
        out_ref[0, :, pl.ds(start, PAIR)] = dv_acc[...].astype(BF)


def self_bwd(lengths, qkv, do, lse):
    nq, rows, width = do.shape
    steps, wide = width // PAIR // STEP, STEP * PAIR
    grid = pltpu.PrefetchScalarGridSpec(
        num_scalar_prefetch=1,
        grid=(nq, steps),
        in_specs=[
            pl.BlockSpec((1, rows, wide), lambda n, p, i: (n, 0, p)),
            pl.BlockSpec((1, rows, wide), lambda n, p, i: (n, 0, steps + p)),
            pl.BlockSpec((1, rows, wide), lambda n, p, i: (n, 0, 2 * steps + p)),
            pl.BlockSpec((1, rows, wide), lambda n, p, i: (n, 0, p)),
            pl.BlockSpec((1, STEP, 2, rows), lambda n, p, i: (n, p, 0, 0)),
        ],
        out_specs=[pl.BlockSpec((1, rows, 3 * width), lambda n, p, i: (n, 0, 0))],
        scratch_shapes=[pltpu.VMEM((rows, PAIR), F32), pltpu.VMEM((rows, PAIR), F32)],
    )
    return pl.pallas_call(
        functools.partial(self_bwd_body, chunk=min(rows, 256)),
        grid_spec=grid,
        out_shape=[jax.ShapeDtypeStruct((nq, rows, 3 * width), BF)],
        compiler_params=params(),
        cost_estimate=pl.CostEstimate(
            flops=40 * nq * rows * rows * width,
            bytes_accessed=16 * nq * rows * width,
            transcendentals=nq * H * rows * rows,
        ),
    )(lengths, qkv, qkv, qkv, do, lse)[0]


def selector(rows, levels):
    row = lax.broadcasted_iota(jnp.int32, (rows, PAIR), 0)
    lane = lax.broadcasted_iota(jnp.int32, (rows, PAIR), 1)
    return (((lane >= DH) == (row % 2 == 1)) & (row < 2 * levels)).astype(BF)


def merge_body(*refs, parts, full):
    values, lses, outs = refs[:parts], refs[parts : 2 * parts], refs[2 * parts :]
    rows = values[0].shape[1]
    row = lax.broadcasted_iota(jnp.int32, (16, rows), 0)
    pick = selector(16, 2)
    for j in range(values[0].shape[2] // PAIR):
        at = slice(j * PAIR, (j + 1) * PAIR)
        top = functools.reduce(jnp.maximum, [lse[0, j] for lse in lses])
        weights = [jnp.exp2(lse[0, j] - top) for lse in lses]
        total = functools.reduce(jnp.add, weights)
        inv = 1.0 / total
        out = 0.0
        for value, weight in zip(values, weights):
            w = weight * inv
            both = jnp.where(row % 2 == 1, w[1:2], w[0:1])
            high = both.astype(BF).astype(F32)
            split = jnp.where(row < 2, high, both - high).astype(BF)
            out = out + value[0, :, at].astype(F32) * dot(split, pick, TN)
        outs[0][0, :, at] = out.astype(BF)
        outs[1][0, j] = top + jnp.log2(total)
        if full:
            outs[2][0, :, at] = out


def merge(parts, full=False):
    nq, rows, width = parts[0][0].shape
    pairs = width // PAIR
    wide = pl.BlockSpec((1, rows, width), lambda n: (n, 0, 0))
    stat = pl.BlockSpec((1, pairs, 2, rows), lambda n: (n, 0, 0, 0))
    return pl.pallas_call(
        functools.partial(merge_body, parts=len(parts), full=full),
        grid=(nq,),
        in_specs=[wide] * len(parts) + [stat] * len(parts),
        out_specs=[wide, stat] + [wide] * full,
        out_shape=[
            jax.ShapeDtypeStruct((nq, rows, width), BF),
            jax.ShapeDtypeStruct((nq, pairs, 2, rows), F32),
        ]
        + [jax.ShapeDtypeStruct((nq, rows, width), F32)] * full,
        compiler_params=params(),
        cost_estimate=pl.CostEstimate(
            flops=4 * nq * rows * width,
            bytes_accessed=nq * rows * width * (2 * len(parts) + 2 + 4 * full),
            transcendentals=nq * H * rows,
        ),
    )(*[p[0] for p in parts], *[p[1] for p in parts])


def stats_body(do_ref, sum_ref, lse_ref, out_ref):
    pick = selector(16, 1)
    for j in range(do_ref.shape[2] // PAIR):
        at = slice(j * PAIR, (j + 1) * PAIR)
        product = do_ref[0, :, at].astype(F32) * sum_ref[0, :, at]
        high = product.astype(BF)
        low = (product - high.astype(F32)).astype(BF)
        out_ref[0, j, 0:2] = lse_ref[0, j]
        out_ref[0, j, 2:4] = (dot(pick, high, NT) + dot(pick, low, NT))[0:2]


def row_stats(do, cross_sum, lse):
    nq, rows, width = do.shape
    pairs = width // PAIR
    wide = pl.BlockSpec((1, rows, width), lambda n: (n, 0, 0))
    return pl.pallas_call(
        stats_body,
        grid=(nq,),
        in_specs=[wide, wide, pl.BlockSpec((1, pairs, 2, rows), lambda n: (n, 0, 0, 0))],
        out_specs=pl.BlockSpec((1, pairs, 4, rows), lambda n: (n, 0, 0, 0)),
        out_shape=jax.ShapeDtypeStruct((nq, pairs, 4, rows), F32),
        compiler_params=params(),
        cost_estimate=pl.CostEstimate(
            flops=4 * nq * rows * width, bytes_accessed=6 * nq * rows * width, transcendentals=0
        ),
    )(do, cross_sum, lse)


def keyval_body(enc_ref, w_ref, out_ref):
    out_ref[...] = dot(enc_ref[...], w_ref[...]).astype(BF)


def keyval(enc, w):
    n, depth = enc.shape
    width = w.shape[1]
    block = 1024
    return pl.pallas_call(
        keyval_body,
        grid=(n // block,),
        in_specs=[
            pl.BlockSpec((block, depth), lambda i: (i, 0)),
            pl.BlockSpec((depth, width), lambda i: (0, 0)),
        ],
        out_specs=pl.BlockSpec((block, width), lambda i: (i, 0)),
        out_shape=jax.ShapeDtypeStruct((n, width), BF),
        compiler_params=params(),
        cost_estimate=pl.CostEstimate(
            flops=2 * n * depth * width, bytes_accessed=2 * n * (depth + width), transcendentals=0
        ),
    )(enc, w)


def feed_forward_body(
    middle_ref,
    att_ref,
    cot_ref,
    gain_ref,
    w_out_ref,
    w_in_ref,
    w_down_ref,
    out_ref,
    grad_ref,
    catt_ref,
    gain_grad_ref,
    w_grad_ref,
    latter,
    normed,
    hidden,
    slopes,
    total,
    back,
):
    step = pl.program_id(0)
    last = pl.num_programs(0) - 1
    gain = gain_ref[...]

    @pl.when(step == 0)
    def _():
        v = middle_ref[...] + dot(att_ref[...], w_out_ref[...])
        latter[...] = v
        normed[...] = (v * rms_parts(v) * gain).astype(BF)

    @pl.when((step < last) & (step % 2 == 0))
    def _():
        act, slope = gelu_and_slope(dot(normed[...], w_in_ref[...]))
        hidden[...] = act.astype(BF)
        slopes[...] = (dot(cot_ref[...], w_down_ref[...], NT) * slope).astype(BF)
        more = dot(slopes[...], w_in_ref[...], NT)
        back[...] = jnp.where(step == 0, more, back[...] + more)
        w_grad_ref[...] = dot(normed[...], slopes[...], TN).astype(BF)

    @pl.when((step < last) & (step % 2 == 1))
    def _():
        more = dot(hidden[...], w_down_ref[...])
        total[...] = jnp.where(step == 1, more, total[...] + more)
        w_grad_ref[...] = dot(hidden[...], cot_ref[...], TN).astype(BF)

    @pl.when(step == last)
    def _():
        v, b = latter[...], back[...]
        out_ref[...] = (v + total[...]).astype(BF)
        r = rms_parts(v)
        gb = gain * b
        grad = r * gb - v * (r * r * r * jnp.mean(v * gb, axis=-1, keepdims=True))
        grad = cot_ref[...].astype(F32) + grad
        gain_grad_ref[...] = jnp.sum(v * r * b, axis=0, keepdims=True)
        grad_ref[...] = grad
        hidden[...] = grad.astype(BF)
        catt_ref[...] = dot(hidden[...], w_out_ref[...], NT).astype(BF)
        w_grad_ref[...] = dot(att_ref[...], hidden[...], TN).astype(BF)


def feed_forward(middle, att, cot, gain, weights):
    tokens, width = middle.shape
    chunks = (weights.shape[1] // width - 1) // 2
    steps = 2 * chunks + 1

    def whole(rows, columns):
        return pl.BlockSpec((rows, columns), lambda s: (0, 0))

    def chunk_of(s):
        return jnp.minimum(s // 2, chunks - 1)

    square = (width, width)
    wide = [pltpu.VMEM((tokens, width), t) for t in (F32, BF, BF, BF, F32, F32)]
    return pl.pallas_call(
        feed_forward_body,
        grid=(steps,),
        in_specs=[whole(tokens, width)] * 3
        + [
            whole(1, width),
            whole(*square),
            pl.BlockSpec(square, lambda s: (0, 1 + chunk_of(s))),
            pl.BlockSpec(square, lambda s: (0, 1 + chunks + chunk_of(s))),
        ],
        out_specs=[whole(tokens, width)] * 3
        + [
            whole(1, width),
            pl.BlockSpec(
                square, lambda s: (0, jnp.where(s == steps - 1, 0, 1 + s // 2 + chunks * (s % 2)))
            ),
        ],
        out_shape=[
            jax.ShapeDtypeStruct((tokens, width), BF),
            jax.ShapeDtypeStruct((tokens, width), F32),
            jax.ShapeDtypeStruct((tokens, width), BF),
            jax.ShapeDtypeStruct((1, width), F32),
            jax.ShapeDtypeStruct(weights.shape, BF),
        ],
        scratch_shapes=wide,
        compiler_params=params(),
        cost_estimate=pl.CostEstimate(
            flops=2 * tokens * width * width * (6 * chunks + 3),
            bytes_accessed=tokens * width * 14 + 4 * width * weights.shape[1],
            transcendentals=tokens * width * chunks,
        ),
    )(middle, att, cot, gain, weights, weights, weights)


def bits_below(n):
    return [1 << b for b in range(n.bit_length() - 1)]


def exchanges():
    dp, psg = lax.axis_size("dp"), lax.axis_size("psg")
    flat = bits_below(dp)
    cut = max(1, len(flat) // 3)
    xs = [("dp", b) for b in flat[:cut]]
    zs = [("dp", b) for b in flat[cut:]]
    ys = [("psg", b) for b in bits_below(psg)[1:]]
    order = [("dp", b) for b in reversed(flat)] + [("psg", b) for b in reversed(bits_below(psg))]
    return ("psg", 1), xs, ys, zs, order


def swap_bit(x, hop):
    axis, bit = hop
    n = lax.axis_size(axis)
    return lax.ppermute(x, axis, [(p, p ^ bit) for p in range(n)])


def my_bit(hop):
    return (lax.axis_index(hop[0]) // hop[1]) % 2


def after(x, *others):
    return lax.optimization_barrier((x, others))[0]


def partner(hop):
    axis, bit = hop
    me = lax.axis_index(axis)
    return {axis: me + bit * (1 - 2 * ((me // bit) % 2))}


def gather_body(*refs, columns, core, orders, order):
    n, n_out = len(columns), 1 + max(c[0] for c in columns)
    ins, outs = refs[:n], refs[n : n + n_out]
    local, send, recv = refs[n + n_out :]
    place = tuple(my_bit(h) for h in order)

    def block(k, have, flip=None):
        out, start, width = columns[k]
        at = tuple(
            slice(None) if h in have else 1 - p if h == flip else p for h, p in zip(order, place)
        )
        return outs[out].at[at + (slice(None), pl.ds(start, width))]

    def copy(k, ref, hop, sem):
        moved = pltpu.make_async_remote_copy(
            src_ref=ref,
            dst_ref=ref,
            send_sem=send.at[k, sem],
            recv_sem=recv.at[k, sem],
            device_id=partner(hop),
            device_id_type=pl.DeviceIdType.MESH,
        )
        moved.start()
        return moved

    own = [pltpu.make_async_copy(ins[k], block(k, ()), local.at[k]) for k in range(n)]
    for c in own:
        c.start()
    barrier = pltpu.get_barrier_semaphore()
    for hop in order:
        pl.semaphore_signal(
            barrier, inc=1, device_id=partner(hop), device_id_type=pl.DeviceIdType.MESH
        )
    pl.semaphore_wait(barrier, len(order))
    for c in own:
        c.wait()
    steps = len(order) - 1
    far = [[] for _ in range(n)]
    near = [[] for _ in range(n)]
    for k in range(n):
        far[k].append(copy(k, block(k, ()), orders[k][0], 0))
        near[k].append(copy(k, block(k, ()), core, steps))
    for t in range(steps):
        for k in range(n):
            have = orders[k][:t]
            far[k][t].wait_recv()
            if t + 1 < steps:
                far[k].append(copy(k, block(k, orders[k][: t + 1]), orders[k][t + 1], t + 1))
            near[k].append(copy(k, block(k, have, orders[k][t]), core, steps + 1 + t))
    for k in range(n):
        for c in far[k]:
            c.wait_send()
        for c in near[k]:
            c.wait()


def gather_rows(stripes, columns, widths):
    core, xs, ys, zs, order = exchanges()
    orders = [zs + xs + ys, zs + ys + xs, xs + zs + ys, ys + zs + xs, xs + ys + zs]
    orders = [orders[k % len(orders)] for k in range(len(stripes))]
    rows, n = stripes[0].shape[0], len(stripes)
    outs = pl.pallas_call(
        functools.partial(gather_body, columns=columns, core=core, orders=orders, order=order),
        in_specs=[pl.BlockSpec(memory_space=pl.ANY)] * n,
        out_specs=[pl.BlockSpec(memory_space=pl.ANY)] * len(widths),
        out_shape=[
            jax.ShapeDtypeStruct((2,) * len(order) + (rows, w), stripes[0].dtype) for w in widths
        ],
        scratch_shapes=[
            pltpu.SemaphoreType.DMA((n,)),
            pltpu.SemaphoreType.DMA((n, 2 * len(order))),
            pltpu.SemaphoreType.DMA((n, 2 * len(order))),
        ],
        compiler_params=pltpu.CompilerParams(collective_id=0, has_side_effects=True),
    )(*stripes)
    return [o.reshape(rows << len(order), o.shape[-1]) for o in outs]


def sum_rows(stripes, work):
    core, xs, ys, zs, order = exchanges()
    hops = [[core] + h for h in (xs + ys + zs, ys + zs + xs, zs + xs + ys)]
    states = [[a.reshape((2,) * len(order) + (-1, a.shape[1])) for a in s] for s in stripes]
    names = [order] * len(stripes)
    made = []
    for step in range(len(order)):
        keep, send = [], []
        for arrays, held, hop in zip(states, names, [h[step] for h in hops]):
            at, bit = held.index(hop), my_bit(hop)
            for side, b in ((keep, bit), (send, 1 - bit)):
                side.append(
                    jnp.concatenate(
                        [lax.dynamic_index_in_dim(a, b, at, keepdims=False) for a in arrays], axis=-1
                    )
                )
        send = lax.optimization_barrier(send)
        got = [swap_bit(x, h[step]) for x, h in zip(send, hops)]
        if step < len(work):
            made.append(work[step](send))
            got = after(got, made[-1])
        got = lax.optimization_barrier(got)
        states = [[(k.astype(F32) + g.astype(F32)).astype(BF)] for k, g in zip(keep, got)]
        names = [[n for n in held if n != h[step]] for held, h in zip(names, hops)]
    return [arrays[0] for arrays in states], made


def rms_parts(v):
    return lax.rsqrt(jnp.mean(v * v, axis=-1, keepdims=True) + 1e-06)


def rms_back(v, gain, b):
    r = rms_parts(v)
    gb = gain * b
    grad = r * gb - v * (r * r * r * jnp.mean(v * gb, axis=-1, keepdims=True))
    return grad, jnp.sum(v * r * b, axis=tuple(range(v.ndim - 1)))


def gelu_and_slope(u):
    t = jnp.tanh(0.7978845608028654 * (u + 0.044715 * u * u * u))
    slope = 0.5 * (1.0 + t) + 0.5 * u * (1.0 - t * t) * (
        0.7978845608028654 * (1.0 + 3.0 * 0.044715 * u * u)
    )
    return 0.5 * u * (1.0 + t), slope


def on_device(
    decoder_input,
    encoder_out,
    cotangent,
    task_ids,
    passage_ids,
    target_lengths,
    query_embed,
    passage_bank,
    self_in,
    self_out,
    cross_query,
    cross_keyval,
    cross_out,
    hidden_in,
    hidden_output_weight,
    norm_gains,
    task_table,
):
    count, rows, width = decoder_input.shape
    group, npass, tokens, _ = encoder_out.shape
    keys = npass * tokens
    psg = lax.axis_size("psg")
    chips = psg // 2
    me = lax.axis_index("psg")
    chip, core = me // 2, me % 2
    shard = self_in.shape[0]
    ff = hidden_in.shape[1]
    n_tasks = task_table.shape[0]

    swap = [(p, p ^ 1) for p in range(psg)]

    def core_swap(x):
        return jax.tree.map(lambda a: lax.ppermute(a, "psg", swap), x)

    def chip_shift(x, step):
        perm = [(p, (p + 2 * step) % psg) for p in range(psg)]
        return jax.tree.map(lambda a: lax.ppermute(a, "psg", perm), x)

    def ids_of(chip_at, core_at):
        return (chip_at * 2 + core_at) * count + jnp.arange(count, dtype=jnp.int32)

    small = jnp.concatenate([norm_gains, task_table], axis=0).T
    small = jnp.pad(small, ((0, 0), (0, 128 - small.shape[1])))
    enc = encoder_out.reshape(group * keys, width)
    w_self_in, w_out, w_rest = gather_rows(
        [self_in[:, k * width : (k + 1) * width] for k in range(3)]
        + [self_out, jnp.concatenate([cross_query, small], axis=1)],
        [(0, 0, width), (0, width, width), (0, 2 * width, width), (1, 0, width), (2, 0, width + 128)],
        [3 * width, width, width + 128],
    )
    w_self_out, w_cross_query, w_small = w_out, w_rest[:, :width], w_rest[:, width:]
    w_keyval = lax.all_gather(cross_keyval, ALL, axis=0, tiled=True)

    embeds = jnp.take(passage_bank, passage_ids, axis=0).astype(F32)
    score = jnp.sum(query_embed[:, None, :] * embeds, axis=-1)
    others = [
        lax.ppermute(score, "psg", [(p, (p + k) % psg) for p in range(psg)]) for k in range(1, psg)
    ]
    every = jnp.concatenate([score] + others, axis=1)
    top = jnp.max(every, axis=1, keepdims=True)
    retrieval = jnp.exp(score - top) / jnp.sum(jnp.exp(every - top), axis=1, keepdims=True)

    smalls = w_small.T.astype(F32)
    gains, table = smalls[:3], smalls[3 : 3 + n_tasks]
    choose = task_ids[:, None] == jnp.arange(n_tasks, dtype=jnp.int32)[None, :]
    task_rows = jnp.sum(jnp.where(choose[:, :, None], table[None], 0.0), axis=1)

    stream = decoder_input.astype(F32) + task_rows[:, None, :]
    normed_one = (stream * rms_parts(stream) * gains[0]).astype(BF)
    col = lax.broadcasted_iota(jnp.int32, (1, 3 * width), 1)
    scale = jnp.where(col < width, QSCALE, 1.0)
    flat = (count * rows, width)
    qkv = (mm(normed_one.reshape(flat), w_self_in) * scale).astype(BF)
    qkv = qkv.reshape(count, rows, 3 * width)
    self_att, self_lse = self_fwd(target_lengths, qkv)
    middle = stream + mm(self_att.reshape(flat), w_self_out).reshape(stream.shape)
    normed_two = (middle * rms_parts(middle) * gains[1]).astype(BF)
    own_q = (mm(normed_two.reshape(flat), w_cross_query) * QSCALE).astype(BF)
    own_q = own_q.reshape(count, rows, width)

    n_dev = width // shard
    fold = hidden_output_weight.shape[0] // shard
    in_turn = after(hidden_in, own_q).reshape(shard, n_dev, fold, shard)
    in_turn = in_turn.swapaxes(1, 2).reshape(shard, ff)
    folded = [hidden_output_weight[shard * k : shard * (k + 1)] for k in range(fold)]
    second = lax.all_gather(
        jnp.concatenate([cross_out, in_turn] + folded, axis=1),
        ALL,
        axis=0,
        tiled=True,
    )

    near_ids = (ids_of(chip, core), ids_of(chip, 1 - core))
    far_ids, far_same_q = [], []
    for step in range(1, chips):
        far_same_q.append([chip_shift(own_q[n : n + 1], step) for n in range(count)])
        source = (chip - step) % chips
        far_ids.append((ids_of(source, core), ids_of(source, 1 - core)))
    peer_q = core_swap(own_q)
    kv = keyval(after(enc, own_q), w_keyval).reshape(group, keys, 2 * width)
    peer_part = cross_fwd(near_ids[1], peer_q, kv, npass)
    latest, crossed = peer_part, None
    far_q, far_local, far_back = [], [], []
    for step in range(1, chips):
        queries, local, back = [], [], []
        for n in range(count):
            same_q = after(far_same_q[step - 1][n], peer_part if crossed is None else crossed)
            crossed_q = core_swap(same_q)
            same = cross_fwd(far_ids[step - 1][0][n : n + 1], same_q, kv, npass)
            crossed_q = after(crossed_q, same, latest)
            crossed = cross_fwd(far_ids[step - 1][1][n : n + 1], crossed_q, kv, npass)
            value, joint = merge([same[:2], core_swap(crossed[:2])])
            latest = value
            back.append(chip_shift((value, joint), chips - step))
            local.append((same[1:], crossed[1:]))
            queries.append((same_q, crossed_q))
        far_q.append(queries)
        far_local.append(local)
        far_back.append(back)
    own_part = cross_fwd(near_ids[0], after(own_q, latest), kv, npass)
    parts = [own_part[:2], core_swap(peer_part[:2])]
    for back in far_back:
        parts.append(tuple(jnp.concatenate([b[k] for b in back], axis=0) for k in range(2)))
    cross_att, cross_lse, cross_sum = merge(parts, full=True)

    output, grad_latter, grad_catt, gain_three, grad_second = feed_forward(
        middle.reshape(flat), cross_att.reshape(flat), cotangent.reshape(flat), gains[2:3], second
    )
    output, grad_latter = output.reshape(stream.shape), grad_latter.reshape(stream.shape)
    grad_catt, gain_three = grad_catt.reshape(stream.shape), gain_three[0]
    sum_second = lax.psum_scatter(grad_second, ALL, scatter_dimension=0, tiled=True)

    own_sent = (grad_catt, row_stats(grad_catt, cross_sum, cross_lse))
    far_same = [chip_shift(own_sent, step) for step in range(1, chips)]
    peer_sent = core_swap(own_sent)
    dq_own, dkv = cross_bwd(near_ids[0], own_q, kv, *after(own_sent, grad_second))
    far_same = [after(same, dq_own) for same in far_same]
    far_sent = [(same, core_swap(same)) for same in far_same]
    dq_peer, dkv = cross_bwd(near_ids[1], peer_q, kv, *after(peer_sent, dq_own), dkv)
    dq_back = core_swap(dq_peer)
    latest = dq_peer
    dq_parts = []
    for step in range(1, chips):
        same, crossed = far_sent[step - 1]
        back = []
        for n in range(count):
            same_q, crossed_q = far_q[step - 1][n]
            one = slice(n, n + 1)
            sent = [x[one] for x in after(crossed, latest)]
            dq_crossed, dkv = cross_bwd(far_ids[step - 1][1][one], crossed_q, kv, *sent, dkv)
            sent = [x[one] for x in same]
            dq_same, dkv = cross_bwd(far_ids[step - 1][0][one], same_q, kv, *sent, dkv)
            joint = (dq_same.astype(F32) + core_swap(dq_crossed).astype(F32)).astype(BF)
            latest = joint
            back.append(chip_shift(joint, chips - step))
        dq_parts.append(jnp.concatenate(back, axis=0))
    dkv_flat = after(dkv, joint).reshape(group * keys, 2 * width)
    grad_cross_keyval = mm(enc, dkv_flat, TN).astype(BF)
    total = dq_own.astype(F32) + dq_back.astype(F32)
    for dq in after(dq_parts, grad_cross_keyval, sum_second):
        total = total + dq.astype(F32)
    grad_cross_q = total.astype(BF).reshape(flat)
    grad_cross_query = mm(normed_two.reshape(flat), grad_cross_q, TN).astype(BF)

    grad_normed_two = mm(grad_cross_q, w_cross_query, NT).reshape(stream.shape)
    grad_middle, gain_two = rms_back(middle, gains[1], grad_normed_two)
    grad_middle = grad_middle + grad_latter
    grad_self_part = grad_middle.astype(BF).reshape(flat)
    grad_self_out = mm(self_att.reshape(flat), grad_self_part, TN).astype(BF)
    grad_satt = mm(grad_self_part, w_self_out, NT).astype(BF).reshape(count, rows, width)
    grad_qkv = self_bwd(target_lengths, qkv, grad_satt, self_lse)
    grad_qkv = grad_qkv.reshape(count * rows, 3 * width)
    grad_normed_one = mm(grad_qkv, w_self_in, NT).reshape(stream.shape)
    grad_stream, gain_one = rms_back(stream, gains[0], grad_normed_one)
    input_grad = grad_stream + grad_middle
    per_query = jnp.sum(input_grad, axis=1)
    grad_table = jnp.sum(jnp.where(choose[:, :, None], per_query[:, None, :], 0.0), axis=0)
    tiny = jnp.concatenate([jnp.stack([gain_one, gain_two, gain_three]), grad_table], axis=0).T
    tiny = jnp.pad(tiny, ((0, 0), (0, 128 - tiny.shape[1]))).astype(BF)
    grad_self_in = mm(normed_one.reshape(flat), grad_qkv, TN).astype(BF)

    def distillation(sent):
        sets = [
            (near_ids[0], *own_part[1:], own_sent[1]),
            (near_ids[1], *peer_part[1:], peer_sent[1]),
        ]
        for step in range(1, chips):
            for side in range(2):
                lse, share = (
                    jnp.concatenate([lo[side][k] for lo in far_local[step - 1]], axis=0)
                    for k in range(2)
                )
                sets.append((far_ids[step - 1][side], lse, share, far_sent[step - 1][side][1]))
        ids = jnp.concatenate([s[0] for s in sets])
        masses = []
        for _, lse, share, stats in sets:
            weight = jnp.exp2(lse - stats[:, :, :2])
            masses.append(jnp.sum(share * weight[:, :, :, None, :], axis=(1, 2, 4)) / (H * rows))
        masses = jnp.concatenate(masses, axis=0)
        place = ids[None, :] == jnp.arange(group, dtype=jnp.int32)[:, None]
        mass = jnp.sum(jnp.where(place[:, :, None], masses[None], 0.0), axis=1)
        query_grad = jnp.sum((after(retrieval, sent) - mass)[:, :, None] * embeds, axis=1)
        hop = 1
        while hop < psg:
            perm = [(p, p ^ hop) for p in range(psg)]
            query_grad = query_grad + lax.ppermute(query_grad, "psg", perm)
            hop *= 2
        return query_grad

    def encoder_part(sent):
        return mm(after(dkv_flat, sent), w_keyval, NT).reshape(encoder_out.shape)

    half = width // 2
    summed, (query_grad, encoder_grad) = sum_rows(
        [
            [grad_self_in[:, :width], grad_cross_query, tiny],
            [grad_self_in[:, width : 2 * width], grad_cross_keyval[:, :width], grad_self_out[:, :half]],
            [grad_self_in[:, 2 * width :], grad_cross_keyval[:, width:], grad_self_out[:, half:]],
        ],
        [distillation, encoder_part],
    )
    summed = [x.astype(F32) for x in summed]
    small_sum = summed[0][:, 2 * width :].T
    sum_in = sum_second[:, width : width + ff].reshape(shard, fold, n_dev, shard)
    sum_in = sum_in.swapaxes(1, 2).reshape(shard, ff)
    return (
        output,
        input_grad,
        encoder_grad,
        jnp.concatenate([x[:, :width] for x in summed], axis=1),
        jnp.concatenate([x[:, 2 * width :] for x in summed[1:]], axis=1),
        summed[0][:, width : 2 * width],
        jnp.concatenate([x[:, width : 2 * width] for x in summed[1:]], axis=1),
        sum_second[:, :width].astype(F32),
        sum_in.astype(F32),
        jnp.concatenate(
            [sum_second[:, width * k : width * (k + 1)] for k in range(1 + fold, 1 + 2 * fold)]
        ).astype(F32),
        small_sum[:3],
        small_sum[3 : 3 + n_tasks],
        query_grad,
    )


def solution(mesh):
    rows = P(ALL, None)
    tokens = P(ALL, None, None)
    passages = P("dp", "psg", None, None)
    columns = P(None, ALL)
    return jax.shard_map(
        on_device,
        mesh=mesh,
        in_specs=(tokens, passages, tokens, P(ALL), P("dp", "psg"), P(ALL), P("dp", None), P())
        + (rows,) * 7
        + (columns, columns),
        out_specs=(tokens, tokens, passages) + (rows,) * 7 + (columns, columns, P("dp", None)),
        check_vma=False,
    )
```

```python
import functools

import jax
import jax.numpy as jnp
from jax import lax
from jax.experimental import pallas as pl
from jax.experimental.pallas import tpu as pltpu
from jax.sharding import PartitionSpec as P

H = 12
DH = 64
PAIR = 2 * DH
BF = jnp.bfloat16
F32 = jnp.float32
LN2 = 0.6931471805599453
QSCALE = 0.125 / LN2
ALL = ("dp", "psg")
NN = (((1,), (0,)), ((), ()))
NT = (((1,), (1,)), ((), ()))
TN = (((0,), (0,)), ((), ()))
VMEM_BYTES = 56 * 2**20


def dot(a, b, dims=NN):
    return lax.dot_general(a, b, dims, preferred_element_type=F32)


def mm(a, b, dims=NN):
    return lax.dot_general(a, b, dims, preferred_element_type=F32)


STEP = 3
SAFE = 80.0


def halves_of(x, h):
    lane = lax.broadcasted_iota(jnp.int32, x.shape, 1)
    return jnp.where((lane >= DH) == (h == 1), x, jnp.zeros((), x.dtype))


def squared_norms(x):
    wide = x.astype(F32)
    return dot(selector(16, 1), (wide * wide).astype(BF), NT)


def params():
    return pltpu.CompilerParams(vmem_limit_bytes=VMEM_BYTES)


def cross_fwd_body(idx, q_ref, k_ref, v_ref, o_ref, lse_ref, share_ref, *, npass):
    keys = k_ref.shape[1]
    blocks = [slice(j * PAIR, (j + 1) * PAIR) for j in range(q_ref.shape[2] // PAIR)]
    col = lax.broadcasted_iota(jnp.int32, (16, keys), 1) // (keys // npass)
    row = lax.broadcasted_iota(jnp.int32, (16, keys), 0)
    member = (col == row).astype(BF)

    def run(shift):
        for j, at in enumerate(blocks):
            q, k, vt = q_ref[0, :, at], k_ref[0, :, at], v_ref[0, :, at].T
            outs = []
            for h in range(2):
                s = dot(k, halves_of(q, h), NT)
                top = jnp.max(s, axis=0, keepdims=True) if shift else None
                p = jnp.exp2(s - top if shift else s).astype(BF)
                ot = dot(jnp.concatenate([vt[h * DH : (h + 1) * DH], member], axis=0), p)
                parts = ot[DH : DH + npass]
                total = jnp.sum(parts, axis=0, keepdims=True)
                inv = 1.0 / total
                outs.append(ot[:DH] * inv)
                lse = jnp.log2(total)
                lse_ref[0, j, h : h + 1, :] = top + lse if shift else lse
                share_ref[0, j, h, :, :] = parts * inv
            o_ref[0, :, at] = jnp.concatenate(outs, axis=0).T.astype(o_ref.dtype)

    longest_q = functools.reduce(jnp.maximum, [squared_norms(q_ref[0, :, at]) for at in blocks])
    longest_k = functools.reduce(jnp.maximum, [squared_norms(k_ref[0, :, at]) for at in blocks])
    small = jnp.max(longest_q) * jnp.max(longest_k) < SAFE * SAFE
    pl.when(small)(lambda: run(False))
    pl.when(jnp.logical_not(small))(lambda: run(True))


def cross_fwd(idx, q, kv, npass):
    nq, rows, width = q.shape
    keys, pairs = kv.shape[1], width // PAIR
    steps, wide = pairs // STEP, STEP * PAIR
    grid = pltpu.PrefetchScalarGridSpec(
        num_scalar_prefetch=1,
        grid=(nq, steps),
        in_specs=[
            pl.BlockSpec((1, rows, wide), lambda n, p, i: (n, 0, p)),
            pl.BlockSpec((1, keys, wide), lambda n, p, i: (i[n], 0, p)),
            pl.BlockSpec((1, keys, wide), lambda n, p, i: (i[n], 0, steps + p)),
        ],
        out_specs=[
            pl.BlockSpec((1, rows, wide), lambda n, p, i: (n, 0, p)),
            pl.BlockSpec((1, STEP, 2, rows), lambda n, p, i: (n, p, 0, 0)),
            pl.BlockSpec((1, STEP, 2, npass, rows), lambda n, p, i: (n, p, 0, 0, 0)),
        ],
    )
    return pl.pallas_call(
        functools.partial(cross_fwd_body, npass=npass),
        grid_spec=grid,
        out_shape=[
            jax.ShapeDtypeStruct(q.shape, BF),
            jax.ShapeDtypeStruct((nq, pairs, 2, rows), F32),
            jax.ShapeDtypeStruct((nq, pairs, 2, npass, rows), F32),
        ],
        compiler_params=params(),
        cost_estimate=pl.CostEstimate(
            flops=16 * nq * rows * keys * width,
            bytes_accessed=4 * nq * (rows + keys) * width,
            transcendentals=nq * H * rows * keys,
        ),
    )(idx, q, kv, kv)


def cross_bwd_body(idx, q_ref, k_ref, v_ref, do_ref, stat_ref, *rest, chunk):
    dq_ref, dkv_ref = rest[-2:]
    first = pl.program_id(1) * STEP
    width = dkv_ref.shape[2] // 2
    rows = q_ref.shape[1]
    for j in range(STEP):
        at = slice(j * PAIR, (j + 1) * PAIR)
        q, k, v, do = q_ref[0, :, at], k_ref[0, :, at], v_ref[0, :, at], do_ref[0, :, at]
        kt = k.T
        dk, dv = 0.0, 0.0
        for c in range(0, rows, chunk):
            outs = []
            for h in range(2):
                qh = halves_of(q[c : c + chunk], h)
                doh = halves_of(do[c : c + chunk], h)
                p = jnp.exp2(dot(k, qh, NT) - stat_ref[0, j, h : h + 1, c : c + chunk])
                dp = dot(v, doh, NT)
                ds = (p * (dp - stat_ref[0, j, 2 + h : 3 + h, c : c + chunk])).astype(BF)
                dv = dv + dot(p.astype(BF), doh)
                dk = dk + dot(ds, qh)
                outs.append(dot(kt[h * DH : (h + 1) * DH], ds))
            dq_ref[0, c : c + chunk, at] = (jnp.concatenate(outs, axis=0).T * 0.125).astype(BF)
        start = pl.multiple_of((first + j) * PAIR, PAIR)
        dkv_ref[0, :, pl.ds(start, PAIR)] = (dk * LN2).astype(BF)
        start = pl.multiple_of(width + (first + j) * PAIR, PAIR)
        dkv_ref[0, :, pl.ds(start, PAIR)] = dv.astype(BF)


def cross_bwd(idx, q, kv, do, stats, earlier=None):
    nq, rows, width = q.shape
    keys, steps, wide = kv.shape[1], width // PAIR // STEP, STEP * PAIR
    in_specs = [
        pl.BlockSpec((1, rows, wide), lambda n, p, i: (n, 0, p)),
        pl.BlockSpec((1, keys, wide), lambda n, p, i: (i[n], 0, p)),
        pl.BlockSpec((1, keys, wide), lambda n, p, i: (i[n], 0, steps + p)),
        pl.BlockSpec((1, rows, wide), lambda n, p, i: (n, 0, p)),
        pl.BlockSpec((1, STEP, 4, rows), lambda n, p, i: (n, p, 0, 0)),
    ]
    operands = [idx, q, kv, kv, do, stats]
    aliases = {}
    if earlier is not None:
        in_specs.append(pl.BlockSpec(memory_space=pl.ANY))
        operands.append(earlier)
        aliases = {6: 1}
    grid = pltpu.PrefetchScalarGridSpec(
        num_scalar_prefetch=1,
        grid=(nq, steps),
        in_specs=in_specs,
        out_specs=[
            pl.BlockSpec((1, rows, wide), lambda n, p, i: (n, 0, p)),
            pl.BlockSpec((1, keys, 2 * width), lambda n, p, i: (i[n], 0, 0)),
        ],
    )
    return pl.pallas_call(
        functools.partial(cross_bwd_body, chunk=min(rows, 256)),
        grid_spec=grid,
        input_output_aliases=aliases,
        out_shape=[jax.ShapeDtypeStruct(q.shape, BF), jax.ShapeDtypeStruct(kv.shape, BF)],
        compiler_params=params(),
        cost_estimate=pl.CostEstimate(
            flops=40 * nq * rows * keys * width,
            bytes_accessed=nq * (6 * rows + 8 * keys) * width,
            transcendentals=nq * H * rows * keys,
        ),
    )(*operands)


def self_mask(rows, length):
    key = lax.broadcasted_iota(jnp.int32, (rows, rows), 0)
    row = lax.broadcasted_iota(jnp.int32, (rows, rows), 1)
    return (key <= row) & (key < length)


def self_fwd_body(length_ref, q_ref, k_ref, v_ref, o_ref, lse_ref):
    rows = q_ref.shape[1]
    allowed = self_mask(rows, length_ref[pl.program_id(0)])
    ones = jnp.ones((16, rows), BF)
    for j in range(STEP):
        at = slice(j * PAIR, (j + 1) * PAIR)
        q, k, vt = q_ref[0, :, at], k_ref[0, :, at], v_ref[0, :, at].T
        outs = []
        for h in range(2):
            s = jnp.where(allowed, dot(k, halves_of(q, h), NT), -1e30)
            top = jnp.max(s, axis=0, keepdims=True)
            p = jnp.exp2(s - top).astype(BF)
            ot = dot(jnp.concatenate([vt[h * DH : (h + 1) * DH], ones], axis=0), p)
            total = ot[DH : DH + 1]
            outs.append(ot[:DH] * (1.0 / total))
            lse_ref[0, j, h : h + 1, :] = top + jnp.log2(total)
        o_ref[0, :, at] = jnp.concatenate(outs, axis=0).T.astype(BF)


def self_fwd(lengths, qkv):
    nq, rows, width = qkv.shape[0], qkv.shape[1], qkv.shape[2] // 3
    pairs = width // PAIR
    steps, wide = pairs // STEP, STEP * PAIR
    grid = pltpu.PrefetchScalarGridSpec(
        num_scalar_prefetch=1,
        grid=(nq, steps),
        in_specs=[
            pl.BlockSpec((1, rows, wide), lambda n, p, i: (n, 0, p)),
            pl.BlockSpec((1, rows, wide), lambda n, p, i: (n, 0, steps + p)),
            pl.BlockSpec((1, rows, wide), lambda n, p, i: (n, 0, 2 * steps + p)),
        ],
        out_specs=[
            pl.BlockSpec((1, rows, wide), lambda n, p, i: (n, 0, p)),
            pl.BlockSpec((1, STEP, 2, rows), lambda n, p, i: (n, p, 0, 0)),
        ],
    )
    return pl.pallas_call(
        self_fwd_body,
        grid_spec=grid,
        out_shape=[
            jax.ShapeDtypeStruct((nq, rows, width), BF),
            jax.ShapeDtypeStruct((nq, pairs, 2, rows), F32),
        ],
        compiler_params=params(),
        cost_estimate=pl.CostEstimate(
            flops=16 * nq * rows * rows * width,
            bytes_accessed=8 * nq * rows * width,
            transcendentals=nq * H * rows * rows,
        ),
    )(lengths, qkv, qkv, qkv)


def self_bwd_body(length_ref, q_ref, k_ref, v_ref, do_ref, lse_ref, out_ref, dk_acc, dv_acc, *, chunk):
    length = length_ref[pl.program_id(0)]
    first = pl.program_id(1) * STEP
    width = out_ref.shape[2] // 3
    rows = q_ref.shape[1]
    for j in range(STEP):
        at = slice(j * PAIR, (j + 1) * PAIR)
        q, k, v, do = q_ref[0, :, at], k_ref[0, :, at], v_ref[0, :, at], do_ref[0, :, at]
        kt = k.T
        start = pl.multiple_of((first + j) * PAIR, PAIR)
        for c in reversed(range(0, rows, chunk)):
            keys = c + chunk
            key = lax.broadcasted_iota(jnp.int32, (keys, chunk), 0)
            row = lax.broadcasted_iota(jnp.int32, (keys, chunk), 1) + c
            allowed = (key <= row) & (key < length)
            outs = []
            dk, dv = 0.0, 0.0
            for h in range(2):
                qh = halves_of(q[c : c + chunk], h)
                doh = halves_of(do[c : c + chunk], h)
                s = jnp.where(allowed, dot(k[:keys], qh, NT), -1e30)
                p = jnp.exp2(s - lse_ref[0, j, h : h + 1, c : c + chunk])
                dp = dot(v[:keys], doh, NT)
                delta = jnp.sum(p * dp, axis=0, keepdims=True)
                ds = (p * (dp - delta)).astype(BF)
                dv = dv + dot(p.astype(BF), doh)
                dk = dk + dot(ds, qh)
                outs.append(dot(kt[h * DH : (h + 1) * DH, :keys], ds))
            if keys == rows:
                dk_acc[...], dv_acc[...] = dk, dv
            else:
                dk_acc[:keys] += dk
                dv_acc[:keys] += dv
            out_ref[0, c : c + chunk, pl.ds(start, PAIR)] = (
                jnp.concatenate(outs, axis=0).T * 0.125
            ).astype(BF)
        start = pl.multiple_of(width + (first + j) * PAIR, PAIR)
        out_ref[0, :, pl.ds(start, PAIR)] = (dk_acc[...] * LN2).astype(BF)
        start = pl.multiple_of(2 * width + (first + j) * PAIR, PAIR)
        out_ref[0, :, pl.ds(start, PAIR)] = dv_acc[...].astype(BF)


def self_bwd(lengths, qkv, do, lse):
    nq, rows, width = do.shape
    steps, wide = width // PAIR // STEP, STEP * PAIR
    grid = pltpu.PrefetchScalarGridSpec(
        num_scalar_prefetch=1,
        grid=(nq, steps),
        in_specs=[
            pl.BlockSpec((1, rows, wide), lambda n, p, i: (n, 0, p)),
            pl.BlockSpec((1, rows, wide), lambda n, p, i: (n, 0, steps + p)),
            pl.BlockSpec((1, rows, wide), lambda n, p, i: (n, 0, 2 * steps + p)),
            pl.BlockSpec((1, rows, wide), lambda n, p, i: (n, 0, p)),
            pl.BlockSpec((1, STEP, 2, rows), lambda n, p, i: (n, p, 0, 0)),
        ],
        out_specs=[pl.BlockSpec((1, rows, 3 * width), lambda n, p, i: (n, 0, 0))],
        scratch_shapes=[pltpu.VMEM((rows, PAIR), F32), pltpu.VMEM((rows, PAIR), F32)],
    )
    return pl.pallas_call(
        functools.partial(self_bwd_body, chunk=min(rows, 256)),
        grid_spec=grid,
        out_shape=[jax.ShapeDtypeStruct((nq, rows, 3 * width), BF)],
        compiler_params=params(),
        cost_estimate=pl.CostEstimate(
            flops=40 * nq * rows * rows * width,
            bytes_accessed=16 * nq * rows * width,
            transcendentals=nq * H * rows * rows,
        ),
    )(lengths, qkv, qkv, qkv, do, lse)[0]


def selector(rows, levels):
    row = lax.broadcasted_iota(jnp.int32, (rows, PAIR), 0)
    lane = lax.broadcasted_iota(jnp.int32, (rows, PAIR), 1)
    return (((lane >= DH) == (row % 2 == 1)) & (row < 2 * levels)).astype(BF)


def merge_body(*refs, parts, full):
    values, lses, outs = refs[:parts], refs[parts : 2 * parts], refs[2 * parts :]
    rows = values[0].shape[1]
    row = lax.broadcasted_iota(jnp.int32, (16, rows), 0)
    pick = selector(16, 2)
    for j in range(values[0].shape[2] // PAIR):
        at = slice(j * PAIR, (j + 1) * PAIR)
        top = functools.reduce(jnp.maximum, [lse[0, j] for lse in lses])
        weights = [jnp.exp2(lse[0, j] - top) for lse in lses]
        total = functools.reduce(jnp.add, weights)
        inv = 1.0 / total
        out = 0.0
        for value, weight in zip(values, weights):
            w = weight * inv
            both = jnp.where(row % 2 == 1, w[1:2], w[0:1])
            high = both.astype(BF).astype(F32)
            split = jnp.where(row < 2, high, both - high).astype(BF)
            out = out + value[0, :, at].astype(F32) * dot(split, pick, TN)
        outs[0][0, :, at] = out.astype(BF)
        outs[1][0, j] = top + jnp.log2(total)
        if full:
            outs[2][0, :, at] = out


def merge(parts, full=False):
    nq, rows, width = parts[0][0].shape
    pairs = width // PAIR
    wide = pl.BlockSpec((1, rows, width), lambda n: (n, 0, 0))
    stat = pl.BlockSpec((1, pairs, 2, rows), lambda n: (n, 0, 0, 0))
    return pl.pallas_call(
        functools.partial(merge_body, parts=len(parts), full=full),
        grid=(nq,),
        in_specs=[wide] * len(parts) + [stat] * len(parts),
        out_specs=[wide, stat] + [wide] * full,
        out_shape=[
            jax.ShapeDtypeStruct((nq, rows, width), BF),
            jax.ShapeDtypeStruct((nq, pairs, 2, rows), F32),
        ]
        + [jax.ShapeDtypeStruct((nq, rows, width), F32)] * full,
        compiler_params=params(),
        cost_estimate=pl.CostEstimate(
            flops=4 * nq * rows * width,
            bytes_accessed=nq * rows * width * (2 * len(parts) + 2 + 4 * full),
            transcendentals=nq * H * rows,
        ),
    )(*[p[0] for p in parts], *[p[1] for p in parts])


def stats_body(do_ref, sum_ref, lse_ref, out_ref):
    pick = selector(16, 1)
    for j in range(do_ref.shape[2] // PAIR):
        at = slice(j * PAIR, (j + 1) * PAIR)
        product = do_ref[0, :, at].astype(F32) * sum_ref[0, :, at]
        high = product.astype(BF)
        low = (product - high.astype(F32)).astype(BF)
        out_ref[0, j, 0:2] = lse_ref[0, j]
        out_ref[0, j, 2:4] = (dot(pick, high, NT) + dot(pick, low, NT))[0:2]


def row_stats(do, cross_sum, lse):
    nq, rows, width = do.shape
    pairs = width // PAIR
    wide = pl.BlockSpec((1, rows, width), lambda n: (n, 0, 0))
    return pl.pallas_call(
        stats_body,
        grid=(nq,),
        in_specs=[wide, wide, pl.BlockSpec((1, pairs, 2, rows), lambda n: (n, 0, 0, 0))],
        out_specs=pl.BlockSpec((1, pairs, 4, rows), lambda n: (n, 0, 0, 0)),
        out_shape=jax.ShapeDtypeStruct((nq, pairs, 4, rows), F32),
        compiler_params=params(),
        cost_estimate=pl.CostEstimate(
            flops=4 * nq * rows * width, bytes_accessed=6 * nq * rows * width, transcendentals=0
        ),
    )(do, cross_sum, lse)


def keyval_body(enc_ref, w_ref, out_ref):
    out_ref[...] = dot(enc_ref[...], w_ref[...]).astype(BF)


def keyval(enc, w):
    n, depth = enc.shape
    width = w.shape[1]
    block = 1024
    return pl.pallas_call(
        keyval_body,
        grid=(n // block,),
        in_specs=[
            pl.BlockSpec((block, depth), lambda i: (i, 0)),
            pl.BlockSpec((depth, width), lambda i: (0, 0)),
        ],
        out_specs=pl.BlockSpec((block, width), lambda i: (i, 0)),
        out_shape=jax.ShapeDtypeStruct((n, width), BF),
        compiler_params=params(),
        cost_estimate=pl.CostEstimate(
            flops=2 * n * depth * width, bytes_accessed=2 * n * (depth + width), transcendentals=0
        ),
    )(enc, w)


def feed_forward_body(
    middle_ref,
    att_ref,
    cot_ref,
    gain_ref,
    w_out_ref,
    w_in_ref,
    w_down_ref,
    out_ref,
    grad_ref,
    catt_ref,
    gain_grad_ref,
    w_grad_ref,
    w_down_grad_ref,
    latter,
    normed,
    hidden,
    slopes,
    total,
    back,
):
    step = pl.program_id(0)
    last = pl.num_programs(0) - 1
    gain = gain_ref[...]

    @pl.when(step == 0)
    def _():
        v = middle_ref[...] + dot(att_ref[...], w_out_ref[...])
        latter[...] = v
        normed[...] = (v * rms_parts(v) * gain).astype(BF)

    @pl.when((step < last) & (step % 2 == 0))
    def _():
        act, slope = gelu_and_slope(dot(normed[...], w_in_ref[...]))
        hidden[...] = act.astype(BF)
        slopes[...] = (dot(cot_ref[...], w_down_ref[...], NT) * slope).astype(BF)
        more = dot(slopes[...], w_in_ref[...], NT)
        back[...] = jnp.where(step == 0, more, back[...] + more)
        w_grad_ref[...] = dot(normed[...], slopes[...], TN).astype(BF)

    @pl.when((step < last) & (step % 2 == 1))
    def _():
        more = dot(hidden[...], w_down_ref[...])
        total[...] = jnp.where(step == 1, more, total[...] + more)
        w_down_grad_ref[...] = dot(hidden[...], cot_ref[...], TN).astype(BF)

    @pl.when(step == last)
    def _():
        v, b = latter[...], back[...]
        out_ref[...] = (v + total[...]).astype(BF)
        r = rms_parts(v)
        gb = gain * b
        grad = r * gb - v * (r * r * r * jnp.mean(v * gb, axis=-1, keepdims=True))
        grad = cot_ref[...].astype(F32) + grad
        gain_grad_ref[...] = jnp.sum(v * r * b, axis=0, keepdims=True)
        grad_ref[...] = grad
        hidden[...] = grad.astype(BF)
        catt_ref[...] = dot(hidden[...], w_out_ref[...], NT).astype(BF)
        w_grad_ref[...] = dot(att_ref[...], hidden[...], TN).astype(BF)


def feed_forward(middle, att, cot, gain, weights, w_down):
    tokens, width = middle.shape
    chunks = w_down.shape[0] // width
    steps = 2 * chunks + 1

    def whole(rows, columns):
        return pl.BlockSpec((rows, columns), lambda s: (0, 0))

    def chunk_of(s):
        return jnp.minimum(s // 2, chunks - 1)

    square = (width, width)
    wide = [pltpu.VMEM((tokens, width), t) for t in (F32, BF, BF, BF, F32, F32)]
    return pl.pallas_call(
        feed_forward_body,
        grid=(steps,),
        in_specs=[whole(tokens, width)] * 3
        + [
            whole(1, width),
            whole(*square),
            pl.BlockSpec(square, lambda s: (0, 1 + chunk_of(s))),
            pl.BlockSpec(square, lambda s: (chunk_of(s), 0)),
        ],
        out_specs=[whole(tokens, width)] * 3
        + [
            whole(1, width),
            pl.BlockSpec(square, lambda s: (0, jnp.where(s == steps - 1, 0, 1 + s // 2))),
            pl.BlockSpec(square, lambda s: (chunk_of(s), 0)),
        ],
        out_shape=[
            jax.ShapeDtypeStruct((tokens, width), BF),
            jax.ShapeDtypeStruct((tokens, width), F32),
            jax.ShapeDtypeStruct((tokens, width), BF),
            jax.ShapeDtypeStruct((1, width), F32),
            jax.ShapeDtypeStruct((width, width + w_down.shape[0]), BF),
            jax.ShapeDtypeStruct(w_down.shape, BF),
        ],
        scratch_shapes=wide,
        compiler_params=params(),
        cost_estimate=pl.CostEstimate(
            flops=2 * tokens * width * width * (6 * chunks + 3),
            bytes_accessed=tokens * width * 14 + 8 * width * weights.shape[1],
            transcendentals=tokens * width * chunks,
        ),
    )(middle, att, cot, gain, weights, weights, w_down)


def bits_below(n):
    return [1 << b for b in range(n.bit_length() - 1)]


def exchanges():
    dp, psg = lax.axis_size("dp"), lax.axis_size("psg")
    flat = bits_below(dp)
    cut = max(1, len(flat) // 3)
    xs = [("dp", b) for b in flat[:cut]]
    zs = [("dp", b) for b in flat[cut:]]
    ys = [("psg", b) for b in bits_below(psg)[1:]]
    order = [("dp", b) for b in reversed(flat)] + [("psg", b) for b in reversed(bits_below(psg))]
    return ("psg", 1), xs, ys, zs, order


def my_bit(hop):
    return (lax.axis_index(hop[0]) // hop[1]) % 2


def after(x, *others):
    return lax.optimization_barrier((x, others))[0]


def partner(hop):
    axis, bit = hop
    me = lax.axis_index(axis)
    return {axis: me + bit * (1 - 2 * ((me // bit) % 2))}


def gather_body(*refs, columns, packing, core, orders, order):
    n, n_out, n_more = len(columns), 1 + max(c[0] for c in columns), len(packing)
    ins, more = refs[:n], refs[n : n + n_more]
    outs, packed = refs[n + n_more : n + n_more + n_out], refs[n + n_more + n_out]
    local, packs, send, recv = refs[n + n_more + n_out + 1 :]
    place = tuple(my_bit(h) for h in order)

    def block(k, have, flip=None):
        out, start, width = columns[k]
        at = tuple(
            slice(None) if h in have else 1 - p if h == flip else p for h, p in zip(order, place)
        )
        return outs[out].at[at + (slice(None), pl.ds(start, width))]

    def copy(k, ref, hop, sem):
        moved = pltpu.make_async_remote_copy(
            src_ref=ref,
            dst_ref=ref,
            send_sem=send.at[k, sem],
            recv_sem=recv.at[k, sem],
            device_id=partner(hop),
            device_id_type=pl.DeviceIdType.MESH,
        )
        moved.start()
        return moved

    own = [pltpu.make_async_copy(ins[k], block(k, ()), local.at[k]) for k in range(n)]
    for c in own:
        c.start()
    beside, start = [], 0
    for k, width in enumerate(packing):
        to = packed.at[:, pl.ds(start, width)]
        beside.append(pltpu.make_async_copy(more[k], to, packs.at[k]))
        beside[k].start()
        start += width
    barrier = pltpu.get_barrier_semaphore()
    for hop in order:
        pl.semaphore_signal(
            barrier, inc=1, device_id=partner(hop), device_id_type=pl.DeviceIdType.MESH
        )
    pl.semaphore_wait(barrier, len(order))
    for c in own:
        c.wait()
    steps = len(order) - 1
    far = [[] for _ in range(n)]
    near = [[] for _ in range(n)]
    for k in range(n):
        far[k].append(copy(k, block(k, ()), orders[k][0], 0))
        near[k].append(copy(k, block(k, ()), core, steps))
    for t in range(steps):
        for k in range(n):
            have = orders[k][:t]
            far[k][t].wait_recv()
            if t + 1 < steps:
                far[k].append(copy(k, block(k, orders[k][: t + 1]), orders[k][t + 1], t + 1))
            near[k].append(copy(k, block(k, have, orders[k][t]), core, steps + 1 + t))
    for k in range(n):
        for c in far[k]:
            c.wait_send()
        for c in near[k]:
            c.wait()
    for c in beside:
        c.wait()


def gather_rows(stripes, columns, widths, beside):
    core, xs, ys, zs, order = exchanges()
    orders = [zs + xs + ys, zs + ys + xs, xs + zs + ys, ys + zs + xs, xs + ys + zs]
    orders = [orders[k % len(orders)] for k in range(len(stripes))]
    rows, n = stripes[0].shape[0], len(stripes)
    packing = [x.shape[1] for x in beside]
    outs = pl.pallas_call(
        functools.partial(
            gather_body, columns=columns, packing=packing, core=core, orders=orders, order=order
        ),
        in_specs=[pl.BlockSpec(memory_space=pl.ANY)] * (n + len(beside)),
        out_specs=[pl.BlockSpec(memory_space=pl.ANY)] * (len(widths) + 1),
        out_shape=[
            jax.ShapeDtypeStruct((2,) * len(order) + (rows, w), stripes[0].dtype) for w in widths
        ]
        + [jax.ShapeDtypeStruct((rows, sum(packing)), beside[0].dtype)],
        scratch_shapes=[
            pltpu.SemaphoreType.DMA((n,)),
            pltpu.SemaphoreType.DMA((len(beside),)),
            pltpu.SemaphoreType.DMA((n, 2 * len(order))),
            pltpu.SemaphoreType.DMA((n, 2 * len(order))),
        ],
        compiler_params=pltpu.CompilerParams(collective_id=0, has_side_effects=True),
    )(*stripes, *beside)
    return [o.reshape(rows << len(order), o.shape[-1]) for o in outs[:-1]] + [outs[-1]]


def sum_body(*refs, n_in, columns, hops, order):
    n, steps = len(columns), len(order)
    n_out = 1 + max(c[3] for c in columns)
    ins, outs = refs[:n_in], refs[n_in : n_in + n_out]
    keeps = refs[n_in + n_out : n_in + n_out + n]
    rest = refs[n_in + n_out + n :]
    arrived, (local, send, recv) = rest[:-3], rest[-3:]
    arrived = [arrived[steps * k : steps * (k + 1)] for k in range(n)]
    held = [[[h for h in order if h not in hops[k][:t]] for t in range(steps + 1)] for k in range(n)]

    def side(k, t, bit):
        return tuple(bit if h == hops[k][t] else slice(None) for h in held[k][t])

    def source(k, t, bit):
        if t == 0:
            given, start, width, _, _ = columns[k]
            return ins[given].at[side(k, 0, bit) + (slice(None), pl.ds(start, width))]
        return arrived[k][t - 1].at[side(k, t, bit)]

    def move(k, t):
        copy = pltpu.make_async_remote_copy(
            src_ref=source(k, t, 1 - my_bit(hops[k][t])),
            dst_ref=arrived[k][t],
            send_sem=send.at[k, t],
            recv_sem=recv.at[k, t],
            device_id=partner(hops[k][t]),
            device_id_type=pl.DeviceIdType.MESH,
        )
        copy.start()
        return copy

    own = [pltpu.make_async_copy(source(k, 0, my_bit(hops[k][0])), keeps[k], local.at[k]) for k in range(n)]
    for c in own:
        c.start()
    barrier = pltpu.get_barrier_semaphore()
    for hop in order:
        pl.semaphore_signal(barrier, inc=1, device_id=partner(hop), device_id_type=pl.DeviceIdType.MESH)
    pl.semaphore_wait(barrier, len(order))
    moving = [[move(k, 0)] for k in range(n)]
    for c in own:
        c.wait()
    for t in range(steps):
        for k in range(n):
            moving[k][t].wait_recv()
            left = held[k][t + 1]
            place = held[k][t].index(hops[k][t])
            bit = my_bit(hops[k][t])

            def add(i, carry, k=k, t=t, left=left, place=place, bit=bit):
                at = tuple((i // 2 ** (len(left) - 1 - d)) % 2 for d in range(len(left)))
                before = keeps[k][at] if t == 0 else arrived[k][t - 1][at[:place] + (bit,) + at[place:]]
                total = before.astype(F32) + arrived[k][t][at].astype(F32)
                if t + 1 < steps:
                    arrived[k][t][at] = total.astype(BF)
                else:
                    _, _, width, out, start = columns[k]
                    outs[out][:, start : start + width] = total
                return carry

            if left:
                lax.fori_loop(0, 2 ** len(left), add, 0)
            else:
                add(0, 0)
            if t + 1 < steps:
                moving[k].append(move(k, t + 1))
    for k in range(n):
        for c in moving[k]:
            c.wait_send()

def sum_rows(arrays, columns, ordering, widths):
    core, xs, ys, zs, order = exchanges()
    axes = (xs + ys + zs, ys + zs + xs, zs + xs + ys)
    hops = [[core] + axes[k] for k in ordering]
    rows = arrays[0].shape[0] >> len(order)
    n, steps = len(columns), len(order)
    views = [a.reshape((2,) * steps + (rows, a.shape[1])) for a in arrays]
    return pl.pallas_call(
        functools.partial(sum_body, n_in=len(arrays), columns=columns, hops=hops, order=order),
        in_specs=[pl.BlockSpec(memory_space=pl.ANY)] * len(arrays),
        out_specs=[pl.BlockSpec(memory_space=pltpu.VMEM)] * len(widths),
        out_shape=[jax.ShapeDtypeStruct((rows, w), F32) for w in widths],
        scratch_shapes=[pltpu.VMEM((2,) * (steps - 1) + (rows, c[2]), BF) for c in columns]
        + [pltpu.VMEM((2,) * (steps - 1 - t) + (rows, c[2]), BF) for c in columns for t in range(steps)]
        + [pltpu.SemaphoreType.DMA((n,)), pltpu.SemaphoreType.DMA((n, steps)), pltpu.SemaphoreType.DMA((n, steps))],
        compiler_params=pltpu.CompilerParams(
            collective_id=1, has_side_effects=True, vmem_limit_bytes=VMEM_BYTES
        ),
    )(*views)


def rms_parts(v):
    return lax.rsqrt(jnp.mean(v * v, axis=-1, keepdims=True) + 1e-06)


def rms_back(v, gain, b):
    r = rms_parts(v)
    gb = gain * b
    grad = r * gb - v * (r * r * r * jnp.mean(v * gb, axis=-1, keepdims=True))
    return grad, jnp.sum(v * r * b, axis=tuple(range(v.ndim - 1)))


def gelu_and_slope(u):
    t = jnp.tanh(0.7978845608028654 * (u + 0.044715 * u * u * u))
    slope = 0.5 * (1.0 + t) + 0.5 * u * (1.0 - t * t) * (
        0.7978845608028654 * (1.0 + 3.0 * 0.044715 * u * u)
    )
    return 0.5 * u * (1.0 + t), slope


def on_device(
    decoder_input,
    encoder_out,
    cotangent,
    task_ids,
    passage_ids,
    target_lengths,
    query_embed,
    passage_bank,
    self_in,
    self_out,
    cross_query,
    cross_keyval,
    cross_out,
    hidden_in,
    hidden_output_weight,
    norm_gains,
    task_table,
):
    count, rows, width = decoder_input.shape
    group, npass, tokens, _ = encoder_out.shape
    keys = npass * tokens
    psg = lax.axis_size("psg")
    chips = psg // 2
    me = lax.axis_index("psg")
    chip, core = me // 2, me % 2
    shard = self_in.shape[0]
    ff = hidden_in.shape[1]
    n_tasks = task_table.shape[0]

    swap = [(p, p ^ 1) for p in range(psg)]

    def core_swap(x):
        return jax.tree.map(lambda a: lax.ppermute(a, "psg", swap), x)

    def chip_shift(x, step):
        perm = [(p, (p + 2 * step) % psg) for p in range(psg)]
        return jax.tree.map(lambda a: lax.ppermute(a, "psg", perm), x)

    def ids_of(chip_at, core_at):
        return (chip_at * 2 + core_at) * count + jnp.arange(count, dtype=jnp.int32)

    small = jnp.concatenate([norm_gains, task_table], axis=0).T
    small = jnp.pad(small, ((0, 0), (0, 128 - small.shape[1])))
    enc = encoder_out.reshape(group * keys, width)
    fold = hidden_output_weight.shape[0] // shard
    folded = hidden_output_weight.reshape(fold, shard, width)
    w_self_in, w_out, w_rest, packed = gather_rows(
        [self_in[:, k * width : (k + 1) * width] for k in range(3)]
        + [self_out, jnp.concatenate([cross_query, small], axis=1)],
        [(0, 0, width), (0, width, width), (0, 2 * width, width), (1, 0, width), (2, 0, width + 128)],
        [3 * width, width, width + 128],
        [cross_out, hidden_in] + [folded[k] for k in range(fold)],
    )
    w_self_out, w_cross_query, w_small = w_out, w_rest[:, :width], w_rest[:, width:]
    w_keyval = lax.all_gather(cross_keyval, ALL, axis=0, tiled=True)

    embeds = jnp.take(passage_bank, passage_ids, axis=0).astype(F32)
    score = jnp.sum(query_embed[:, None, :] * embeds, axis=-1)
    others = [
        lax.ppermute(score, "psg", [(p, (p + k) % psg) for p in range(psg)]) for k in range(1, psg)
    ]
    every = jnp.concatenate([score] + others, axis=1)
    top = jnp.max(every, axis=1, keepdims=True)
    retrieval = jnp.exp(score - top) / jnp.sum(jnp.exp(every - top), axis=1, keepdims=True)

    smalls = w_small.T.astype(F32)
    gains, table = smalls[:3], smalls[3 : 3 + n_tasks]
    choose = task_ids[:, None] == jnp.arange(n_tasks, dtype=jnp.int32)[None, :]
    task_rows = jnp.sum(jnp.where(choose[:, :, None], table[None], 0.0), axis=1)

    stream = decoder_input.astype(F32) + task_rows[:, None, :]
    normed_one = (stream * rms_parts(stream) * gains[0]).astype(BF)
    col = lax.broadcasted_iota(jnp.int32, (1, 3 * width), 1)
    scale = jnp.where(col < width, QSCALE, 1.0)
    flat = (count * rows, width)
    qkv = (mm(normed_one.reshape(flat), w_self_in) * scale).astype(BF)
    qkv = qkv.reshape(count, rows, 3 * width)
    self_att, self_lse = self_fwd(target_lengths, qkv)
    second = lax.all_gather(packed, ALL, axis=0, tiled=True)
    w_down = [
        second[:, width * k : width * (k + 1)].reshape(width // shard, shard, width)
        for k in range(1 + ff // width, 1 + ff // width + fold)
    ]
    w_down = jnp.concatenate(w_down, axis=1).reshape(ff, width)
    middle = stream + mm(self_att.reshape(flat), w_self_out).reshape(stream.shape)
    normed_two = (middle * rms_parts(middle) * gains[1]).astype(BF)
    own_q = (mm(normed_two.reshape(flat), w_cross_query) * QSCALE).astype(BF)
    own_q = own_q.reshape(count, rows, width)

    near_ids = (ids_of(chip, core), ids_of(chip, 1 - core))
    far_ids, far_same_q = [], []
    for step in range(1, chips):
        far_same_q.append([chip_shift(own_q[n : n + 1], step) for n in range(count)])
        source = (chip - step) % chips
        far_ids.append((ids_of(source, core), ids_of(source, 1 - core)))
    peer_q = core_swap(own_q)
    kv = keyval(after(enc, own_q), w_keyval).reshape(group, keys, 2 * width)
    peer_part = cross_fwd(near_ids[1], peer_q, kv, npass)
    latest, crossed = peer_part, None
    far_q, far_local, far_back = [], [], []
    for step in range(1, chips):
        queries, local, back = [], [], []
        for n in range(count):
            same_q = after(far_same_q[step - 1][n], peer_part if crossed is None else crossed)
            crossed_q = core_swap(same_q)
            same = cross_fwd(far_ids[step - 1][0][n : n + 1], same_q, kv, npass)
            crossed_q = after(crossed_q, same, latest)
            crossed = cross_fwd(far_ids[step - 1][1][n : n + 1], crossed_q, kv, npass)
            value, joint = merge([same[:2], core_swap(crossed[:2])])
            latest = value
            back.append(chip_shift((value, joint), chips - step))
            local.append((same[1:], crossed[1:]))
            queries.append((same_q, crossed_q))
        far_q.append(queries)
        far_local.append(local)
        far_back.append(back)
    own_part = cross_fwd(near_ids[0], after(own_q, latest), kv, npass)
    parts = [own_part[:2], core_swap(peer_part[:2])]
    for back in after(far_back, w_down, own_part):
        parts.append(tuple(jnp.concatenate([b[k] for b in back], axis=0) for k in range(2)))
    cross_att, cross_lse, cross_sum = merge(parts, full=True)

    output, grad_latter, grad_catt, gain_three, grad_second, grad_down = feed_forward(
        middle.reshape(flat),
        cross_att.reshape(flat),
        cotangent.reshape(flat),
        gains[2:3],
        second,
        w_down,
    )
    output, grad_latter = output.reshape(stream.shape), grad_latter.reshape(stream.shape)
    grad_catt, gain_three = grad_catt.reshape(stream.shape), gain_three[0]
    sum_down = lax.psum_scatter(grad_down, ALL, scatter_dimension=0, tiled=True)
    sum_second = lax.psum_scatter(grad_second, ALL, scatter_dimension=0, tiled=True)

    own_sent = (grad_catt, row_stats(grad_catt, cross_sum, cross_lse))
    far_same = [chip_shift(own_sent, step) for step in range(1, chips)]
    peer_sent = core_swap(own_sent)
    dq_own, dkv = cross_bwd(near_ids[0], own_q, kv, *after(own_sent, grad_second))
    far_same = [after(same, dq_own) for same in far_same]
    far_sent = [(same, core_swap(same)) for same in far_same]
    dq_peer, dkv = cross_bwd(near_ids[1], peer_q, kv, *after(peer_sent, dq_own), dkv)
    dq_back = core_swap(dq_peer)
    latest = dq_peer
    dq_parts = []
    for step in range(1, chips):
        same, crossed = far_sent[step - 1]
        back = []
        for n in range(count):
            same_q, crossed_q = far_q[step - 1][n]
            one = slice(n, n + 1)
            sent = [x[one] for x in after(crossed, latest)]
            dq_crossed, dkv = cross_bwd(far_ids[step - 1][1][one], crossed_q, kv, *sent, dkv)
            sent = [x[one] for x in same]
            dq_same, dkv = cross_bwd(far_ids[step - 1][0][one], same_q, kv, *sent, dkv)
            joint = (dq_same.astype(F32) + core_swap(dq_crossed).astype(F32)).astype(BF)
            latest = joint
            back.append(chip_shift(joint, chips - step))
        dq_parts.append(jnp.concatenate(back, axis=0))
    sets = [
        (near_ids[0], *own_part[1:], own_sent[1]),
        (near_ids[1], *peer_part[1:], peer_sent[1]),
    ]
    for step in range(1, chips):
        for side in range(2):
            lse, share = (
                jnp.concatenate([lo[side][k] for lo in far_local[step - 1]], axis=0)
                for k in range(2)
            )
            sets.append((far_ids[step - 1][side], lse, share, far_sent[step - 1][side][1]))
    ids = jnp.concatenate([s[0] for s in sets])
    masses = []
    for _, lse, share, stats in sets:
        weight = jnp.exp2(lse - stats[:, :, :2])
        masses.append(jnp.sum(share * weight[:, :, :, None, :], axis=(1, 2, 4)) / (H * rows))
    masses = jnp.concatenate(masses, axis=0)
    place = ids[None, :] == jnp.arange(group, dtype=jnp.int32)[:, None]
    mass = jnp.sum(jnp.where(place[:, :, None], masses[None], 0.0), axis=1)
    query_grad = jnp.sum((retrieval - mass)[:, :, None] * embeds, axis=1)
    hop = 1
    while hop < psg:
        perm = [(p, p ^ hop) for p in range(psg)]
        query_grad = query_grad + lax.ppermute(query_grad, "psg", perm)
        hop *= 2

    dkv_flat = after(dkv, joint).reshape(group * keys, 2 * width)
    grad_cross_keyval = mm(enc, dkv_flat, TN).astype(BF)
    total = dq_own.astype(F32) + dq_back.astype(F32)
    for dq in after(dq_parts, grad_cross_keyval, sum_down, query_grad):
        total = total + dq.astype(F32)
    grad_cross_q = total.astype(BF).reshape(flat)
    grad_cross_query = mm(normed_two.reshape(flat), grad_cross_q, TN).astype(BF)

    grad_normed_two = mm(grad_cross_q, w_cross_query, NT).reshape(stream.shape)
    grad_middle, gain_two = rms_back(middle, gains[1], grad_normed_two)
    grad_middle = grad_middle + grad_latter
    grad_self_part = grad_middle.astype(BF).reshape(flat)
    grad_self_out = mm(self_att.reshape(flat), grad_self_part, TN).astype(BF)
    grad_satt = mm(grad_self_part, w_self_out, NT).astype(BF).reshape(count, rows, width)
    grad_qkv = self_bwd(target_lengths, qkv, grad_satt, self_lse)
    grad_qkv = grad_qkv.reshape(count * rows, 3 * width)
    grad_normed_one = mm(grad_qkv, w_self_in, NT).reshape(stream.shape)
    grad_stream, gain_one = rms_back(stream, gains[0], grad_normed_one)
    input_grad = grad_stream + grad_middle
    per_query = jnp.sum(input_grad, axis=1)
    grad_table = jnp.sum(jnp.where(choose[:, :, None], per_query[:, None, :], 0.0), axis=0)
    tiny = jnp.concatenate([jnp.stack([gain_one, gain_two, gain_three]), grad_table], axis=0).T
    tiny = jnp.pad(tiny, ((0, 0), (0, 128 - tiny.shape[1]))).astype(BF)
    grad_self_in = mm(normed_one.reshape(flat), grad_qkv, TN).astype(BF)

    given = [
        after(grad_self_in, sum_second),
        grad_self_out,
        grad_cross_query,
        grad_cross_keyval,
        tiny,
    ]
    (summed,) = sum_rows(
        given,
        [
            (0, 0, width, 0, 0),
            (0, width, width, 0, width),
            (0, 2 * width, width, 0, 2 * width),
            (1, 0, width, 0, 3 * width),
            (2, 0, width, 0, 4 * width),
            (3, 0, width, 0, 5 * width),
            (3, width, width, 0, 6 * width),
            (4, 0, tiny.shape[1], 0, 7 * width),
        ],
        [0, 1, 2, 0, 1, 2, 0, 1],
        [7 * width + tiny.shape[1]],
    )
    small_sum = summed[:, 7 * width :].T
    encoder_grad = mm(dkv_flat, w_keyval, NT).reshape(encoder_out.shape)
    return (
        output,
        input_grad,
        encoder_grad,
        summed[:, : 3 * width],
        summed[:, 3 * width : 4 * width],
        summed[:, 4 * width : 5 * width],
        summed[:, 5 * width : 7 * width],
        sum_second[:, :width].astype(F32),
        sum_second[:, width:].astype(F32),
        sum_down.astype(F32),
        small_sum[:3],
        small_sum[3 : 3 + n_tasks],
        query_grad,
    )


def solution(mesh):
    rows = P(ALL, None)
    tokens = P(ALL, None, None)
    passages = P("dp", "psg", None, None)
    columns = P(None, ALL)
    return jax.shard_map(
        on_device,
        mesh=mesh,
        in_specs=(tokens, passages, tokens, P(ALL), P("dp", "psg"), P(ALL), P("dp", None), P())
        + (rows,) * 7
        + (columns, columns),
        out_specs=(tokens, tokens, passages) + (rows,) * 7 + (columns, columns, P("dp", None)),
        check_vma=False,
    )
```

```python
import functools

import jax
import jax.numpy as jnp
from jax import lax
from jax.experimental import pallas as pl
from jax.experimental.pallas import tpu as pltpu
from jax.sharding import PartitionSpec as P

H = 12
DH = 64
PAIR = 2 * DH
BF = jnp.bfloat16
F32 = jnp.float32
LN2 = 0.6931471805599453
QSCALE = 0.125 / LN2
ALL = ("dp", "psg")
NN = (((1,), (0,)), ((), ()))
NT = (((1,), (1,)), ((), ()))
TN = (((0,), (0,)), ((), ()))
VMEM_BYTES = 56 * 2**20


def dot(a, b, dims=NN):
    return lax.dot_general(a, b, dims, preferred_element_type=F32)


def mm(a, b, dims=NN):
    return lax.dot_general(a, b, dims, preferred_element_type=F32)


STEP = 3
SAFE = 80.0


def halves_of(x, h):
    lane = lax.broadcasted_iota(jnp.int32, x.shape, 1)
    return jnp.where((lane >= DH) == (h == 1), x, jnp.zeros((), x.dtype))


def squared_norms(x):
    wide = x.astype(F32)
    return dot(selector(16, 1), (wide * wide).astype(BF), NT)


def params():
    return pltpu.CompilerParams(vmem_limit_bytes=VMEM_BYTES)


def cross_fwd_body(idx, q_ref, k_ref, v_ref, o_ref, lse_ref, share_ref, *, npass):
    keys = k_ref.shape[1]
    blocks = [slice(j * PAIR, (j + 1) * PAIR) for j in range(q_ref.shape[2] // PAIR)]
    col = lax.broadcasted_iota(jnp.int32, (16, keys), 1) // (keys // npass)
    row = lax.broadcasted_iota(jnp.int32, (16, keys), 0)
    member = (col == row).astype(BF)

    def run(shift):
        for j, at in enumerate(blocks):
            q, k, vt = q_ref[0, :, at], k_ref[0, :, at], v_ref[0, :, at].T
            outs = []
            for h in range(2):
                s = dot(k, halves_of(q, h), NT)
                top = jnp.max(s, axis=0, keepdims=True) if shift else None
                p = jnp.exp2(s - top if shift else s).astype(BF)
                ot = dot(jnp.concatenate([vt[h * DH : (h + 1) * DH], member], axis=0), p)
                parts = ot[DH : DH + npass]
                total = jnp.sum(parts, axis=0, keepdims=True)
                inv = 1.0 / total
                outs.append(ot[:DH] * inv)
                lse = jnp.log2(total)
                lse_ref[0, j, h : h + 1, :] = top + lse if shift else lse
                share_ref[0, j, h, :, :] = parts * inv
            o_ref[0, :, at] = jnp.concatenate(outs, axis=0).T.astype(o_ref.dtype)

    longest_q = functools.reduce(jnp.maximum, [squared_norms(q_ref[0, :, at]) for at in blocks])
    longest_k = functools.reduce(jnp.maximum, [squared_norms(k_ref[0, :, at]) for at in blocks])
    small = jnp.max(longest_q) * jnp.max(longest_k) < SAFE * SAFE
    pl.when(small)(lambda: run(False))
    pl.when(jnp.logical_not(small))(lambda: run(True))


def cross_fwd(idx, q, kv, npass):
    nq, rows, width = q.shape
    keys, pairs = kv.shape[1], width // PAIR
    steps, wide = pairs // STEP, STEP * PAIR
    grid = pltpu.PrefetchScalarGridSpec(
        num_scalar_prefetch=1,
        grid=(nq, steps),
        in_specs=[
            pl.BlockSpec((1, rows, wide), lambda n, p, i: (n, 0, p)),
            pl.BlockSpec((1, keys, wide), lambda n, p, i: (i[n], 0, p)),
            pl.BlockSpec((1, keys, wide), lambda n, p, i: (i[n], 0, steps + p)),
        ],
        out_specs=[
            pl.BlockSpec((1, rows, wide), lambda n, p, i: (n, 0, p)),
            pl.BlockSpec((1, STEP, 2, rows), lambda n, p, i: (n, p, 0, 0)),
            pl.BlockSpec((1, STEP, 2, npass, rows), lambda n, p, i: (n, p, 0, 0, 0)),
        ],
    )
    return pl.pallas_call(
        functools.partial(cross_fwd_body, npass=npass),
        grid_spec=grid,
        out_shape=[
            jax.ShapeDtypeStruct(q.shape, BF),
            jax.ShapeDtypeStruct((nq, pairs, 2, rows), F32),
            jax.ShapeDtypeStruct((nq, pairs, 2, npass, rows), F32),
        ],
        compiler_params=params(),
        cost_estimate=pl.CostEstimate(
            flops=16 * nq * rows * keys * width,
            bytes_accessed=4 * nq * (rows + keys) * width,
            transcendentals=nq * H * rows * keys,
        ),
    )(idx, q, kv, kv)


def cross_bwd_body(idx, q_ref, k_ref, v_ref, do_ref, stat_ref, *rest, chunk):
    dq_ref, dkv_ref = rest[-2:]
    first = pl.program_id(1) * STEP
    width = dkv_ref.shape[2] // 2
    rows = q_ref.shape[1]
    for j in range(STEP):
        at = slice(j * PAIR, (j + 1) * PAIR)
        q, k, v, do = q_ref[0, :, at], k_ref[0, :, at], v_ref[0, :, at], do_ref[0, :, at]
        kt = k.T
        dk, dv = 0.0, 0.0
        for c in range(0, rows, chunk):
            outs = []
            for h in range(2):
                qh = halves_of(q[c : c + chunk], h)
                doh = halves_of(do[c : c + chunk], h)
                p = jnp.exp2(dot(k, qh, NT) - stat_ref[0, j, h : h + 1, c : c + chunk])
                dp = dot(v, doh, NT)
                ds = (p * (dp - stat_ref[0, j, 2 + h : 3 + h, c : c + chunk])).astype(BF)
                dv = dv + dot(p.astype(BF), doh)
                dk = dk + dot(ds, qh)
                outs.append(dot(kt[h * DH : (h + 1) * DH], ds))
            dq_ref[0, c : c + chunk, at] = (jnp.concatenate(outs, axis=0).T * 0.125).astype(BF)
        start = pl.multiple_of((first + j) * PAIR, PAIR)
        dkv_ref[0, :, pl.ds(start, PAIR)] = (dk * LN2).astype(BF)
        start = pl.multiple_of(width + (first + j) * PAIR, PAIR)
        dkv_ref[0, :, pl.ds(start, PAIR)] = dv.astype(BF)


def cross_bwd(idx, q, kv, do, stats, earlier=None):
    nq, rows, width = q.shape
    keys, steps, wide = kv.shape[1], width // PAIR // STEP, STEP * PAIR
    in_specs = [
        pl.BlockSpec((1, rows, wide), lambda n, p, i: (n, 0, p)),
        pl.BlockSpec((1, keys, wide), lambda n, p, i: (i[n], 0, p)),
        pl.BlockSpec((1, keys, wide), lambda n, p, i: (i[n], 0, steps + p)),
        pl.BlockSpec((1, rows, wide), lambda n, p, i: (n, 0, p)),
        pl.BlockSpec((1, STEP, 4, rows), lambda n, p, i: (n, p, 0, 0)),
    ]
    operands = [idx, q, kv, kv, do, stats]
    aliases = {}
    if earlier is not None:
        in_specs.append(pl.BlockSpec(memory_space=pl.ANY))
        operands.append(earlier)
        aliases = {6: 1}
    grid = pltpu.PrefetchScalarGridSpec(
        num_scalar_prefetch=1,
        grid=(nq, steps),
        in_specs=in_specs,
        out_specs=[
            pl.BlockSpec((1, rows, wide), lambda n, p, i: (n, 0, p)),
            pl.BlockSpec((1, keys, 2 * width), lambda n, p, i: (i[n], 0, 0)),
        ],
    )
    return pl.pallas_call(
        functools.partial(cross_bwd_body, chunk=min(rows, 256)),
        grid_spec=grid,
        input_output_aliases=aliases,
        out_shape=[jax.ShapeDtypeStruct(q.shape, BF), jax.ShapeDtypeStruct(kv.shape, BF)],
        compiler_params=params(),
        cost_estimate=pl.CostEstimate(
            flops=40 * nq * rows * keys * width,
            bytes_accessed=nq * (6 * rows + 8 * keys) * width,
            transcendentals=nq * H * rows * keys,
        ),
    )(*operands)


def self_mask(rows, length):
    key = lax.broadcasted_iota(jnp.int32, (rows, rows), 0)
    row = lax.broadcasted_iota(jnp.int32, (rows, rows), 1)
    return (key <= row) & (key < length)


def self_fwd_body(length_ref, q_ref, k_ref, v_ref, o_ref, lse_ref):
    rows = q_ref.shape[1]
    allowed = self_mask(rows, length_ref[pl.program_id(0)])
    ones = jnp.ones((16, rows), BF)
    for j in range(STEP):
        at = slice(j * PAIR, (j + 1) * PAIR)
        q, k, vt = q_ref[0, :, at], k_ref[0, :, at], v_ref[0, :, at].T
        outs = []
        for h in range(2):
            s = jnp.where(allowed, dot(k, halves_of(q, h), NT), -1e30)
            top = jnp.max(s, axis=0, keepdims=True)
            p = jnp.exp2(s - top).astype(BF)
            ot = dot(jnp.concatenate([vt[h * DH : (h + 1) * DH], ones], axis=0), p)
            total = ot[DH : DH + 1]
            outs.append(ot[:DH] * (1.0 / total))
            lse_ref[0, j, h : h + 1, :] = top + jnp.log2(total)
        o_ref[0, :, at] = jnp.concatenate(outs, axis=0).T.astype(BF)


def self_fwd(lengths, qkv):
    nq, rows, width = qkv.shape[0], qkv.shape[1], qkv.shape[2] // 3
    pairs = width // PAIR
    steps, wide = pairs // STEP, STEP * PAIR
    grid = pltpu.PrefetchScalarGridSpec(
        num_scalar_prefetch=1,
        grid=(nq, steps),
        in_specs=[
            pl.BlockSpec((1, rows, wide), lambda n, p, i: (n, 0, p)),
            pl.BlockSpec((1, rows, wide), lambda n, p, i: (n, 0, steps + p)),
            pl.BlockSpec((1, rows, wide), lambda n, p, i: (n, 0, 2 * steps + p)),
        ],
        out_specs=[
            pl.BlockSpec((1, rows, wide), lambda n, p, i: (n, 0, p)),
            pl.BlockSpec((1, STEP, 2, rows), lambda n, p, i: (n, p, 0, 0)),
        ],
    )
    return pl.pallas_call(
        self_fwd_body,
        grid_spec=grid,
        out_shape=[
            jax.ShapeDtypeStruct((nq, rows, width), BF),
            jax.ShapeDtypeStruct((nq, pairs, 2, rows), F32),
        ],
        compiler_params=params(),
        cost_estimate=pl.CostEstimate(
            flops=16 * nq * rows * rows * width,
            bytes_accessed=8 * nq * rows * width,
            transcendentals=nq * H * rows * rows,
        ),
    )(lengths, qkv, qkv, qkv)


def self_bwd_body(length_ref, q_ref, k_ref, v_ref, do_ref, lse_ref, out_ref, dk_acc, dv_acc, *, chunk):
    length = length_ref[pl.program_id(0)]
    first = pl.program_id(1) * STEP
    width = out_ref.shape[2] // 3
    rows = q_ref.shape[1]
    for j in range(STEP):
        at = slice(j * PAIR, (j + 1) * PAIR)
        q, k, v, do = q_ref[0, :, at], k_ref[0, :, at], v_ref[0, :, at], do_ref[0, :, at]
        kt = k.T
        start = pl.multiple_of((first + j) * PAIR, PAIR)
        for c in reversed(range(0, rows, chunk)):
            keys = c + chunk
            key = lax.broadcasted_iota(jnp.int32, (keys, chunk), 0)
            row = lax.broadcasted_iota(jnp.int32, (keys, chunk), 1) + c
            allowed = (key <= row) & (key < length)
            outs = []
            dk, dv = 0.0, 0.0
            for h in range(2):
                qh = halves_of(q[c : c + chunk], h)
                doh = halves_of(do[c : c + chunk], h)
                s = jnp.where(allowed, dot(k[:keys], qh, NT), -1e30)
                p = jnp.exp2(s - lse_ref[0, j, h : h + 1, c : c + chunk])
                dp = dot(v[:keys], doh, NT)
                delta = jnp.sum(p * dp, axis=0, keepdims=True)
                ds = (p * (dp - delta)).astype(BF)
                dv = dv + dot(p.astype(BF), doh)
                dk = dk + dot(ds, qh)
                outs.append(dot(kt[h * DH : (h + 1) * DH, :keys], ds))
            if keys == rows:
                dk_acc[...], dv_acc[...] = dk, dv
            else:
                dk_acc[:keys] += dk
                dv_acc[:keys] += dv
            out_ref[0, c : c + chunk, pl.ds(start, PAIR)] = (
                jnp.concatenate(outs, axis=0).T * 0.125
            ).astype(BF)
        start = pl.multiple_of(width + (first + j) * PAIR, PAIR)
        out_ref[0, :, pl.ds(start, PAIR)] = (dk_acc[...] * LN2).astype(BF)
        start = pl.multiple_of(2 * width + (first + j) * PAIR, PAIR)
        out_ref[0, :, pl.ds(start, PAIR)] = dv_acc[...].astype(BF)


def self_bwd(lengths, qkv, do, lse):
    nq, rows, width = do.shape
    steps, wide = width // PAIR // STEP, STEP * PAIR
    grid = pltpu.PrefetchScalarGridSpec(
        num_scalar_prefetch=1,
        grid=(nq, steps),
        in_specs=[
            pl.BlockSpec((1, rows, wide), lambda n, p, i: (n, 0, p)),
            pl.BlockSpec((1, rows, wide), lambda n, p, i: (n, 0, steps + p)),
            pl.BlockSpec((1, rows, wide), lambda n, p, i: (n, 0, 2 * steps + p)),
            pl.BlockSpec((1, rows, wide), lambda n, p, i: (n, 0, p)),
            pl.BlockSpec((1, STEP, 2, rows), lambda n, p, i: (n, p, 0, 0)),
        ],
        out_specs=[pl.BlockSpec((1, rows, 3 * width), lambda n, p, i: (n, 0, 0))],
        scratch_shapes=[pltpu.VMEM((rows, PAIR), F32), pltpu.VMEM((rows, PAIR), F32)],
    )
    return pl.pallas_call(
        functools.partial(self_bwd_body, chunk=min(rows, 256)),
        grid_spec=grid,
        out_shape=[jax.ShapeDtypeStruct((nq, rows, 3 * width), BF)],
        compiler_params=params(),
        cost_estimate=pl.CostEstimate(
            flops=40 * nq * rows * rows * width,
            bytes_accessed=16 * nq * rows * width,
            transcendentals=nq * H * rows * rows,
        ),
    )(lengths, qkv, qkv, qkv, do, lse)[0]


def selector(rows, levels):
    row = lax.broadcasted_iota(jnp.int32, (rows, PAIR), 0)
    lane = lax.broadcasted_iota(jnp.int32, (rows, PAIR), 1)
    return (((lane >= DH) == (row % 2 == 1)) & (row < 2 * levels)).astype(BF)


def merge_body(*refs, parts, full):
    values, lses, outs = refs[:parts], refs[parts : 2 * parts], refs[2 * parts :]
    rows = values[0].shape[1]
    row = lax.broadcasted_iota(jnp.int32, (16, rows), 0)
    pick = selector(16, 2)
    for j in range(values[0].shape[2] // PAIR):
        at = slice(j * PAIR, (j + 1) * PAIR)
        top = functools.reduce(jnp.maximum, [lse[0, j] for lse in lses])
        weights = [jnp.exp2(lse[0, j] - top) for lse in lses]
        total = functools.reduce(jnp.add, weights)
        inv = 1.0 / total
        out = 0.0
        for value, weight in zip(values, weights):
            w = weight * inv
            both = jnp.where(row % 2 == 1, w[1:2], w[0:1])
            high = both.astype(BF).astype(F32)
            split = jnp.where(row < 2, high, both - high).astype(BF)
            out = out + value[0, :, at].astype(F32) * dot(split, pick, TN)
        outs[0][0, :, at] = out.astype(BF)
        outs[1][0, j] = top + jnp.log2(total)
        if full:
            outs[2][0, :, at] = out


def merge(parts, full=False):
    nq, rows, width = parts[0][0].shape
    pairs = width // PAIR
    wide = pl.BlockSpec((1, rows, width), lambda n: (n, 0, 0))
    stat = pl.BlockSpec((1, pairs, 2, rows), lambda n: (n, 0, 0, 0))
    return pl.pallas_call(
        functools.partial(merge_body, parts=len(parts), full=full),
        grid=(nq,),
        in_specs=[wide] * len(parts) + [stat] * len(parts),
        out_specs=[wide, stat] + [wide] * full,
        out_shape=[
            jax.ShapeDtypeStruct((nq, rows, width), BF),
            jax.ShapeDtypeStruct((nq, pairs, 2, rows), F32),
        ]
        + [jax.ShapeDtypeStruct((nq, rows, width), F32)] * full,
        compiler_params=params(),
        cost_estimate=pl.CostEstimate(
            flops=4 * nq * rows * width,
            bytes_accessed=nq * rows * width * (2 * len(parts) + 2 + 4 * full),
            transcendentals=nq * H * rows,
        ),
    )(*[p[0] for p in parts], *[p[1] for p in parts])


def stats_body(do_ref, sum_ref, lse_ref, out_ref):
    pick = selector(16, 1)
    for j in range(do_ref.shape[2] // PAIR):
        at = slice(j * PAIR, (j + 1) * PAIR)
        product = do_ref[0, :, at].astype(F32) * sum_ref[0, :, at]
        high = product.astype(BF)
        low = (product - high.astype(F32)).astype(BF)
        out_ref[0, j, 0:2] = lse_ref[0, j]
        out_ref[0, j, 2:4] = (dot(pick, high, NT) + dot(pick, low, NT))[0:2]


def row_stats(do, cross_sum, lse):
    nq, rows, width = do.shape
    pairs = width // PAIR
    wide = pl.BlockSpec((1, rows, width), lambda n: (n, 0, 0))
    return pl.pallas_call(
        stats_body,
        grid=(nq,),
        in_specs=[wide, wide, pl.BlockSpec((1, pairs, 2, rows), lambda n: (n, 0, 0, 0))],
        out_specs=pl.BlockSpec((1, pairs, 4, rows), lambda n: (n, 0, 0, 0)),
        out_shape=jax.ShapeDtypeStruct((nq, pairs, 4, rows), F32),
        compiler_params=params(),
        cost_estimate=pl.CostEstimate(
            flops=4 * nq * rows * width, bytes_accessed=6 * nq * rows * width, transcendentals=0
        ),
    )(do, cross_sum, lse)


def keyval_body(enc_ref, w_ref, out_ref):
    out_ref[...] = dot(enc_ref[...], w_ref[...]).astype(BF)


def keyval(enc, w):
    n, depth = enc.shape
    width = w.shape[1]
    block = 1024
    return pl.pallas_call(
        keyval_body,
        grid=(n // block,),
        in_specs=[
            pl.BlockSpec((block, depth), lambda i: (i, 0)),
            pl.BlockSpec((depth, width), lambda i: (0, 0)),
        ],
        out_specs=pl.BlockSpec((block, width), lambda i: (i, 0)),
        out_shape=jax.ShapeDtypeStruct((n, width), BF),
        compiler_params=params(),
        cost_estimate=pl.CostEstimate(
            flops=2 * n * depth * width, bytes_accessed=2 * n * (depth + width), transcendentals=0
        ),
    )(enc, w)


def feed_forward_body(
    middle_ref,
    att_ref,
    cot_ref,
    gain_ref,
    w_out_ref,
    w_in_ref,
    w_down_ref,
    out_ref,
    grad_ref,
    catt_ref,
    gain_grad_ref,
    w_grad_ref,
    w_down_grad_ref,
    latter,
    normed,
    hidden,
    slopes,
    total,
    back,
):
    step = pl.program_id(0)
    last = pl.num_programs(0) - 1
    gain = gain_ref[...]

    @pl.when(step == 0)
    def _():
        v = middle_ref[...] + dot(att_ref[...], w_out_ref[...])
        latter[...] = v
        normed[...] = (v * rms_parts(v) * gain).astype(BF)

    @pl.when((step < last) & (step % 2 == 0))
    def _():
        act, slope = gelu_and_slope(dot(normed[...], w_in_ref[...]))
        hidden[...] = act.astype(BF)
        slopes[...] = (dot(cot_ref[...], w_down_ref[...], NT) * slope).astype(BF)
        more = dot(slopes[...], w_in_ref[...], NT)
        back[...] = jnp.where(step == 0, more, back[...] + more)
        w_grad_ref[...] = dot(normed[...], slopes[...], TN).astype(BF)

    @pl.when((step < last) & (step % 2 == 1))
    def _():
        more = dot(hidden[...], w_down_ref[...])
        total[...] = jnp.where(step == 1, more, total[...] + more)
        w_down_grad_ref[...] = dot(hidden[...], cot_ref[...], TN).astype(BF)

    @pl.when(step == last)
    def _():
        v, b = latter[...], back[...]
        out_ref[...] = (v + total[...]).astype(BF)
        r = rms_parts(v)
        gb = gain * b
        grad = r * gb - v * (r * r * r * jnp.mean(v * gb, axis=-1, keepdims=True))
        grad = cot_ref[...].astype(F32) + grad
        gain_grad_ref[...] = jnp.sum(v * r * b, axis=0, keepdims=True)
        grad_ref[...] = grad
        hidden[...] = grad.astype(BF)
        catt_ref[...] = dot(hidden[...], w_out_ref[...], NT).astype(BF)
        w_grad_ref[...] = dot(att_ref[...], hidden[...], TN).astype(BF)


def feed_forward(middle, att, cot, gain, weights, w_down):
    tokens, width = middle.shape
    chunks = w_down.shape[0] // width
    steps = 2 * chunks + 1

    def whole(rows, columns):
        return pl.BlockSpec((rows, columns), lambda s: (0, 0))

    def chunk_of(s):
        return jnp.minimum(s // 2, chunks - 1)

    square = (width, width)
    wide = [pltpu.VMEM((tokens, width), t) for t in (F32, BF, BF, BF, F32, F32)]
    return pl.pallas_call(
        feed_forward_body,
        grid=(steps,),
        in_specs=[whole(tokens, width)] * 3
        + [
            whole(1, width),
            whole(*square),
            pl.BlockSpec(square, lambda s: (0, 1 + chunk_of(s))),
            pl.BlockSpec(square, lambda s: (chunk_of(s), 0)),
        ],
        out_specs=[whole(tokens, width)] * 3
        + [
            whole(1, width),
            pl.BlockSpec(square, lambda s: (0, jnp.where(s == steps - 1, 0, 1 + s // 2))),
            pl.BlockSpec(square, lambda s: (chunk_of(s), 0)),
        ],
        out_shape=[
            jax.ShapeDtypeStruct((tokens, width), BF),
            jax.ShapeDtypeStruct((tokens, width), F32),
            jax.ShapeDtypeStruct((tokens, width), BF),
            jax.ShapeDtypeStruct((1, width), F32),
            jax.ShapeDtypeStruct((width, width + w_down.shape[0]), BF),
            jax.ShapeDtypeStruct(w_down.shape, BF),
        ],
        scratch_shapes=wide,
        compiler_params=params(),
        cost_estimate=pl.CostEstimate(
            flops=2 * tokens * width * width * (6 * chunks + 3),
            bytes_accessed=tokens * width * 14 + 8 * width * weights.shape[1],
            transcendentals=tokens * width * chunks,
        ),
    )(middle, att, cot, gain, weights, weights, w_down)


def bits_below(n):
    return [1 << b for b in range(n.bit_length() - 1)]


def exchanges():
    dp, psg = lax.axis_size("dp"), lax.axis_size("psg")
    flat = bits_below(dp)
    cut = max(1, len(flat) // 3)
    xs = [("dp", b) for b in flat[:cut]]
    zs = [("dp", b) for b in flat[cut:]]
    ys = [("psg", b) for b in bits_below(psg)[1:]]
    order = [("dp", b) for b in reversed(flat)] + [("psg", b) for b in reversed(bits_below(psg))]
    return ("psg", 1), xs, ys, zs, order


def my_bit(hop):
    return (lax.axis_index(hop[0]) // hop[1]) % 2


def after(x, *others):
    return lax.optimization_barrier((x, others))[0]


def partner(hop):
    axis, bit = hop
    me = lax.axis_index(axis)
    return {axis: me + bit * (1 - 2 * ((me // bit) % 2))}


def gather_body(*refs, columns, packing, core, orders, order):
    n, n_out, n_more = len(columns), 1 + max(c[0] for c in columns), len(packing)
    ins, more = refs[:n], refs[n : n + n_more]
    outs, packed = refs[n + n_more : n + n_more + n_out], refs[n + n_more + n_out]
    local, packs, send, recv = refs[n + n_more + n_out + 1 :]
    place = tuple(my_bit(h) for h in order)

    def block(k, have, flip=None):
        out, start, width = columns[k]
        at = tuple(
            slice(None) if h in have else 1 - p if h == flip else p for h, p in zip(order, place)
        )
        return outs[out].at[at + (slice(None), pl.ds(start, width))]

    def copy(k, ref, hop, sem):
        moved = pltpu.make_async_remote_copy(
            src_ref=ref,
            dst_ref=ref,
            send_sem=send.at[k, sem],
            recv_sem=recv.at[k, sem],
            device_id=partner(hop),
            device_id_type=pl.DeviceIdType.MESH,
        )
        moved.start()
        return moved

    own = [pltpu.make_async_copy(ins[k], block(k, ()), local.at[k]) for k in range(n)]
    for c in own:
        c.start()
    beside, start = [], 0
    for k, width in enumerate(packing):
        to = packed.at[:, pl.ds(start, width)]
        beside.append(pltpu.make_async_copy(more[k], to, packs.at[k]))
        beside[k].start()
        start += width
    barrier = pltpu.get_barrier_semaphore()
    for hop in order:
        pl.semaphore_signal(
            barrier, inc=1, device_id=partner(hop), device_id_type=pl.DeviceIdType.MESH
        )
    pl.semaphore_wait(barrier, len(order))
    for c in own:
        c.wait()
    steps = len(order) - 1
    far = [[] for _ in range(n)]
    near = [[] for _ in range(n)]
    for k in range(n):
        far[k].append(copy(k, block(k, ()), orders[k][0], 0))
        near[k].append(copy(k, block(k, ()), core, steps))
    for t in range(steps):
        for k in range(n):
            have = orders[k][:t]
            far[k][t].wait_recv()
            if t + 1 < steps:
                far[k].append(copy(k, block(k, orders[k][: t + 1]), orders[k][t + 1], t + 1))
            near[k].append(copy(k, block(k, have, orders[k][t]), core, steps + 1 + t))
    for k in range(n):
        for c in far[k]:
            c.wait_send()
        for c in near[k]:
            c.wait()
    for c in beside:
        c.wait()


def gather_rows(stripes, columns, widths, beside):
    core, xs, ys, zs, order = exchanges()
    orders = [zs + xs + ys, zs + ys + xs, xs + zs + ys, ys + zs + xs, xs + ys + zs]
    orders = [orders[k % len(orders)] for k in range(len(stripes))]
    rows, n = stripes[0].shape[0], len(stripes)
    packing = [x.shape[1] for x in beside]
    outs = pl.pallas_call(
        functools.partial(
            gather_body, columns=columns, packing=packing, core=core, orders=orders, order=order
        ),
        in_specs=[pl.BlockSpec(memory_space=pl.ANY)] * (n + len(beside)),
        out_specs=[pl.BlockSpec(memory_space=pl.ANY)] * (len(widths) + 1),
        out_shape=[
            jax.ShapeDtypeStruct((2,) * len(order) + (rows, w), stripes[0].dtype) for w in widths
        ]
        + [jax.ShapeDtypeStruct((rows, sum(packing)), beside[0].dtype)],
        scratch_shapes=[
            pltpu.SemaphoreType.DMA((n,)),
            pltpu.SemaphoreType.DMA((len(beside),)),
            pltpu.SemaphoreType.DMA((n, 2 * len(order))),
            pltpu.SemaphoreType.DMA((n, 2 * len(order))),
        ],
        compiler_params=pltpu.CompilerParams(collective_id=0, has_side_effects=True),
    )(*stripes, *beside)
    return [o.reshape(rows << len(order), o.shape[-1]) for o in outs[:-1]] + [outs[-1]]


def sum_body(*refs, n_in, columns, hops, order):
    n, steps = len(columns), len(order)
    n_out = 1 + max(c[3] for c in columns)
    ins, outs = refs[:n_in], refs[n_in : n_in + n_out]
    keeps = refs[n_in + n_out : n_in + n_out + n]
    rest = refs[n_in + n_out + n :]
    arrived, (local, send, recv) = rest[:-3], rest[-3:]
    arrived = [arrived[steps * k : steps * (k + 1)] for k in range(n)]
    held = [[[h for h in order if h not in hops[k][:t]] for t in range(steps + 1)] for k in range(n)]

    def side(k, t, bit):
        return tuple(bit if h == hops[k][t] else slice(None) for h in held[k][t])

    def source(k, t, bit):
        if t == 0:
            given, start, width, _, _ = columns[k]
            return ins[given].at[side(k, 0, bit) + (slice(None), pl.ds(start, width))]
        return arrived[k][t - 1].at[side(k, t, bit)]

    def move(k, t):
        copy = pltpu.make_async_remote_copy(
            src_ref=source(k, t, 1 - my_bit(hops[k][t])),
            dst_ref=arrived[k][t],
            send_sem=send.at[k, t],
            recv_sem=recv.at[k, t],
            device_id=partner(hops[k][t]),
            device_id_type=pl.DeviceIdType.MESH,
        )
        copy.start()
        return copy

    own = [pltpu.make_async_copy(source(k, 0, my_bit(hops[k][0])), keeps[k], local.at[k]) for k in range(n)]
    for c in own:
        c.start()
    barrier = pltpu.get_barrier_semaphore()
    for hop in order:
        pl.semaphore_signal(barrier, inc=1, device_id=partner(hop), device_id_type=pl.DeviceIdType.MESH)
    pl.semaphore_wait(barrier, len(order))
    moving = [[move(k, 0)] for k in range(n)]
    for c in own:
        c.wait()
    for t in range(steps):
        for k in range(n):
            moving[k][t].wait_recv()
            left = held[k][t + 1]
            place = held[k][t].index(hops[k][t])
            bit = my_bit(hops[k][t])

            def add(i, carry, k=k, t=t, left=left, place=place, bit=bit):
                at = tuple((i // 2 ** (len(left) - 1 - d)) % 2 for d in range(len(left)))
                before = keeps[k][at] if t == 0 else arrived[k][t - 1][at[:place] + (bit,) + at[place:]]
                total = before.astype(F32) + arrived[k][t][at].astype(F32)
                if t + 1 < steps:
                    arrived[k][t][at] = total.astype(BF)
                else:
                    _, _, width, out, start = columns[k]
                    outs[out][:, start : start + width] = total
                return carry

            if left:
                lax.fori_loop(0, 2 ** len(left), add, 0)
            else:
                add(0, 0)
            if t + 1 < steps:
                moving[k].append(move(k, t + 1))
    for k in range(n):
        for c in moving[k]:
            c.wait_send()

def sum_rows(arrays, columns, ordering, widths):
    core, xs, ys, zs, order = exchanges()
    axes = (xs + ys + zs, ys + zs + xs, zs + xs + ys)
    hops = [[core] + axes[k] for k in ordering]
    rows = arrays[0].shape[0] >> len(order)
    n, steps = len(columns), len(order)
    views = [a.reshape((2,) * steps + (rows, a.shape[1])) for a in arrays]
    return pl.pallas_call(
        functools.partial(sum_body, n_in=len(arrays), columns=columns, hops=hops, order=order),
        in_specs=[pl.BlockSpec(memory_space=pl.ANY)] * len(arrays),
        out_specs=[pl.BlockSpec(memory_space=pltpu.VMEM)] * len(widths),
        out_shape=[jax.ShapeDtypeStruct((rows, w), F32) for w in widths],
        scratch_shapes=[pltpu.VMEM((2,) * (steps - 1) + (rows, c[2]), BF) for c in columns]
        + [pltpu.VMEM((2,) * (steps - 1 - t) + (rows, c[2]), BF) for c in columns for t in range(steps)]
        + [pltpu.SemaphoreType.DMA((n,)), pltpu.SemaphoreType.DMA((n, steps)), pltpu.SemaphoreType.DMA((n, steps))],
        compiler_params=pltpu.CompilerParams(
            collective_id=1, has_side_effects=True, vmem_limit_bytes=VMEM_BYTES
        ),
    )(*views)


def rms_parts(v):
    return lax.rsqrt(jnp.mean(v * v, axis=-1, keepdims=True) + 1e-06)


def rms_back(v, gain, b):
    r = rms_parts(v)
    gb = gain * b
    grad = r * gb - v * (r * r * r * jnp.mean(v * gb, axis=-1, keepdims=True))
    return grad, jnp.sum(v * r * b, axis=tuple(range(v.ndim - 1)))


def gelu_and_slope(u):
    t = jnp.tanh(0.7978845608028654 * (u + 0.044715 * u * u * u))
    slope = 0.5 * (1.0 + t) + 0.5 * u * (1.0 - t * t) * (
        0.7978845608028654 * (1.0 + 3.0 * 0.044715 * u * u)
    )
    return 0.5 * u * (1.0 + t), slope


def on_device(
    decoder_input,
    encoder_out,
    cotangent,
    task_ids,
    passage_ids,
    target_lengths,
    query_embed,
    passage_bank,
    self_in,
    self_out,
    cross_query,
    cross_keyval,
    cross_out,
    hidden_in,
    hidden_output_weight,
    norm_gains,
    task_table,
):
    count, rows, width = decoder_input.shape
    group, npass, tokens, _ = encoder_out.shape
    keys = npass * tokens
    psg = lax.axis_size("psg")
    chips = psg // 2
    me = lax.axis_index("psg")
    chip, core = me // 2, me % 2
    shard = self_in.shape[0]
    ff = hidden_in.shape[1]
    n_tasks = task_table.shape[0]

    swap = [(p, p ^ 1) for p in range(psg)]

    def core_swap(x):
        return jax.tree.map(lambda a: lax.ppermute(a, "psg", swap), x)

    def chip_shift(x, step):
        perm = [(p, (p + 2 * step) % psg) for p in range(psg)]
        return jax.tree.map(lambda a: lax.ppermute(a, "psg", perm), x)

    def ids_of(chip_at, core_at):
        return (chip_at * 2 + core_at) * count + jnp.arange(count, dtype=jnp.int32)

    small = jnp.concatenate([norm_gains, task_table], axis=0).T
    small = jnp.pad(small, ((0, 0), (0, 128 - small.shape[1])))
    enc = encoder_out.reshape(group * keys, width)
    fold = hidden_output_weight.shape[0] // shard
    folded = hidden_output_weight.reshape(fold, shard, width)
    w_self_in, w_out, w_rest, packed = gather_rows(
        [self_in[:, k * width : (k + 1) * width] for k in range(3)]
        + [self_out, jnp.concatenate([cross_query, small], axis=1)],
        [(0, 0, width), (0, width, width), (0, 2 * width, width), (1, 0, width), (2, 0, width + 128)],
        [3 * width, width, width + 128],
        [cross_out, hidden_in] + [folded[k] for k in range(fold)],
    )
    w_self_out, w_cross_query, w_small = w_out, w_rest[:, :width], w_rest[:, width:]
    w_keyval = lax.all_gather(cross_keyval, ALL, axis=0, tiled=True)

    embeds = jnp.take(passage_bank, passage_ids, axis=0).astype(F32)
    score = jnp.sum(query_embed[:, None, :] * embeds, axis=-1)
    others = [
        lax.ppermute(score, "psg", [(p, (p + k) % psg) for p in range(psg)]) for k in range(1, psg)
    ]
    every = jnp.concatenate([score] + others, axis=1)
    top = jnp.max(every, axis=1, keepdims=True)
    retrieval = jnp.exp(score - top) / jnp.sum(jnp.exp(every - top), axis=1, keepdims=True)

    smalls = w_small.T.astype(F32)
    gains, table = smalls[:3], smalls[3 : 3 + n_tasks]
    choose = task_ids[:, None] == jnp.arange(n_tasks, dtype=jnp.int32)[None, :]
    task_rows = jnp.sum(jnp.where(choose[:, :, None], table[None], 0.0), axis=1)

    stream = decoder_input.astype(F32) + task_rows[:, None, :]
    normed_one = (stream * rms_parts(stream) * gains[0]).astype(BF)
    col = lax.broadcasted_iota(jnp.int32, (1, 3 * width), 1)
    scale = jnp.where(col < width, QSCALE, 1.0)
    flat = (count * rows, width)
    qkv = (mm(normed_one.reshape(flat), w_self_in) * scale).astype(BF)
    qkv = qkv.reshape(count, rows, 3 * width)
    self_att, self_lse = self_fwd(target_lengths, qkv)
    second = lax.all_gather(packed, ALL, axis=0, tiled=True)
    w_down = [
        second[:, width * k : width * (k + 1)].reshape(width // shard, shard, width)
        for k in range(1 + ff // width, 1 + ff // width + fold)
    ]
    w_down = jnp.concatenate(w_down, axis=1).reshape(ff, width)
    middle = stream + mm(self_att.reshape(flat), w_self_out).reshape(stream.shape)
    normed_two = (middle * rms_parts(middle) * gains[1]).astype(BF)
    own_q = (mm(normed_two.reshape(flat), w_cross_query) * QSCALE).astype(BF)
    own_q = own_q.reshape(count, rows, width)

    near_ids = (ids_of(chip, core), ids_of(chip, 1 - core))
    far_ids, far_same_q = [], []
    for step in range(1, chips):
        far_same_q.append([chip_shift(own_q[n : n + 1], step) for n in range(count)])
        source = (chip - step) % chips
        far_ids.append((ids_of(source, core), ids_of(source, 1 - core)))
    peer_q = core_swap(own_q)
    kv = keyval(after(enc, own_q), w_keyval).reshape(group, keys, 2 * width)
    peer_part = cross_fwd(near_ids[1], peer_q, kv, npass)
    latest, crossed = peer_part, None
    far_q, far_local, far_back = [], [], []
    for step in range(1, chips):
        queries, local, back = [], [], []
        for n in range(count):
            same_q = after(far_same_q[step - 1][n], peer_part if crossed is None else crossed)
            crossed_q = core_swap(same_q)
            same = cross_fwd(far_ids[step - 1][0][n : n + 1], same_q, kv, npass)
            crossed_q = after(crossed_q, same, latest)
            crossed = cross_fwd(far_ids[step - 1][1][n : n + 1], crossed_q, kv, npass)
            value, joint = merge([same[:2], core_swap(crossed[:2])])
            latest = value
            back.append(chip_shift((value, joint), chips - step))
            local.append((same[1:], crossed[1:]))
            queries.append((same_q, crossed_q))
        far_q.append(queries)
        far_local.append(local)
        far_back.append(back)
    own_part = cross_fwd(near_ids[0], after(own_q, latest), kv, npass)
    parts = [own_part[:2], core_swap(peer_part[:2])]
    for back in after(far_back, w_down, own_part):
        parts.append(tuple(jnp.concatenate([b[k] for b in back], axis=0) for k in range(2)))
    cross_att, cross_lse, cross_sum = merge(parts, full=True)

    output, grad_latter, grad_catt, gain_three, grad_second, grad_down = feed_forward(
        middle.reshape(flat),
        cross_att.reshape(flat),
        cotangent.reshape(flat),
        gains[2:3],
        second,
        w_down,
    )
    output, grad_latter = output.reshape(stream.shape), grad_latter.reshape(stream.shape)
    grad_catt, gain_three = grad_catt.reshape(stream.shape), gain_three[0]
    sum_down = lax.psum_scatter(grad_down, ALL, scatter_dimension=0, tiled=True)
    sum_second = lax.psum_scatter(grad_second, ALL, scatter_dimension=0, tiled=True)

    own_sent = (grad_catt, row_stats(grad_catt, cross_sum, cross_lse))
    far_same = [chip_shift(own_sent, step) for step in range(1, chips)]
    peer_sent = core_swap(own_sent)
    dq_own, dkv = cross_bwd(near_ids[0], own_q, kv, *after(own_sent, grad_second))
    far_same = [after(same, dq_own) for same in far_same]
    far_sent = [(same, core_swap(same)) for same in far_same]
    dq_peer, dkv = cross_bwd(near_ids[1], peer_q, kv, *after(peer_sent, dq_own), dkv)
    dq_back = core_swap(dq_peer)
    latest = dq_peer
    dq_parts = []
    for step in range(1, chips):
        same, crossed = far_sent[step - 1]
        back = []
        for n in range(count):
            same_q, crossed_q = far_q[step - 1][n]
            one = slice(n, n + 1)
            sent = [x[one] for x in after(crossed, latest)]
            dq_crossed, dkv = cross_bwd(far_ids[step - 1][1][one], crossed_q, kv, *sent, dkv)
            sent = [x[one] for x in same]
            dq_same, dkv = cross_bwd(far_ids[step - 1][0][one], same_q, kv, *sent, dkv)
            joint = (dq_same.astype(F32) + core_swap(dq_crossed).astype(F32)).astype(BF)
            latest = joint
            back.append(chip_shift(joint, chips - step))
        dq_parts.append(jnp.concatenate(back, axis=0))
    sets = [
        (near_ids[0], *own_part[1:], own_sent[1]),
        (near_ids[1], *peer_part[1:], peer_sent[1]),
    ]
    for step in range(1, chips):
        for side in range(2):
            lse, share = (
                jnp.concatenate([lo[side][k] for lo in far_local[step - 1]], axis=0)
                for k in range(2)
            )
            sets.append((far_ids[step - 1][side], lse, share, far_sent[step - 1][side][1]))
    ids = jnp.concatenate([s[0] for s in sets])
    masses = []
    for _, lse, share, stats in sets:
        weight = jnp.exp2(lse - stats[:, :, :2])
        masses.append(jnp.sum(share * weight[:, :, :, None, :], axis=(1, 2, 4)) / (H * rows))
    masses = jnp.concatenate(masses, axis=0)
    place = ids[None, :] == jnp.arange(group, dtype=jnp.int32)[:, None]
    mass = jnp.sum(jnp.where(place[:, :, None], masses[None], 0.0), axis=1)
    query_grad = jnp.sum((retrieval - mass)[:, :, None] * embeds, axis=1)
    hop = 1
    while hop < psg:
        perm = [(p, p ^ hop) for p in range(psg)]
        query_grad = query_grad + lax.ppermute(query_grad, "psg", perm)
        hop *= 2

    dkv_flat = after(dkv, joint).reshape(group * keys, 2 * width)
    grad_cross_keyval = mm(enc, dkv_flat, TN).astype(BF)
    total = dq_own.astype(F32) + dq_back.astype(F32)
    for dq in after(dq_parts, grad_cross_keyval, sum_down, query_grad):
        total = total + dq.astype(F32)
    grad_cross_q = total.astype(BF).reshape(flat)
    grad_cross_query = mm(normed_two.reshape(flat), grad_cross_q, TN).astype(BF)

    grad_normed_two = mm(grad_cross_q, w_cross_query, NT).reshape(stream.shape)
    grad_middle, gain_two = rms_back(middle, gains[1], grad_normed_two)
    grad_middle = grad_middle + grad_latter
    grad_self_part = grad_middle.astype(BF).reshape(flat)
    grad_self_out = mm(self_att.reshape(flat), grad_self_part, TN).astype(BF)
    grad_satt = mm(grad_self_part, w_self_out, NT).astype(BF).reshape(count, rows, width)
    grad_qkv = self_bwd(target_lengths, qkv, grad_satt, self_lse)
    grad_qkv = grad_qkv.reshape(count * rows, 3 * width)
    grad_normed_one = mm(grad_qkv, w_self_in, NT).reshape(stream.shape)
    grad_stream, gain_one = rms_back(stream, gains[0], grad_normed_one)
    input_grad = grad_stream + grad_middle
    per_query = jnp.sum(input_grad, axis=1)
    grad_table = jnp.sum(jnp.where(choose[:, :, None], per_query[:, None, :], 0.0), axis=0)
    tiny = jnp.concatenate([jnp.stack([gain_one, gain_two, gain_three]), grad_table], axis=0).T
    tiny = jnp.pad(tiny, ((0, 0), (0, 128 - tiny.shape[1]))).astype(BF)
    grad_self_in = mm(normed_one.reshape(flat), grad_qkv, TN).astype(BF)

    given = [
        after(grad_self_in, sum_second),
        grad_self_out,
        grad_cross_query,
        grad_cross_keyval,
        tiny,
    ]
    half = width // 2
    stripes = [
        (array, half * k, half)
        for array, halves in ((0, 6), (1, 2), (2, 2), (3, 4))
        for k in range(halves)
    ]
    stripes = [(*stripe, 0, half * k) for k, stripe in enumerate(stripes)]
    stripes.append((4, 0, tiny.shape[1], 0, 7 * width))
    (summed,) = sum_rows(
        given,
        stripes,
        [(0, 1, 2, 0, 1)[k % 5] for k in range(len(stripes))],
        [7 * width + tiny.shape[1]],
    )
    small_sum = summed[:, 7 * width :].T
    encoder_grad = mm(dkv_flat, w_keyval, NT).reshape(encoder_out.shape)
    return (
        output,
        input_grad,
        encoder_grad,
        summed[:, : 3 * width],
        summed[:, 3 * width : 4 * width],
        summed[:, 4 * width : 5 * width],
        summed[:, 5 * width : 7 * width],
        sum_second[:, :width].astype(F32),
        sum_second[:, width:].astype(F32),
        sum_down.astype(F32),
        small_sum[:3],
        small_sum[3 : 3 + n_tasks],
        query_grad,
    )


def solution(mesh):
    rows = P(ALL, None)
    tokens = P(ALL, None, None)
    passages = P("dp", "psg", None, None)
    columns = P(None, ALL)
    return jax.shard_map(
        on_device,
        mesh=mesh,
        in_specs=(tokens, passages, tokens, P(ALL), P("dp", "psg"), P(ALL), P("dp", None), P())
        + (rows,) * 7
        + (columns, columns),
        out_specs=(tokens, tokens, passages) + (rows,) * 7 + (columns, columns, P("dp", None)),
        check_vma=False,
    )
```
